128 devices in a mesh: dp: 16 (over x, z_hi, core), fsdp: 8 (over y, z_lo).
Axes of the slice: x: 4, y: 4, z: 4 (z_hi: 2, z_lo: 2; z = z_hi * 2 + z_lo), core: 2. Of those that a mesh axis runs over, the one named last changes fastest.
Arguments:
- frames: bfloat16 [65536, 2048], P(('dp', 'fsdp')), may hold values from -120 to 120, as said below
- bounds: int32 [2, 65536], P(None, ('dp', 'fsdp')), may hold values from -1 to 399, as said below
- destinations: int32 [16, 8, 16], P(None, 'fsdp'), may hold values from -1 to 15, as said below
- kernel: float32 [9, 2048], replicated, may hold values from -2 to 2
- norm_gain: float32 [2048], replicated, may hold values from 0.5 to 2
- norm_shift: float32 [2048], replicated, may hold values from -3 to 3
- panel: bfloat16 [2048, 2048], P('fsdp'), may hold values from -0.125 to 0.125
- cotangent: bfloat16 [49152, 2048], P(('dp', 'fsdp')), may hold values from -6 to 6
Outputs:
- mapped: bfloat16 [49152, 2048], P(('dp', 'fsdp'))
- input_grad: bfloat16 [65536, 2048], P(('dp', 'fsdp'))
- panel_grad: float32 [2048, 2048], P('fsdp')
- kernel_grad: float32 [9, 2048], replicated
- norm_grads: float32 [2, 2048], replicated
The draws below stay inside these ranges and needn't reach their ends.
Inputs may be any that keep to these rules, and one draw needn't show every extreme that they name: `bounds`: A frame's count of earlier and later frames of its utterance along the stream of live frames; both are -1 on padding frames, which fill each device's last blocks; every device has a multiple of 32 live frames, the same ones that destinations marks live. Utterances hold at most 400 frames, and one holds exactly 400. destinations[d, f, b] is the data index in column f that receives block b of device (d, f), or -1 for a padding block. A device's live blocks come first and number from 8 to 16; a device sends at most one block to each device of its column, and every device receives exactly 12 blocks. Input features; padding frames hold arbitrary values.
All inputs are finite; a program needn't handle non-finite values.
Results may differ from the reference program's by a relative error of at most 0.005.
Values may be sent and summed in bfloat16 or wider, within the bound.
A program may use at most 128 MiB of HBM per device.

```python
import math
import jax
import jax.numpy as jnp
from jax import lax

D = 2048
OUTW = 2048
KERN = 9
BLOCK_FRAMES = 32
ARRIVAL_BLOCKS = 16
DEVICE_BLOCKS = 12
LIVE_ROW_COUNT = 49152
N_DP = 16
N_FSDP = 8


def live_counts(key):
    key = jax.random.fold_in(key, 11)
    excess = N_DP // 4
    pattern = jnp.where(jnp.arange(N_DP) < N_DP // 2, excess, -excess).astype(jnp.int32)
    column_keys = jax.random.split(key, N_FSDP)
    orders = jax.vmap(lambda single: jax.random.permutation(single, N_DP))(column_keys)
    return (DEVICE_BLOCKS + pattern[orders].T).astype(jnp.int32)


def draw_destinations(key, part):
    counts = live_counts(key)
    key = jax.random.fold_in(key, 3)
    key_offset, key_order = jax.random.split(key)
    offsets = jax.random.randint(key_offset, (N_FSDP,), 0, N_DP).astype(jnp.int32)
    orders = jax.vmap(lambda single: jax.random.permutation(single, N_DP))(jax.random.split(key_order, N_FSDP))
    starts = (jnp.cumsum(counts, axis=0) - counts).astype(jnp.int32)
    slot_index = jnp.arange(ARRIVAL_BLOCKS, dtype=jnp.int32)
    labels = (starts[:, :, None] + slot_index[None, None, :] + offsets[None, :, None]) % N_DP
    column = jnp.arange(N_FSDP, dtype=jnp.int32)[None, :, None]
    targets = orders[column, labels]
    return jnp.where(slot_index[None, None, :] < counts[:, :, None], targets, -1).astype(jnp.int32)


def draw_bounds(key, part):
    counts = live_counts(key)
    key = jax.random.fold_in(key, 7)
    device_list = N_DP * N_FSDP
    stream = device_list * DEVICE_BLOCKS * BLOCK_FRAMES
    places = jnp.arange(stream, dtype=jnp.int32)
    random_flag = (jax.random.randint(key, (stream,), 0, 200) == 0) & (places >= 400)
    start_flag = random_flag | (places % 400 == 0)
    start_of = lax.cummax(jnp.where(start_flag, places, 0), axis=0)
    end_flag = jnp.concatenate([start_flag[1:], jnp.ones((1,), dtype=jnp.bool_)])
    end_of = lax.cummin(jnp.where(end_flag, places, stream), axis=0, reverse=True)
    before_live = places - start_of
    after_live = end_of - places
    live_frames = (counts.reshape(device_list) * BLOCK_FRAMES).astype(jnp.int32)
    offsets = (jnp.cumsum(live_frames) - live_frames).astype(jnp.int32)
    slot_rows = ARRIVAL_BLOCKS * BLOCK_FRAMES
    row_index = jnp.arange(slot_rows, dtype=jnp.int32)
    frame_index = offsets[:, None] + row_index[None, :]
    live_slot = row_index[None, :] < live_frames[:, None]
    safe_index = jnp.where(live_slot, frame_index, 0)
    before_all = jnp.where(live_slot, before_live[safe_index], -1)
    after_all = jnp.where(live_slot, after_live[safe_index], -1)
    return jnp.stack([before_all.reshape(-1), after_all.reshape(-1)]).astype(jnp.int32)


def draw_frames(key, part):
    key = jax.random.fold_in(key, 5)
    key_base, key_rows, key_cols = jax.random.split(key, 3)
    length = N_DP * N_FSDP * ARRIVAL_BLOCKS * BLOCK_FRAMES
    ramp_scale = 1.0 + 2.0 * jnp.arange(length, dtype=jnp.float32) / (length - 1)
    row_scale = ramp_scale[:, None] * jnp.exp(jax.random.uniform(key_rows, (length, 1)) * 2.302585)
    col_scale = jnp.exp(jax.random.uniform(key_cols, (1, D)) * 2.302585)
    base_draw = jnp.clip(jax.random.normal(key_base, (length, D)), -4.0, 4.0)
    return (0.1 * base_draw * row_scale * col_scale).astype(jnp.bfloat16)


def level_of(stream_key, dims, pieces, least, largest):
    def one(axis_at, blocks):
        steps = jax.random.uniform(jax.random.fold_in(jax.random.fold_in(stream_key, 6), axis_at), (blocks,), jnp.float32, least / len(pieces), largest / len(pieces))
        return jnp.repeat(jnp.exp(steps), dims[axis_at] // blocks).reshape((-1,) + (1,) * (len(dims) - axis_at - 1))

    factor_of = one(*pieces[0])
    for cut in pieces[1:]:
        factor_of = factor_of * one(*cut)
    return factor_of


def bell_draw(key, shape, deviation, limit, cuts=(), kind=jnp.bfloat16):
    entries = deviation * jax.random.normal(key, shape, jnp.float32)
    if cuts:
        entries = entries * level_of(key, shape, cuts, -0.22, 0.18)
    return jnp.clip(entries, -limit, limit).astype(kind)


def setup_inputs(seed: int = 0) -> dict:
    key_of = jax.random.split(jax.random.key(seed), 9)
    frames = draw_frames(jax.random.fold_in(key_of[8], 71), 0)
    bounds = draw_bounds(jax.random.fold_in(key_of[8], 71), 0)
    destinations = draw_destinations(jax.random.fold_in(key_of[8], 71), 0)
    kernel = bell_draw(key_of[3], (KERN, D), KERN ** -0.5, 2.0, (), jnp.float32)
    norm_gain = jnp.clip(jnp.exp(jax.random.uniform(key_of[4], (D,), jnp.float32, math.log(0.5), math.log(2.0))), 0.5, 2.0)
    norm_shift = bell_draw(key_of[5], (D,), 0.5, 3.0, (), jnp.float32)
    panel = bell_draw(key_of[6], (D, OUTW), D ** -0.5, 0.125, ((0, 8),))
    cotangent = bell_draw(key_of[7], (LIVE_ROW_COUNT, OUTW), 1.0, 6.0, ((0, 128),))
    return dict(frames=frames, bounds=bounds, destinations=destinations, kernel=kernel, norm_gain=norm_gain, norm_shift=norm_shift, panel=panel, cotangent=cotangent)


epsilon = 1e-05

def tap_mask(before_rows, after_rows, offset):
    return (before_rows >= max(-offset, 0)) & (after_rows >= max(offset, 0))

def conv_rows(extended, kernel, before_rows, after_rows):
    half_span = kernel.shape[0] // 2
    length = before_rows.shape[0]
    accum = jnp.zeros((length, extended.shape[1]), jnp.float32)
    for tap_index in range(kernel.shape[0]):
        offset = tap_index - half_span
        window = extended[tap_index:tap_index + length].astype(jnp.float32) * kernel[tap_index]
        accum = accum + jnp.where(tap_mask(before_rows, after_rows, offset)[:, None], window, 0.0)
    return accum

def conv_back(extended, kernel, before_rows, after_rows):
    half_span = kernel.shape[0] // 2
    length = before_rows.shape[0]
    accum = jnp.zeros((length, extended.shape[1]), jnp.float32)
    for tap_index in range(kernel.shape[0]):
        offset = tap_index - half_span
        first_row = 2 * half_span - tap_index
        window = extended[first_row:first_row + length] * kernel[tap_index]
        accum = accum + jnp.where(tap_mask(before_rows, after_rows, -offset)[:, None], window, 0.0)
    return accum

def kernel_terms(extended, gradient, before_rows, after_rows, kernel_taps):
    half_span = kernel_taps // 2
    length = before_rows.shape[0]
    tap_sums = []
    for tap_index in range(kernel_taps):
        offset = tap_index - half_span
        window = extended[tap_index:tap_index + length].astype(jnp.float32)
        masked = jnp.where(tap_mask(before_rows, after_rows, offset)[:, None], window * gradient, 0.0)
        tap_sums.append(lax.optimization_barrier(jnp.sum(masked, axis=0)))
    return jnp.stack(tap_sums)

def rim_rows(values, live_rows, half_span):
    leading = values[:half_span]
    trailing = lax.dynamic_slice_in_dim(values, live_rows - half_span, half_span, 0)
    return (leading, trailing)

def extend(values, previous, following, live_rows):
    half_span = previous.shape[0]
    padding = jnp.zeros((half_span, values.shape[1]), values.dtype)
    joined = jnp.concatenate([previous, values, padding], axis=0)
    return lax.dynamic_update_slice_in_dim(joined, following, live_rows + half_span, 0)

def neighbours(leading, trailing):
    zeroed = jnp.zeros_like(leading[:1])
    previous = jnp.concatenate([zeroed, trailing[:-1]], axis=0)
    following = jnp.concatenate([leading[1:], zeroed], axis=0)
    return (previous, following)

def reference(frames, bounds, destinations, kernel, norm_gain, norm_shift, panel, cotangent):
    device_list = N_DP * N_FSDP
    slot_rows = ARRIVAL_BLOCKS * BLOCK_FRAMES
    frame_features = frames.shape[1]
    out_width = cotangent.shape[1]
    half_span = kernel.shape[0] // 2
    total_live = float(LIVE_ROW_COUNT)
    blocks = frames.reshape(device_list, slot_rows, frame_features)
    before_all = bounds[0].reshape(device_list, slot_rows)
    after_all = bounds[1].reshape(device_list, slot_rows)
    live_all = lax.optimization_barrier(jnp.sum((before_all >= 0).astype(jnp.int32), axis=1)).astype(jnp.int32)
    leading = blocks[:, :half_span]
    trailing = jax.vmap(lambda values, live_rows: lax.dynamic_slice_in_dim(values, live_rows - half_span, half_span, 0))(blocks, live_all)
    previous, following = neighbours(leading, trailing)
    device_ids = jnp.arange(device_list, dtype=jnp.int32)

    def conv_of(device):
        extended = extend(blocks[device], previous[device], following[device], live_all[device])
        return (extended, conv_rows(extended, kernel, before_all[device], after_all[device]))
    average = lax.optimization_barrier(jnp.sum(lax.map(lambda device: lax.optimization_barrier(jnp.sum(conv_of(device)[1], axis=0)), device_ids), axis=0)) / total_live

    def spread_of(device):
        live_mask = (before_all[device] >= 0)[:, None]
        centred = jnp.where(live_mask, conv_of(device)[1] - average, 0.0)
        return lax.optimization_barrier(jnp.sum(centred * centred, axis=0))
    variance = lax.optimization_barrier(jnp.sum(lax.map(spread_of, device_ids), axis=0)) / total_live
    inverse = lax.rsqrt(variance + epsilon)

    def forward_of(device):
        extended, filtered = conv_of(device)
        whitened = (filtered - average) * inverse
        normed = whitened * norm_gain + norm_shift
        logistic = jax.nn.sigmoid(normed)
        return (extended, whitened, normed, logistic)

    def activation_of(device):
        extended, whitened, normed, logistic = forward_of(device)
        live_mask = (before_all[device] >= 0)[:, None]
        return jnp.where(live_mask, normed * logistic, 0.0).astype(jnp.bfloat16)
    layer_activation = lax.map(activation_of, device_ids)
    labels = jnp.arange(N_DP, dtype=jnp.int32)
    present = jnp.any(destinations[:, :, :, None] == labels[None, None, None, :], axis=2).astype(jnp.int32)
    earlier = (jnp.cumsum(present, axis=0) - present).astype(jnp.int32)
    target_peer = jnp.maximum(destinations, 0).astype(jnp.int32)
    position = jnp.take_along_axis(earlier, target_peer, axis=2).astype(jnp.int32)
    column = jnp.arange(N_FSDP, dtype=jnp.int32)[None, :, None]
    target_device = ((target_peer * N_FSDP + column) * DEVICE_BLOCKS + position).astype(jnp.int32)
    live_block = (destinations >= 0).reshape(-1)
    target_device = jnp.where(live_block, target_device.reshape(-1), device_list * DEVICE_BLOCKS).astype(jnp.int32)
    evened_blocks = jnp.zeros((device_list * DEVICE_BLOCKS, BLOCK_FRAMES, frame_features), jnp.bfloat16)
    evened_blocks = evened_blocks.at[target_device].set(layer_activation.reshape(device_list * ARRIVAL_BLOCKS, BLOCK_FRAMES, frame_features), mode='drop')
    evened_activation = evened_blocks.reshape(LIVE_ROW_COUNT, frame_features)
    mapped = jnp.dot(evened_activation, panel, preferred_element_type=jnp.float32).astype(jnp.bfloat16)
    panel_grad = lax.dot_general(evened_activation, cotangent, (((0,), (0,)), ((), ())), preferred_element_type=jnp.float32)
    safe_target = jnp.minimum(target_device, device_list * DEVICE_BLOCKS - 1).astype(jnp.int32)
    back_rows = jnp.take(cotangent.reshape(device_list * DEVICE_BLOCKS, BLOCK_FRAMES, out_width), safe_target, axis=0)
    back_rows = jnp.where(live_block[:, None, None], back_rows, jnp.zeros_like(back_rows))
    back_rows = back_rows.reshape(device_list, slot_rows, out_width)
    act_grad = lax.map(lambda device: jnp.dot(back_rows[device], panel.T, preferred_element_type=jnp.float32).astype(jnp.bfloat16), device_ids)

    def normed_grad_of(device):
        extended, whitened, normed, logistic = forward_of(device)
        slope = logistic + normed * logistic * (1.0 - logistic)
        return (extended, whitened, act_grad[device].astype(jnp.float32) * slope)

    def norm_terms(device):
        extended, whitened, normed_grad = normed_grad_of(device)
        return jnp.stack([lax.optimization_barrier(jnp.sum(normed_grad * whitened, axis=0)), lax.optimization_barrier(jnp.sum(normed_grad, axis=0))])
    norm_grads = lax.optimization_barrier(jnp.sum(lax.map(norm_terms, device_ids), axis=0))

    def conv_grad_of(device):
        extended, whitened, normed_grad = normed_grad_of(device)
        live_mask = (before_all[device] >= 0)[:, None]
        inner = normed_grad - norm_grads[1] / total_live - whitened * norm_grads[0] / total_live
        return (extended, jnp.where(live_mask, norm_gain * inverse * inner, 0.0))

    def kernel_part(device):
        extended, conv_grad = conv_grad_of(device)
        grad_leading, grad_trailing = rim_rows(conv_grad, live_all[device], half_span)
        terms = kernel_terms(extended, conv_grad, before_all[device], after_all[device], kernel.shape[0])
        return (terms, grad_leading, grad_trailing)
    kernel_parts, grad_leading, grad_trailing = lax.map(kernel_part, device_ids)
    kernel_grad = lax.optimization_barrier(jnp.sum(kernel_parts, axis=0))
    grad_previous, grad_following = neighbours(grad_leading, grad_trailing)

    def input_grad_of(device):
        conv_grad = conv_grad_of(device)[1]
        extended = extend(conv_grad, grad_previous[device], grad_following[device], live_all[device])
        return conv_back(extended, kernel, before_all[device], after_all[device]).astype(jnp.bfloat16)
    input_grad = lax.map(input_grad_of, device_ids).reshape(device_list * slot_rows, frame_features)
    return (mapped, input_grad, panel_grad, kernel_grad, norm_grads)
```

```python
import jax
import jax.numpy as jnp
from jax import lax
from jax.experimental import pallas as pl
from jax.experimental.pallas import tpu as pltpu
from jax.sharding import PartitionSpec as P

MESH = pl.DeviceIdType.MESH
F32 = jnp.float32
BF16 = jnp.bfloat16
EPSILON = 1e-05

D = 2048
TAPS = 9
BLOCK = 32
SLOTS = 512
ROWS = 384
N_DP = 16
N_FSDP = 8
CHUNKS = D // 128
TOTAL = float(ROWS * N_DP * N_FSDP)

RANK, DEST, SEND, PICK, LIVE = 0, 16, 32, 48, 60


def routing(destinations, data_index):
    plan_table = destinations[:, 0, :]
    mine_row = lax.dynamic_index_in_dim(plan_table, data_index, 0, keepdims=False)
    labels = jnp.arange(N_DP, dtype=jnp.int32)
    peers = (data_index + labels) % N_DP
    send_match = mine_row[None, :] == peers[:, None]
    send_row = jnp.sum(jnp.where(send_match, labels[None, :], 0), axis=1)
    arrives = jnp.any(plan_table == data_index, axis=1)
    earlier = (labels[None, :] < peers[:, None]) & arrives[None, :]
    rank_row = jnp.minimum(jnp.sum(earlier.astype(jnp.int32), axis=1), 11)
    source_rank = jnp.sum(((labels[None, :] < labels[:, None]) & arrives[None, :]).astype(jnp.int32), axis=1)
    wanted = jnp.arange(12, dtype=jnp.int32)
    chosen = arrives[None, :] & (source_rank[None, :] == wanted[:, None])
    source_slot = (data_index - labels + N_DP) % N_DP
    pick_slot = jnp.sum(jnp.where(chosen, source_slot[None, :], 0), axis=1)
    back_slot = jnp.where(mine_row >= 0, (data_index - mine_row + N_DP) % N_DP, 0)
    blocks = jnp.sum((mine_row >= 0).astype(jnp.int32))
    tail = jnp.stack([BLOCK * blocks, 2 * blocks - 1, BLOCK * blocks - 8, blocks])
    idx = jnp.concatenate(
        [rank_row, back_slot, send_row, pick_slot, tail]
    )
    flags = jnp.concatenate([labels < blocks, labels + 1 == blocks]).astype(F32)
    count = jnp.full((8, 128), (BLOCK * blocks).astype(F32))
    return idx, jnp.concatenate([jnp.broadcast_to(flags[:, None], (32, 128)), count])


class Sems:
    def __init__(self):
        self.used = 0

    def take(self, count):
        at = self.used
        self.used += count
        return at


SEMS = Sems()
S_HALO = SEMS.take(2)
S_OWN = SEMS.take(3)
S_FWD = SEMS.take(2)
S_FAR = SEMS.take(4)
S_PAIR = SEMS.take(7)
S_COT = SEMS.take(16)
S_ST1 = SEMS.take(8)
S_ST2 = SEMS.take(16)
S_ACT = SEMS.take(16)
S_AT = SEMS.take(1)
S_CP = SEMS.take(1)
S_NG1 = SEMS.take(8)
S_NG2 = SEMS.take(16)
S_BHALO = SEMS.take(4)
S_R1 = SEMS.take(4)
S_R2 = SEMS.take(4)
S_R3 = SEMS.take(4)
S_GAT = SEMS.take(8)
S_GPAIR = SEMS.take(1)
S_K1 = SEMS.take(16)
S_K2 = SEMS.take(8)
S_K3 = SEMS.take(16)


def fused(
    idx,
    flags,
    bounds,
    frames,
    cotangent,
    panel,
    kern,
    gain,
    shift,
    mapped,
    igrad,
    pgrad,
    kgrad,
    ngrad,
    fr,
    cot,
    cs,
    cr,
    cp,
    cpp,
    ext,
    filt,
    ngx,
    msk,
    pan,
    act,
    ar,
    at,
    atp,
    gp,
    r1,
    s1,
    r2,
    s2,
    r3,
    pgb,
    pst,
    mst,
    htrail,
    hprev,
    hnext,
    st1,
    st2,
    stat,
    ng1,
    ng2,
    bsend,
    brecv,
    kg,
    kg1,
    kg2,
    kg3,
    ssem,
    rsem,
    lsem,
):
    dp = lax.axis_index("dp")
    f = lax.axis_index("fsdp")
    c = dp % 2
    zh = (dp // 2) % 2
    x = dp // 4
    y = f // 2
    zl = f % 2
    z = zh * 2 + zl
    partner = dp + 1 - 2 * c
    me = dp * N_FSDP + f
    follow = (me + 1) % (N_DP * N_FSDP)
    lead = (me + N_DP * N_FSDP - 1) % (N_DP * N_FSDP)

    def remote(src, dst, sem, to_dp, to_f):
        return pltpu.make_async_remote_copy(
            src_ref=src,
            dst_ref=dst,
            send_sem=ssem.at[sem],
            recv_sem=rsem.at[sem],
            device_id=(to_dp, to_f),
            device_id_type=MESH,
        )

    def loop(count, body, start=0):
        def step(k, carry):
            body(k)
            return carry

        lax.fori_loop(start, count, step, 0)

    def lanes(j):
        return pl.ds(pl.multiple_of(j * 128, 128), 128)

    def rows(at_row, count):
        return pl.ds(pl.multiple_of(at_row, count), count)

    load_frames = pltpu.make_async_copy(frames, fr, lsem.at[0])
    load_cot = pltpu.make_async_copy(cotangent, cot, lsem.at[1])
    load_panel = pltpu.make_async_copy(panel, pan.at[rows(f * 256, 256)], lsem.at[2])
    load_frames.start()
    load_panel.start()
    load_cot.start()

    barrier = pltpu.get_barrier_semaphore()

    def greet(to_dp, to_f):
        pl.semaphore_signal(barrier, inc=1, device_id=(to_dp, to_f), device_id_type=MESH)

    loop(N_DP, lambda k: greet((dp + k) % N_DP, f), 1)
    loop(N_FSDP, lambda k: greet(dp, (f + k) % N_FSDP), 1)
    greet(follow // N_FSDP, follow % N_FSDP)
    greet(lead // N_FSDP, lead % N_FSDP)
    greet(x * 4 + (1 - zh) * 2 + c, y * 2 + 1 - zl)

    for q in range(4):
        part = slice(128 * q, 128 * q + 128)
        before = jnp.broadcast_to(bounds[0:1, part].astype(F32), (128, 128)).T
        after = jnp.broadcast_to(bounds[1:2, part].astype(F32), (128, 128)).T
        for tap in range(TAPS):
            o = tap - 4
            keep = (before >= float(max(-o, 0))) & (after >= float(max(o, 0)))
            msk[tap, part, :] = jnp.where(keep, 1.0, 0.0)

    pl.semaphore_wait(barrier, 25)

    def unit(f_of):
        return pan.at[pl.ds(pl.multiple_of(f_of * 256 + c * 128, 128), 128)]

    def half_unit(f_of, h):
        return pan.at[pl.ds(pl.multiple_of(f_of * 256 + c * 128 + h * 64, 64), 64)]

    def shard_at(dy, dz):
        return ((y + dy) % 4) * 2 + (zl + dz) % 2

    f_z, f_up, f_down = shard_at(0, 1), shard_at(1, 0), shard_at(3, 0)
    f_upz, f_downz = shard_at(1, 1), shard_at(3, 1)
    f_far, f_farz = shard_at(2, 0), shard_at(2, 1)

    def send_unit(f_of, sem, to_f):
        return remote(unit(f_of), unit(f_of), sem, dp, to_f)

    def send_half(f_of, h, sem, to_f):
        return remote(half_unit(f_of, h), half_unit(f_of, h), sem, dp, to_f)

    def to_partner(f_of, n):
        return remote(unit(f_of), unit(f_of), S_PAIR + n, partner, f)

    own_copies = [
        send_unit(f, S_OWN, f_z),
        send_unit(f, S_OWN + 1, f_up),
        send_unit(f, S_OWN + 2, f_down),
    ]
    fwd_copies = [send_unit(f_z, S_FWD, f_up), send_unit(f_z, S_FWD + 1, f_down)]
    far_copies = [
        send_half(f_down, 0, S_FAR, f_up),
        send_half(f_up, 1, S_FAR + 1, f_down),
        send_half(f_downz, 0, S_FAR + 2, f_up),
        send_half(f_upz, 1, S_FAR + 3, f_down),
    ]
    pair_copies = [
        to_partner(g, n)
        for n, g in enumerate([f_z, f_down, f_up, f_downz, f_upz, f_far, f_farz])
    ]

    load_frames.wait()
    htrail[...] = fr[idx[LIVE + 1]]
    halo_next = remote(htrail, hprev, S_HALO, follow // N_FSDP, follow % N_FSDP)
    halo_prev = remote(fr.at[0], hnext, S_HALO + 1, lead // N_FSDP, lead % N_FSDP)
    halo_next.start()
    halo_prev.start()

    load_panel.wait()
    for copy in own_copies:
        copy.start()

    load_cot.wait()

    def cot_block(k):
        return cot[idx[RANK + k]]

    cr[0] = cot_block(0)

    def cot_copy(k):
        return remote(cs.at[k], cr.at[k], S_COT + k, (dp + k) % N_DP, f)

    def send_cot(k):
        cs[k] = cot_block(k)
        cot_copy(k).start()

    loop(N_DP, send_cot, 1)

    def widen(j):
        for q in range(4):
            part = fr[8 * q : 8 * q + 8, :, lanes(j)].reshape(128, 128)
            ext[j, 8 + 128 * q : 136 + 128 * q, :] = part.astype(F32)
        ext[j, 520:528, :] = jnp.zeros((8, 128), F32)

    loop(CHUNKS, widen)

    halo_next.wait_recv()
    halo_prev.wait_recv()

    def place(ref, j, previous, following):
        ref[j, 0:8, :] = previous
        for b in range(8, 17):
            at_row = 8 + BLOCK * b
            here = ref[j, at_row : at_row + 8, :]
            last = flags[15 + b : 16 + b, :]
            ref[j, at_row : at_row + 8, :] = here * (1.0 - last) + following * last

    def place_frames(j):
        place(
            ext,
            j,
            hprev[:, lanes(j)].astype(F32)[8:16],
            hnext[:, lanes(j)].astype(F32)[0:8],
        )

    loop(CHUNKS, place_frames)

    def fold(value):
        return jnp.sum(value, axis=0, keepdims=True)

    def conv(j):
        taps = kern[:, lanes(j)]

        def part(i, total):
            base = i * 64
            accum = jnp.zeros((64, 128), F32)
            for tap in range(TAPS):
                window = ext[j, pl.ds(base + 4 + tap, 64), :] * taps[tap : tap + 1]
                accum = accum + msk[tap, rows(base, 64), :] * window
            filt[j, rows(base, 64), :] = accum
            return total + jnp.sum(accum.reshape(8, 8, 128), axis=0)

        total = lax.fori_loop(0, 8, part, jnp.zeros((8, 128), F32))
        total = fold(total)
        mean = total / flags[32:33, :]

        def spread(i, total):
            base = i * 64
            off = (filt[j, rows(base, 64), :] - mean) * msk[4, rows(base, 64), :]
            return total + jnp.sum((off * off).reshape(8, 8, 128), axis=0)

        squares = fold(lax.fori_loop(0, 8, spread, jnp.zeros((8, 128), F32)))
        st1[0, pl.ds(j, 1), :] = total
        st1[0, pl.ds(16 + j, 1), :] = squares

    loop(CHUNKS, conv)
    st1[0, 32:40, :] = flags[32:40, :]

    def over_fsdp(buf, sem):
        def copy(k):
            return remote(buf.at[0], buf.at[k], sem + k, dp, (f + k) % N_FSDP)

        return copy

    def over_dp(buf, sem):
        def copy(k):
            return remote(buf.at[0], buf.at[k], sem + k, (dp + k) % N_DP, f)

        return copy

    def begin(copy, count):
        loop(count, lambda k: copy(k).start(), 1)

    def arrive(copy, count):
        loop(count, lambda k: copy(k).wait_recv(), 1)

    def merge(buf, count, mine):
        def slot(p):
            return (mine - p + count) % count

        def add(p, carry):
            sums, number = carry
            return sums + buf[slot(p), 0:16, :], number + buf[slot(p), 32:40, :]

        sums, number = lax.fori_loop(
            0, count, add, (jnp.zeros((16, 128), F32), jnp.zeros((8, 128), F32))
        )
        mean = sums / jnp.concatenate([number, number], axis=0)

        def spread(p, squares):
            n_p = buf[slot(p), 32:40, :]
            n_p = jnp.concatenate([n_p, n_p], axis=0)
            off = buf[slot(p), 0:16, :] / n_p - mean
            return squares + (buf[slot(p), 16:32, :] + n_p * off * off)

        squares = lax.fori_loop(0, count, spread, jnp.zeros((16, 128), F32))
        return sums, squares, number

    def ordered(buf, count, mine, shape):
        def add(p, total):
            return total + buf[(mine - p + count) % count]

        return lax.fori_loop(0, count, add, jnp.zeros(shape, F32))

    copy_st1 = over_fsdp(st1, S_ST1)
    copy_st2 = over_dp(st2, S_ST2)
    begin(copy_st1, N_FSDP)

    own_copies[0].wait_recv()
    fwd_copies[0].start()
    fwd_copies[1].start()
    pair_copies[0].start()
    own_copies[1].wait_recv()
    far_copies[0].start()
    pair_copies[1].start()
    own_copies[2].wait_recv()
    far_copies[1].start()
    pair_copies[2].start()

    arrive(copy_st1, N_FSDP)
    sums, squares, number = merge(st1, N_FSDP, f)
    st2[0, 0:16, :] = sums
    st2[0, 16:32, :] = squares
    st2[0, 32:40, :] = number
    begin(copy_st2, N_DP)

    fwd_copies[0].wait_recv()
    far_copies[2].start()
    pair_copies[3].start()
    fwd_copies[1].wait_recv()
    far_copies[3].start()
    pair_copies[4].start()

    loop(N_DP, lambda k: cot_copy(k).wait_recv(), 1)

    def back_block(b):
        block = cr[idx[DEST + b]]
        kept = jnp.broadcast_to(flags[pl.ds(b, 1), 0:1].astype(BF16), (BLOCK, D))
        cp[rows(b * BLOCK, BLOCK), :] = block * kept

    loop(16, back_block)
    copy_cp = remote(cp, cpp, S_CP, partner, f)
    copy_cp.start()

    arrive(copy_st2, N_DP)
    sums, squares, number = merge(st2, N_DP, dp)
    stat[0:16, :] = sums / TOTAL
    stat[16:32, :] = lax.rsqrt(squares / TOTAL + EPSILON)

    def act_grad(f_of):
        value = lax.dot_general(
            cp[...],
            pan[rows(f_of * 256, 256), :],
            (((1,), (1,)), ((), ())),
            preferred_element_type=F32,
        )
        value = value.astype(BF16).astype(F32)
        ngx[f_of * 2, 8:520, :] = value[:, 0:128]
        ngx[f_of * 2 + 1, 8:520, :] = value[:, 128:256]

    far_copies[0].wait_recv()
    far_copies[1].wait_recv()
    pair_copies[5].start()
    far_copies[2].wait_recv()
    far_copies[3].wait_recv()
    pair_copies[6].start()
    for copy in pair_copies:
        copy.wait_recv()
    loop(N_FSDP, act_grad)

    def activate(j):
        average = stat[pl.ds(j, 1), :]
        inverse = stat[pl.ds(16 + j, 1), :]
        g = gain[pl.ds(j, 1), :]
        b = shift[pl.ds(j, 1), :]
        sum_w = jnp.zeros((8, 128), F32)
        sum_1 = jnp.zeros((8, 128), F32)
        for q in range(4):
            base = 128 * q
            keep = msk[4, base : base + 128, :]
            whitened = (filt[j, base : base + 128, :] - average) * inverse
            normed = whitened * g + b
            logistic = 1.0 / (1.0 + jnp.exp(-normed))
            value = normed * logistic * keep
            slope = logistic + normed * logistic * (1.0 - logistic)
            grad = ngx[j, 8 + base : 136 + base, :] * slope
            filt[j, base : base + 128, :] = whitened
            ngx[j, 8 + base : 136 + base, :] = grad
            act[4 * q : 4 * q + 4, :, lanes(j)] = value.astype(BF16).reshape(4, BLOCK, 128)
            at[j % 2, rows((j // 2) * 128, 128), base : base + 128] = value.T.astype(BF16)
            sum_w = sum_w + jnp.sum((grad * whitened).reshape(16, 8, 128), axis=0)
            sum_1 = sum_1 + jnp.sum(grad.reshape(16, 8, 128), axis=0)
        ng1[0, pl.ds(j, 1), :] = fold(sum_w)
        ng1[0, pl.ds(16 + j, 1), :] = fold(sum_1)
        bsend[0, j] = ngx[j, 8:16, :]
        bsend[1, j] = filt[j, 0:8, :]
        bsend[2, j] = ngx[j, pl.ds(idx[LIVE], 8), :]
        bsend[3, j] = filt[j, pl.ds(idx[LIVE + 2], 8), :]

    loop(CHUNKS, activate)

    copy_ng1 = over_fsdp(ng1, S_NG1)
    copy_ng2 = over_dp(ng2, S_NG2)
    begin(copy_ng1, N_FSDP)
    halo_copies = [
        remote(bsend.at[0], brecv.at[0], S_BHALO, lead // N_FSDP, lead % N_FSDP),
        remote(bsend.at[1], brecv.at[1], S_BHALO + 1, lead // N_FSDP, lead % N_FSDP),
        remote(bsend.at[2], brecv.at[2], S_BHALO + 2, follow // N_FSDP, follow % N_FSDP),
        remote(bsend.at[3], brecv.at[3], S_BHALO + 3, follow // N_FSDP, follow % N_FSDP),
    ]
    for copy in halo_copies:
        copy.start()
    copy_at = remote(at.at[1 - c], atp, S_AT, partner, f)
    copy_at.start()

    def act_block(k):
        return act[idx[SEND + k]]

    ar[0] = act_block(0)

    def act_copy(k):
        return remote(cs.at[k], ar.at[k], S_ACT + k, (dp + k) % N_DP, f)

    def send_act(k):
        cot_copy(k).wait_send()
        cs[k] = act_block(k)
        act_copy(k).start()

    loop(N_DP, send_act, 1)

    arrive(copy_ng1, N_FSDP)
    ng2[0] = ordered(ng1, N_FSDP, f, (32, 128))
    begin(copy_ng2, N_DP)

    copy_cp.wait_recv()
    copy_at.wait_recv()
    first = y * (1 - c) + x * c
    second = x * (1 - c) + y * c

    def first_peer(a):
        return ((x * (1 - c) + a * c) * 4 + zh * 2 + c, (a * (1 - c) + y * c) * 2 + zl)

    def second_peer(b):
        return ((b * (1 - c) + x * c) * 4 + zh * 2 + c, (y * (1 - c) + b * c) * 2 + zl)

    def copy_r1(k):
        a = (first + k) % 4
        return remote(gp.at[a], r1.at[k - 1], S_R1 + k, *first_peer(a))

    def copy_r2(k):
        b = (second + k) % 4
        return remote(s1.at[b], r2.at[k - 1], S_R2 + k, *second_peer(b))

    def copy_r3(k):
        to_z = (z + k) % 4
        return remote(
            s2.at[to_z], r3.at[k - 1], S_R3 + k, x * 4 + (to_z // 2) * 2 + c, y * 2 + to_z % 2
        )

    for k in (1, 2, 3, 4):
        a = (first + k) % 4

        def product(b, a=a):
            y_of = a * (1 - c) + b * c
            x_of = b * (1 - c) + a * c
            d_rows = rows(y_of * 256, 256)
            columns = pl.ds(pl.multiple_of(x_of * 512, 512), 512)
            value = jnp.dot(at[c, d_rows, :], cp[:, columns], preferred_element_type=F32)
            value = value + jnp.dot(
                atp[d_rows, :], cpp[:, columns], preferred_element_type=F32
            )
            for h in range(2):
                for low in range(2):
                    piece = value[low * 128 : low * 128 + 128, h * 256 : h * 256 + 256]
                    gp[a, b, h * 2 + low] = piece.astype(BF16)

        loop(4, product)
        if k < 4:
            copy_r1(k).start()

    arrive(copy_ng2, N_DP)
    ng_total = ordered(ng2, N_DP, dp, (32, 128))
    stat[32:64, :] = ng_total
    for j in range(CHUNKS):
        ngrad[0:1, 128 * j : 128 * j + 128] = ng_total[j : j + 1]
        ngrad[1:2, 128 * j : 128 * j + 128] = ng_total[16 + j : 17 + j]
    for copy in halo_copies:
        copy.wait_recv()

    def back(j):
        taps = kern[:, lanes(j)]
        scale = gain[pl.ds(j, 1), :] * stat[pl.ds(16 + j, 1), :]
        mean_w = stat[pl.ds(32 + j, 1), :] / TOTAL
        mean_1 = stat[pl.ds(48 + j, 1), :] / TOTAL

        def center(grad, whitened):
            return scale * (grad - mean_1 - whitened * mean_w)

        for q in range(4):
            base = 128 * q
            ngx[j, 8 + base : 136 + base, :] = center(
                ngx[j, 8 + base : 136 + base, :], filt[j, base : base + 128, :]
            )
        ngx[j, 520:528, :] = jnp.zeros((8, 128), F32)
        place(
            ngx, j, center(brecv[2, j], brecv[3, j]), center(brecv[0, j], brecv[1, j])
        )

        def part(i, sums):
            base = i * 32
            accum = jnp.zeros((32, 128), F32)
            here = ext[j, pl.ds(pl.multiple_of(base + 8, 8), 32), :]
            new = []
            for tap in range(TAPS):
                window = ngx[j, pl.ds(base + 12 - tap, 32), :]
                window = window * msk[8 - tap, rows(base, 32), :]
                accum = accum + window * taps[tap : tap + 1]
                new.append(sums[tap] + jnp.sum((window * here).reshape(4, 8, 128), axis=0))
            fr[pl.ds(i * 2, 2), :, lanes(j)] = accum.astype(BF16).reshape(2, 16, 128)
            return tuple(new)

        sums = lax.fori_loop(
            0, 16, part, tuple(jnp.zeros((8, 128), F32) for _ in range(TAPS))
        )
        kg[j, 8:16, :] = jnp.zeros((8, 128), F32)
        for tap in range(TAPS):
            kg[j, tap : tap + 1, :] = fold(sums[tap])

    halo_prev.wait_send()
    loop(CHUNKS, back)
    store_igrad = pltpu.make_async_copy(fr, igrad, lsem.at[0])
    store_igrad.start()

    def copy_k1(k):
        peer = (dp + k) % N_DP
        return remote(kg.at[peer], kg1.at[k], S_K1 + k, peer, f)

    begin(copy_k1, N_DP)
    kg1[0] = kg[dp]

    for k in (1, 2, 3):
        copy_r1(k).wait_recv()

    def add_first(b):
        for n in range(4):
            value = gp[first, b, n].astype(F32)
            for k in range(3):
                value = value + r1[k, b, n].astype(F32)
            s1[b, n] = value.astype(BF16)

    loop(4, add_first)
    for k in (1, 2, 3):
        copy_r2(k).start()

    arrive(copy_k1, N_DP)
    kg2[0] = ordered(kg1, N_DP, dp, (16, 128))
    copy_k2 = over_fsdp(kg2, S_K2)
    begin(copy_k2, N_FSDP)

    loop(N_DP, lambda k: act_copy(k).wait_recv(), 1)

    def pick(r):
        cot[r] = ar[idx[PICK + r]]

    loop(12, pick)

    def project(n):
        columns = pl.ds(pl.multiple_of(n * 256, 256), 256)
        value = jnp.dot(cot[...].reshape(ROWS, D), pan[:, columns], preferred_element_type=F32)
        mst[:, columns] = value.astype(BF16)

    loop(4, project)

    for k in (1, 2, 3):
        copy_r2(k).wait_recv()

    def add_second(n):
        value = s1[second, n].astype(F32)
        for k in range(3):
            value = value + r2[k, n].astype(F32)
        s2[n] = value.astype(BF16)

    loop(4, add_second)
    for k in (1, 2, 3):
        copy_r3(k).start()

    arrive(copy_k2, N_FSDP)
    kg3[dp] = ordered(kg2, N_FSDP, f, (16, 128))

    def copy_k3(k):
        return remote(kg3.at[dp], kg3.at[dp], S_K3 + k, (dp + k) % N_DP, f)

    begin(copy_k3, N_DP)

    loop(8, project, 4)
    store_mapped = pltpu.make_async_copy(mst, mapped, lsem.at[1])
    store_mapped.start()

    for k in (1, 2, 3):
        copy_r3(k).wait_recv()
    value = s2[z].astype(F32)
    for k in range(3):
        value = value + r3[k].astype(F32)
    place_of = x * 2 + zh
    pgb[c, place_of] = value.astype(BF16)

    def copy_gather(k):
        to = (place_of + k) % 8
        mine = pgb.at[c, place_of]
        return remote(mine, mine, S_GAT + k, to * 2 + c, f)

    begin(copy_gather, 8)
    arrive(copy_gather, 8)
    copy_gpair = remote(pgb.at[c], pgb.at[c], S_GPAIR, partner, f)
    copy_gpair.start()

    arrive(copy_k3, N_DP)
    for j in range(CHUNKS):
        kgrad[:, 128 * j : 128 * j + 128] = kg3[j, 0:TAPS, :]

    copy_gpair.wait_recv()
    for u in range(8):
        pst[0:128, 256 * u : 256 * u + 256] = pgb[0, u].astype(F32)
        pst[128:256, 256 * u : 256 * u + 256] = pgb[1, u].astype(F32)
    store_pgrad = pltpu.make_async_copy(pst, pgrad, lsem.at[2])
    store_pgrad.start()

    halo_next.wait_send()
    for copy in own_copies + fwd_copies + far_copies + pair_copies + halo_copies:
        copy.wait_send()
    copy_cp.wait_send()
    copy_at.wait_send()
    copy_gpair.wait_send()
    for k in (1, 2, 3):
        copy_r1(k).wait_send()
        copy_r2(k).wait_send()
        copy_r3(k).wait_send()
    for copy in (copy_st2, act_copy, copy_ng2, copy_k1, copy_k3):
        loop(N_DP, lambda k, copy=copy: copy(k).wait_send(), 1)
    for copy in (copy_st1, copy_ng1, copy_k2, copy_gather):
        loop(N_FSDP, lambda k, copy=copy: copy(k).wait_send(), 1)
    store_igrad.wait()
    store_mapped.wait()
    store_pgrad.wait()


def shards(frames, bounds, destinations, kernel, norm_gain, norm_shift, panel, cotangent):
    idx, flags = routing(destinations, lax.axis_index("dp"))
    hbm = pl.BlockSpec(memory_space=pl.ANY)
    vmem = pl.BlockSpec(memory_space=pltpu.VMEM)
    shape = jax.ShapeDtypeStruct
    mapped, input_grad, *rest = pl.pallas_call(
        fused,
        out_shape=(
            shape((ROWS, D), BF16),
            shape((32, 16, D), BF16),
            shape((256, D), F32),
            shape((TAPS, D), F32),
            shape((2, D), F32),
        ),
        in_specs=[pl.BlockSpec(memory_space=pltpu.SMEM), vmem, vmem, hbm, hbm, hbm, vmem, vmem, vmem],
        out_specs=(hbm, hbm, hbm, vmem, vmem),
        scratch_shapes=[
            pltpu.VMEM((32, 16, D), BF16),
            pltpu.VMEM((12, BLOCK, D), BF16),
            pltpu.VMEM((16, BLOCK, D), BF16),
            pltpu.VMEM((16, BLOCK, D), BF16),
            pltpu.VMEM((SLOTS, D), BF16),
            pltpu.VMEM((SLOTS, D), BF16),
            pltpu.VMEM((CHUNKS, 528, 128), F32),
            pltpu.VMEM((CHUNKS, 512, 128), F32),
            pltpu.VMEM((CHUNKS, 528, 128), F32),
            pltpu.VMEM((TAPS, 512, 128), F32),
            pltpu.VMEM((D, D), BF16),
            pltpu.VMEM((16, BLOCK, D), BF16),
            pltpu.VMEM((16, BLOCK, D), BF16),
            pltpu.VMEM((2, 1024, 512), BF16),
            pltpu.VMEM((1024, 512), BF16),
            pltpu.VMEM((4, 4, 4, 128, 256), BF16),
            pltpu.VMEM((3, 4, 4, 128, 256), BF16),
            pltpu.VMEM((4, 4, 128, 256), BF16),
            pltpu.VMEM((3, 4, 128, 256), BF16),
            pltpu.VMEM((4, 128, 256), BF16),
            pltpu.VMEM((3, 128, 256), BF16),
            pltpu.VMEM((2, 8, 128, 256), BF16),
            pltpu.VMEM((256, D), F32),
            pltpu.VMEM((ROWS, D), BF16),
            pltpu.VMEM((16, D), BF16),
            pltpu.VMEM((16, D), BF16),
            pltpu.VMEM((16, D), BF16),
            pltpu.VMEM((N_FSDP, 40, 128), F32),
            pltpu.VMEM((N_DP, 40, 128), F32),
            pltpu.VMEM((64, 128), F32),
            pltpu.VMEM((N_FSDP, 32, 128), F32),
            pltpu.VMEM((N_DP, 32, 128), F32),
            pltpu.VMEM((4, CHUNKS, 8, 128), F32),
            pltpu.VMEM((4, CHUNKS, 8, 128), F32),
            pltpu.VMEM((CHUNKS, 16, 128), F32),
            pltpu.VMEM((N_DP, 16, 128), F32),
            pltpu.VMEM((N_FSDP, 16, 128), F32),
            pltpu.VMEM((CHUNKS, 16, 128), F32),
            pltpu.SemaphoreType.DMA((SEMS.used,)),
            pltpu.SemaphoreType.DMA((SEMS.used,)),
            pltpu.SemaphoreType.DMA((3,)),
        ],
        compiler_params=pltpu.CompilerParams(
            collective_id=0, has_side_effects=True, vmem_limit_bytes=62 * 1024 * 1024
        ),
    )(
        idx,
        flags,
        bounds,
        frames.reshape(32, 16, D),
        cotangent.reshape(12, BLOCK, D),
        panel,
        kernel,
        norm_gain.reshape(CHUNKS, 128),
        norm_shift.reshape(CHUNKS, 128),
    )
    return (mapped, input_grad.reshape(SLOTS, D), *rest)


def solution(mesh):
    placed = (
        P(("dp", "fsdp"), None),
        P(None, ("dp", "fsdp")),
        P(None, "fsdp", None),
        P(),
        P(),
        P(),
        P("fsdp", None),
        P(("dp", "fsdp"), None),
    )
    return jax.shard_map(
        shards,
        mesh=mesh,
        in_specs=placed,
        out_specs=(P(("dp", "fsdp"), None), P(("dp", "fsdp"), None), P("fsdp", None), P(), P()),
        check_vma=False,
    )
```

```python
import jax
import jax.numpy as jnp
from jax import lax
from jax.experimental import pallas as pl
from jax.experimental.pallas import tpu as pltpu
from jax.sharding import PartitionSpec as P

MESH = pl.DeviceIdType.MESH
F32 = jnp.float32
BF16 = jnp.bfloat16
EPSILON = 1e-05

D = 2048
TAPS = 9
BLOCK = 32
SLOTS = 512
ROWS = 384
N_DP = 16
N_FSDP = 8
CHUNKS = D // 128
TOTAL = float(ROWS * N_DP * N_FSDP)

RANK, DEST, SEND, PICK, LIVE = 0, 16, 32, 48, 60


def peer_at(dp, slot):
    return (
        ((dp // 4 + slot // 4) % 4) * 4
        + ((dp // 2 + slot // 2) % 2) * 2
        + (dp + slot) % 2
    )


def slot_of(dp, source):
    return (
        ((dp // 4 - source // 4 + 4) % 4) * 4
        + ((dp // 2 + source // 2) % 2) * 2
        + (dp + source) % 2
    )


def routing(destinations, data_index):
    plan_table = destinations[:, 0, :]
    mine_row = lax.dynamic_index_in_dim(plan_table, data_index, 0, keepdims=False)
    labels = jnp.arange(N_DP, dtype=jnp.int32)
    peers = peer_at(data_index, labels)
    send_match = mine_row[None, :] == peers[:, None]
    send_row = jnp.sum(jnp.where(send_match, labels[None, :], 0), axis=1)
    arrives = jnp.any(plan_table == data_index, axis=1)
    earlier = (labels[None, :] < peers[:, None]) & arrives[None, :]
    rank_row = jnp.minimum(jnp.sum(earlier.astype(jnp.int32), axis=1), 11)
    source_rank = jnp.sum(((labels[None, :] < labels[:, None]) & arrives[None, :]).astype(jnp.int32), axis=1)
    wanted = jnp.arange(12, dtype=jnp.int32)
    chosen = arrives[None, :] & (source_rank[None, :] == wanted[:, None])
    source_slot = slot_of(data_index, labels)
    pick_slot = jnp.sum(jnp.where(chosen, source_slot[None, :], 0), axis=1)
    back_slot = jnp.where(mine_row >= 0, slot_of(data_index, jnp.maximum(mine_row, 0)), 0)
    blocks = jnp.sum((mine_row >= 0).astype(jnp.int32))
    tail = jnp.stack([BLOCK * blocks, 2 * blocks - 1, BLOCK * blocks - 8, blocks])
    idx = jnp.concatenate(
        [rank_row, back_slot, send_row, pick_slot, tail]
    )
    flags = jnp.concatenate([labels < blocks, labels + 1 == blocks]).astype(F32)
    count = jnp.full((8, 128), (BLOCK * blocks).astype(F32))
    return idx, jnp.concatenate([jnp.broadcast_to(flags[:, None], (32, 128)), count])


class Sems:
    def __init__(self):
        self.used = 0

    def take(self, count):
        at = self.used
        self.used += count
        return at


SEMS = Sems()
S_HALO = SEMS.take(2)
S_OWN = SEMS.take(3)
S_FWD = SEMS.take(2)
S_FAR = SEMS.take(4)
S_PAIR = SEMS.take(7)
S_COT = SEMS.take(16)
S_ST1 = SEMS.take(8)
S_ST2 = SEMS.take(16)
S_ACT = SEMS.take(16)
S_AT = SEMS.take(1)
S_CP = SEMS.take(1)
S_NG1 = SEMS.take(8)
S_NG2 = SEMS.take(16)
S_BHALO = SEMS.take(4)
S_R1 = SEMS.take(6)
S_R2 = SEMS.take(4)
S_R3 = SEMS.take(4)
S_GAT = SEMS.take(8)
S_GPAIR = SEMS.take(1)
S_K1 = SEMS.take(16)
S_K2 = SEMS.take(8)
S_K3 = SEMS.take(16)


def fused(
    idx,
    flags,
    bounds,
    frames,
    cotangent,
    panel,
    kern,
    gain,
    shift,
    mapped,
    igrad,
    pgrad,
    kgrad,
    ngrad,
    fr,
    cot,
    cs,
    cr,
    cp,
    cpp,
    ext,
    filt,
    ngx,
    msk,
    pan,
    act,
    ar,
    at,
    atp,
    gp,
    r1,
    rd,
    s1,
    r2,
    s2,
    r3,
    pgb,
    pst,
    mst,
    htrail,
    hprev,
    hnext,
    st1,
    st2,
    stat,
    ng1,
    ng2,
    bsend,
    brecv,
    kg,
    kg1,
    kg2,
    kg3,
    ssem,
    rsem,
    lsem,
):
    dp = lax.axis_index("dp")
    f = lax.axis_index("fsdp")
    c = dp % 2
    zh = (dp // 2) % 2
    x = dp // 4
    y = f // 2
    zl = f % 2
    z = zh * 2 + zl
    partner = dp + 1 - 2 * c
    me = dp * N_FSDP + f
    follow = (me + 1) % (N_DP * N_FSDP)
    lead = (me + N_DP * N_FSDP - 1) % (N_DP * N_FSDP)

    def remote(src, dst, sem, to_dp, to_f):
        return pltpu.make_async_remote_copy(
            src_ref=src,
            dst_ref=dst,
            send_sem=ssem.at[sem],
            recv_sem=rsem.at[sem],
            device_id=(to_dp, to_f),
            device_id_type=MESH,
        )

    def loop(count, body, start=0):
        def step(k, carry):
            body(k)
            return carry

        lax.fori_loop(start, count, step, 0)

    def lanes(j):
        return pl.ds(pl.multiple_of(j * 128, 128), 128)

    def rows(at_row, count):
        return pl.ds(pl.multiple_of(at_row, count), count)

    load_frames = pltpu.make_async_copy(frames, fr, lsem.at[0])
    load_cot = pltpu.make_async_copy(cotangent, cot, lsem.at[1])
    load_panel = pltpu.make_async_copy(panel, pan.at[rows(f * 256, 256)], lsem.at[2])
    load_frames.start()
    load_panel.start()
    load_cot.start()

    barrier = pltpu.get_barrier_semaphore()

    def greet(to_dp, to_f):
        pl.semaphore_signal(barrier, inc=1, device_id=(to_dp, to_f), device_id_type=MESH)

    loop(N_DP, lambda k: greet((dp + k) % N_DP, f), 1)
    loop(N_FSDP, lambda k: greet(dp, (f + k) % N_FSDP), 1)
    greet(follow // N_FSDP, follow % N_FSDP)
    greet(lead // N_FSDP, lead % N_FSDP)
    greet(x * 4 + (1 - zh) * 2 + c, y * 2 + 1 - zl)

    for q in range(4):
        part = slice(128 * q, 128 * q + 128)
        before = jnp.broadcast_to(bounds[0:1, part].astype(F32), (128, 128)).T
        after = jnp.broadcast_to(bounds[1:2, part].astype(F32), (128, 128)).T
        for tap in range(TAPS):
            o = tap - 4
            keep = (before >= float(max(-o, 0))) & (after >= float(max(o, 0)))
            msk[tap, part, :] = jnp.where(keep, 1.0, 0.0)

    def unit(f_of):
        return pan.at[pl.ds(pl.multiple_of(f_of * 256 + c * 128, 128), 128)]

    def half_unit(f_of, h):
        return pan.at[pl.ds(pl.multiple_of(f_of * 256 + c * 128 + h * 64, 64), 64)]

    def shard_at(dy, dz):
        return ((y + dy) % 4) * 2 + (zl + dz) % 2

    f_z, f_up, f_down = shard_at(0, 1), shard_at(1, 0), shard_at(3, 0)
    f_upz, f_downz = shard_at(1, 1), shard_at(3, 1)
    f_far, f_farz = shard_at(2, 0), shard_at(2, 1)

    def send_unit(f_of, sem, to_f):
        return remote(unit(f_of), unit(f_of), sem, dp, to_f)

    def send_half(f_of, h, sem, to_f):
        return remote(half_unit(f_of, h), half_unit(f_of, h), sem, dp, to_f)

    def to_partner(f_of, n):
        return remote(unit(f_of), unit(f_of), S_PAIR + n, partner, f)

    own_copies = [
        send_unit(f, S_OWN, f_z),
        send_unit(f, S_OWN + 1, f_up),
        send_unit(f, S_OWN + 2, f_down),
    ]
    fwd_copies = [send_unit(f_z, S_FWD, f_up), send_unit(f_z, S_FWD + 1, f_down)]
    far_copies = [
        send_half(f_down, 0, S_FAR, f_up),
        send_half(f_up, 1, S_FAR + 1, f_down),
        send_half(f_downz, 0, S_FAR + 2, f_up),
        send_half(f_upz, 1, S_FAR + 3, f_down),
    ]
    pair_copies = [
        to_partner(g, n)
        for n, g in enumerate([f_z, f_down, f_up, f_downz, f_upz, f_far, f_farz])
    ]

    load_frames.wait()
    htrail[...] = fr[idx[LIVE + 1]]

    def widen(j):
        for q in range(4):
            part = fr[8 * q : 8 * q + 8, :, lanes(j)].reshape(128, 128)
            ext[j, 8 + 128 * q : 136 + 128 * q, :] = part.astype(F32)
        ext[j, 0:8, :] = jnp.zeros((8, 128), F32)
        ext[j, 520:528, :] = jnp.zeros((8, 128), F32)

    loop(CHUNKS, widen)

    def conv_at(j, base, count, taps):
        accum = jnp.zeros((count, 128), F32)
        for tap in range(TAPS):
            window = ext[j, pl.ds(base + 4 + tap, count), :] * taps[tap : tap + 1]
            accum = accum + msk[tap, pl.ds(base, count), :] * window
        filt[j, pl.ds(base, count), :] = accum

    def conv(j):
        taps = kern[:, lanes(j)]
        loop(8, lambda i: conv_at(j, pl.multiple_of(i * 64, 64), 64, taps))

    loop(CHUNKS, conv)

    load_cot.wait()
    load_panel.wait()
    pl.semaphore_wait(barrier, 25)

    halo_next = remote(htrail, hprev, S_HALO, follow // N_FSDP, follow % N_FSDP)
    halo_prev = remote(fr.at[0], hnext, S_HALO + 1, lead // N_FSDP, lead % N_FSDP)
    halo_next.start()
    halo_prev.start()
    for copy in own_copies:
        copy.start()

    def same_z(m):
        return (m // 2) * 4 + m % 2

    def other_z(m):
        return (m // 2) * 4 + m % 2 + 2

    def cot_copy(k):
        return remote(cs.at[k], cr.at[k], S_COT + k, peer_at(dp, k), f)

    def send_cot(k):
        cs[k] = cot[idx[RANK + k]]
        cot_copy(k).start()

    cr[0] = cot[idx[RANK]]
    loop(8, lambda m: send_cot(same_z(m)), 1)

    def fill_cot(k):
        cs[k] = cot[idx[RANK + k]]

    loop(8, lambda m: fill_cot(other_z(m)))

    halo_next.wait_recv()
    halo_prev.wait_recv()

    def place(ref, j, previous, following):
        ref[j, 0:8, :] = previous
        for b in range(8, 17):
            at_row = 8 + BLOCK * b
            here = ref[j, at_row : at_row + 8, :]
            last = flags[15 + b : 16 + b, :]
            ref[j, at_row : at_row + 8, :] = here * (1.0 - last) + following * last

    def fold(value):
        return jnp.sum(value, axis=0, keepdims=True)

    def edges(j):
        place(
            ext,
            j,
            hprev[:, lanes(j)].astype(F32)[8:16],
            hnext[:, lanes(j)].astype(F32)[0:8],
        )
        taps = kern[:, lanes(j)]
        conv_at(j, 0, 8, taps)
        for b in range(8, 17):
            conv_at(j, BLOCK * b - 8, 8, taps)

        total = jnp.zeros((8, 128), F32)
        for q in range(8):
            part = filt[j, 64 * q : 64 * q + 64, :]
            total = total + jnp.sum(part.reshape(8, 8, 128), axis=0)
        total = fold(total)
        mean = total / flags[32:33, :]
        squares = jnp.zeros((8, 128), F32)
        for q in range(8):
            off = (filt[j, 64 * q : 64 * q + 64, :] - mean) * msk[4, 64 * q : 64 * q + 64, :]
            squares = squares + jnp.sum((off * off).reshape(8, 8, 128), axis=0)
        st1[0, pl.ds(j, 1), :] = total
        st1[0, pl.ds(16 + j, 1), :] = fold(squares)

    loop(CHUNKS, edges)
    st1[0, 32:40, :] = flags[32:40, :]

    def over_fsdp(buf, sem):
        def copy(k):
            return remote(buf.at[0], buf.at[k], sem + k, dp, (f + k) % N_FSDP)

        return copy

    def over_dp(buf, sem):
        def copy(k):
            return remote(buf.at[0], buf.at[k], sem + k, (dp + k) % N_DP, f)

        return copy

    def begin(copy, count):
        loop(count, lambda k: copy(k).start(), 1)

    def arrive(copy, count):
        loop(count, lambda k: copy(k).wait_recv(), 1)

    def merge(buf, count, mine):
        def slot(p):
            return (mine - p + count) % count

        def add(p, carry):
            sums, number = carry
            return sums + buf[slot(p), 0:16, :], number + buf[slot(p), 32:40, :]

        sums, number = lax.fori_loop(
            0, count, add, (jnp.zeros((16, 128), F32), jnp.zeros((8, 128), F32))
        )
        mean = sums / jnp.concatenate([number, number], axis=0)

        def spread(p, squares):
            n_p = buf[slot(p), 32:40, :]
            n_p = jnp.concatenate([n_p, n_p], axis=0)
            off = buf[slot(p), 0:16, :] / n_p - mean
            return squares + (buf[slot(p), 16:32, :] + n_p * off * off)

        squares = lax.fori_loop(0, count, spread, jnp.zeros((16, 128), F32))
        return sums, squares, number

    def ordered(buf, count, mine, shape):
        def add(p, total):
            return total + buf[(mine - p + count) % count]

        return lax.fori_loop(0, count, add, jnp.zeros(shape, F32))

    copy_st1 = over_fsdp(st1, S_ST1)
    copy_st2 = over_dp(st2, S_ST2)
    begin(copy_st1, N_FSDP)

    own_copies[0].wait_recv()
    fwd_copies[0].start()
    fwd_copies[1].start()
    pair_copies[0].start()
    loop(8, lambda m: cot_copy(other_z(m)).start())
    own_copies[1].wait_recv()
    far_copies[0].start()
    pair_copies[1].start()
    own_copies[2].wait_recv()
    far_copies[1].start()
    pair_copies[2].start()

    arrive(copy_st1, N_FSDP)
    sums, squares, number = merge(st1, N_FSDP, f)
    st2[0, 0:16, :] = sums
    st2[0, 16:32, :] = squares
    st2[0, 32:40, :] = number
    begin(copy_st2, N_DP)

    arrive(copy_st2, N_DP)
    sums, squares, number = merge(st2, N_DP, dp)
    stat[0:16, :] = sums / TOTAL
    stat[16:32, :] = lax.rsqrt(squares / TOTAL + EPSILON)

    def activate(j):
        average = stat[pl.ds(j, 1), :]
        inverse = stat[pl.ds(16 + j, 1), :]
        g = gain[pl.ds(j, 1), :]
        b = shift[pl.ds(j, 1), :]
        for q in range(4):
            base = 128 * q
            keep = msk[4, base : base + 128, :]
            whitened = (filt[j, base : base + 128, :] - average) * inverse
            normed = whitened * g + b
            logistic = 1.0 / (1.0 + jnp.exp(-normed))
            value = normed * logistic * keep
            filt[j, base : base + 128, :] = whitened
            act[4 * q : 4 * q + 4, :, lanes(j)] = value.astype(BF16).reshape(4, BLOCK, 128)
            at[j % 2, rows((j // 2) * 128, 128), base : base + 128] = value.T.astype(BF16)

    loop(CHUNKS, activate)
    copy_at = remote(at.at[1 - c], atp, S_AT, partner, f)
    copy_at.start()

    fwd_copies[0].wait_recv()
    far_copies[2].start()
    pair_copies[3].start()
    fwd_copies[1].wait_recv()
    far_copies[3].start()
    pair_copies[4].start()
    far_copies[0].wait_recv()
    far_copies[1].wait_recv()
    pair_copies[5].start()

    loop(N_DP, lambda k: cot_copy(k).wait_recv(), 1)

    def back_block(b):
        block = cr[idx[DEST + b]]
        kept = jnp.broadcast_to(flags[pl.ds(b, 1), 0:1].astype(BF16), (BLOCK, D))
        cp[rows(b * BLOCK, BLOCK), :] = block * kept

    loop(16, back_block)
    copy_cp = remote(cp, cpp, S_CP, partner, f)
    copy_cp.start()

    ar[0] = act[idx[SEND]]

    def act_copy(k):
        return remote(cs.at[k], ar.at[k], S_ACT + k, peer_at(dp, k), f)

    def send_act(k):
        cot_copy(k).wait_send()
        cs[k] = act[idx[SEND + k]]
        act_copy(k).start()

    loop(N_DP, send_act, 1)

    up, down, across = (y + 1) % 4, (y + 3) % 4, (y + 2) % 4
    f_above, f_below = up * 2 + zl, down * 2 + zl

    def half(ref, h):
        return ref.at[pl.ds(2 * h, 2)]

    across_up = remote(half(gp.at[across], 0), rd.at[0], S_R1, dp, f_above)
    across_down = remote(half(gp.at[across], 1), rd.at[1], S_R1 + 1, dp, f_below)
    plain_up = remote(half(gp.at[up], 1), half(r1.at[0], 1), S_R1 + 2, dp, f_above)
    plain_down = remote(half(gp.at[down], 0), half(r1.at[1], 0), S_R1 + 3, dp, f_below)
    added_up = remote(half(gp.at[up], 0), half(r1.at[0], 0), S_R1 + 4, dp, f_above)
    added_down = remote(half(gp.at[down], 1), half(r1.at[1], 1), S_R1 + 5, dp, f_below)

    def copy_r2(k):
        b = (x + k) % 4
        return remote(s1.at[b], r2.at[k - 1], S_R2 + k, b * 4 + zh * 2 + c, f)

    def copy_r3(k):
        to_z = (z + k) % 4
        return remote(
            s2.at[to_z], r3.at[k - 1], S_R3 + k, x * 4 + (to_z // 2) * 2 + c, y * 2 + to_z % 2
        )

    def products(a):
        def product(b):
            d_rows = rows(a * 256, 256)
            columns = pl.ds(pl.multiple_of(b * 512, 512), 512)
            value = jnp.dot(at[c, d_rows, :], cp[:, columns], preferred_element_type=F32)
            value = value + jnp.dot(
                atp[d_rows, :], cpp[:, columns], preferred_element_type=F32
            )
            for h in range(2):
                for low in range(2):
                    piece = value[low * 128 : low * 128 + 128, h * 256 : h * 256 + 256]
                    gp[a, b, h * 2 + low] = piece.astype(BF16)

        loop(4, product)

    copy_at.wait_recv()
    copy_cp.wait_recv()
    products(across)
    across_up.start()
    across_down.start()
    far_copies[2].wait_recv()
    far_copies[3].wait_recv()
    pair_copies[6].start()
    products(up)
    plain_up.start()
    products(down)
    plain_down.start()
    for copy in pair_copies:
        copy.wait_recv()

    def act_grad(f_of):
        value = lax.dot_general(
            cp[...],
            pan[rows(f_of * 256, 256), :],
            (((1,), (1,)), ((), ())),
            preferred_element_type=F32,
        )
        value = value.astype(BF16).astype(F32)
        ngx[f_of * 2, 8:520, :] = value[:, 0:128]
        ngx[f_of * 2 + 1, 8:520, :] = value[:, 128:256]

    loop(N_FSDP, act_grad)

    def slopes(j):
        g = gain[pl.ds(j, 1), :]
        b = shift[pl.ds(j, 1), :]
        sum_w = jnp.zeros((8, 128), F32)
        sum_1 = jnp.zeros((8, 128), F32)
        for q in range(4):
            base = 128 * q
            whitened = filt[j, base : base + 128, :]
            normed = whitened * g + b
            logistic = 1.0 / (1.0 + jnp.exp(-normed))
            slope = logistic + normed * logistic * (1.0 - logistic)
            grad = ngx[j, 8 + base : 136 + base, :] * slope
            ngx[j, 8 + base : 136 + base, :] = grad
            sum_w = sum_w + jnp.sum((grad * whitened).reshape(16, 8, 128), axis=0)
            sum_1 = sum_1 + jnp.sum(grad.reshape(16, 8, 128), axis=0)
        ng1[0, pl.ds(j, 1), :] = fold(sum_w)
        ng1[0, pl.ds(16 + j, 1), :] = fold(sum_1)
        bsend[0, j] = ngx[j, 8:16, :]
        bsend[1, j] = filt[j, 0:8, :]
        bsend[2, j] = ngx[j, pl.ds(idx[LIVE], 8), :]
        bsend[3, j] = filt[j, pl.ds(idx[LIVE + 2], 8), :]

    loop(CHUNKS, slopes)

    copy_ng1 = over_fsdp(ng1, S_NG1)
    copy_ng2 = over_dp(ng2, S_NG2)
    begin(copy_ng1, N_FSDP)
    halo_copies = [
        remote(bsend.at[0], brecv.at[0], S_BHALO, lead // N_FSDP, lead % N_FSDP),
        remote(bsend.at[1], brecv.at[1], S_BHALO + 1, lead // N_FSDP, lead % N_FSDP),
        remote(bsend.at[2], brecv.at[2], S_BHALO + 2, follow // N_FSDP, follow % N_FSDP),
        remote(bsend.at[3], brecv.at[3], S_BHALO + 3, follow // N_FSDP, follow % N_FSDP),
    ]
    for copy in halo_copies:
        copy.start()

    def pass_on(a, h, n):
        def add(i):
            b, m = i // 4, i % 4
            value = gp[a, 2 * h + b, m].astype(F32) + rd[n, b, m].astype(F32)
            gp[a, 2 * h + b, m] = value.astype(BF16)

        loop(8, add)

    across_up.wait_recv()
    pass_on(up, 0, 0)
    added_up.start()
    across_down.wait_recv()
    pass_on(down, 1, 1)
    added_down.start()

    arrive(copy_ng1, N_FSDP)
    ng2[0] = ordered(ng1, N_FSDP, f, (32, 128))
    begin(copy_ng2, N_DP)
    products(y)

    arrive(copy_ng2, N_DP)
    ng_total = ordered(ng2, N_DP, dp, (32, 128))
    stat[32:64, :] = ng_total
    for j in range(CHUNKS):
        ngrad[0:1, 128 * j : 128 * j + 128] = ng_total[j : j + 1]
        ngrad[1:2, 128 * j : 128 * j + 128] = ng_total[16 + j : 17 + j]
    for copy in halo_copies:
        copy.wait_recv()

    def back(j):
        taps = kern[:, lanes(j)]
        scale = gain[pl.ds(j, 1), :] * stat[pl.ds(16 + j, 1), :]
        mean_w = stat[pl.ds(32 + j, 1), :] / TOTAL
        mean_1 = stat[pl.ds(48 + j, 1), :] / TOTAL

        def center(grad, whitened):
            return scale * (grad - mean_1 - whitened * mean_w)

        for q in range(4):
            base = 128 * q
            ngx[j, 8 + base : 136 + base, :] = center(
                ngx[j, 8 + base : 136 + base, :], filt[j, base : base + 128, :]
            )
        ngx[j, 520:528, :] = jnp.zeros((8, 128), F32)
        place(
            ngx, j, center(brecv[2, j], brecv[3, j]), center(brecv[0, j], brecv[1, j])
        )

        def part(i, sums):
            base = i * 32
            accum = jnp.zeros((32, 128), F32)
            here = ext[j, pl.ds(pl.multiple_of(base + 8, 8), 32), :]
            new = []
            for tap in range(TAPS):
                window = ngx[j, pl.ds(base + 12 - tap, 32), :]
                window = window * msk[8 - tap, rows(base, 32), :]
                accum = accum + window * taps[tap : tap + 1]
                new.append(sums[tap] + jnp.sum((window * here).reshape(4, 8, 128), axis=0))
            fr[pl.ds(i * 2, 2), :, lanes(j)] = accum.astype(BF16).reshape(2, 16, 128)
            return tuple(new)

        sums = lax.fori_loop(
            0, 16, part, tuple(jnp.zeros((8, 128), F32) for _ in range(TAPS))
        )
        kg[j, 8:16, :] = jnp.zeros((8, 128), F32)
        for tap in range(TAPS):
            kg[j, tap : tap + 1, :] = fold(sums[tap])

    halo_prev.wait_send()
    loop(CHUNKS, back)
    store_igrad = pltpu.make_async_copy(fr, igrad, lsem.at[0])
    store_igrad.start()

    def copy_k1(k):
        peer = (dp + k) % N_DP
        return remote(kg.at[peer], kg1.at[k], S_K1 + k, peer, f)

    begin(copy_k1, N_DP)
    kg1[0] = kg[dp]

    for copy in (plain_up, plain_down, added_up, added_down):
        copy.wait_recv()

    def add_first(b):
        for n in range(4):
            value = gp[y, b, n].astype(F32)
            for k in range(2):
                value = value + r1[k, b, n].astype(F32)
            s1[b, n] = value.astype(BF16)

    loop(4, add_first)
    for k in (1, 2, 3):
        copy_r2(k).start()

    arrive(copy_k1, N_DP)
    kg2[0] = ordered(kg1, N_DP, dp, (16, 128))
    copy_k2 = over_fsdp(kg2, S_K2)
    begin(copy_k2, N_FSDP)

    loop(N_DP, lambda k: act_copy(k).wait_recv(), 1)

    def pick(r):
        cot[r] = ar[idx[PICK + r]]

    loop(12, pick)

    def project(n):
        columns = pl.ds(pl.multiple_of(n * 256, 256), 256)
        value = jnp.dot(cot[...].reshape(ROWS, D), pan[:, columns], preferred_element_type=F32)
        mst[:, columns] = value.astype(BF16)

    loop(4, project)

    for k in (1, 2, 3):
        copy_r2(k).wait_recv()

    def add_second(n):
        value = s1[x, n].astype(F32)
        for k in range(3):
            value = value + r2[k, n].astype(F32)
        s2[n] = value

    loop(4, add_second)
    for k in (1, 2, 3):
        copy_r3(k).start()

    arrive(copy_k2, N_FSDP)
    kg3[dp] = ordered(kg2, N_FSDP, f, (16, 128))

    def copy_k3(k):
        return remote(kg3.at[dp], kg3.at[dp], S_K3 + k, (dp + k) % N_DP, f)

    begin(copy_k3, N_DP)

    loop(8, project, 4)
    store_mapped = pltpu.make_async_copy(mst, mapped, lsem.at[1])
    store_mapped.start()

    for k in (1, 2, 3):
        copy_r3(k).wait_recv()
    value = s2[z]
    for k in range(3):
        value = value + r3[k]
    place_of = x * 2 + zh
    pgb[c, place_of] = value.astype(BF16)

    def copy_gather(k):
        to = (place_of + k) % 8
        mine = pgb.at[c, place_of]
        return remote(mine, mine, S_GAT + k, to * 2 + c, f)

    begin(copy_gather, 8)
    arrive(copy_gather, 8)
    copy_gpair = remote(pgb.at[c], pgb.at[c], S_GPAIR, partner, f)
    copy_gpair.start()

    arrive(copy_k3, N_DP)
    for j in range(CHUNKS):
        kgrad[:, 128 * j : 128 * j + 128] = kg3[j, 0:TAPS, :]

    copy_gpair.wait_recv()
    for u in range(8):
        pst[0:128, 256 * u : 256 * u + 256] = pgb[0, u].astype(F32)
        pst[128:256, 256 * u : 256 * u + 256] = pgb[1, u].astype(F32)
    store_pgrad = pltpu.make_async_copy(pst, pgrad, lsem.at[2])
    store_pgrad.start()

    halo_next.wait_send()
    for copy in own_copies + fwd_copies + far_copies + pair_copies + halo_copies:
        copy.wait_send()
    copy_cp.wait_send()
    copy_at.wait_send()
    for copy in (across_up, across_down, plain_up, plain_down, added_up, added_down):
        copy.wait_send()
    copy_gpair.wait_send()
    for k in (1, 2, 3):
        copy_r2(k).wait_send()
        copy_r3(k).wait_send()
    for copy in (copy_st2, act_copy, copy_ng2, copy_k1, copy_k3):
        loop(N_DP, lambda k, copy=copy: copy(k).wait_send(), 1)
    for copy in (copy_st1, copy_ng1, copy_k2, copy_gather):
        loop(N_FSDP, lambda k, copy=copy: copy(k).wait_send(), 1)
    store_igrad.wait()
    store_mapped.wait()
    store_pgrad.wait()


def shards(frames, bounds, destinations, kernel, norm_gain, norm_shift, panel, cotangent):
    idx, flags = routing(destinations, lax.axis_index("dp"))
    hbm = pl.BlockSpec(memory_space=pl.ANY)
    vmem = pl.BlockSpec(memory_space=pltpu.VMEM)
    shape = jax.ShapeDtypeStruct
    mapped, input_grad, *rest = pl.pallas_call(
        fused,
        out_shape=(
            shape((ROWS, D), BF16),
            shape((32, 16, D), BF16),
            shape((256, D), F32),
            shape((TAPS, D), F32),
            shape((2, D), F32),
        ),
        in_specs=[pl.BlockSpec(memory_space=pltpu.SMEM), vmem, vmem, hbm, hbm, hbm, vmem, vmem, vmem],
        out_specs=(hbm, hbm, hbm, vmem, vmem),
        scratch_shapes=[
            pltpu.VMEM((32, 16, D), BF16),
            pltpu.VMEM((12, BLOCK, D), BF16),
            pltpu.VMEM((16, BLOCK, D), BF16),
            pltpu.VMEM((16, BLOCK, D), BF16),
            pltpu.VMEM((SLOTS, D), BF16),
            pltpu.VMEM((SLOTS, D), BF16),
            pltpu.VMEM((CHUNKS, 528, 128), F32),
            pltpu.VMEM((CHUNKS, 512, 128), F32),
            pltpu.VMEM((CHUNKS, 528, 128), F32),
            pltpu.VMEM((TAPS, 512, 128), F32),
            pltpu.VMEM((D, D), BF16),
            pltpu.VMEM((16, BLOCK, D), BF16),
            pltpu.VMEM((16, BLOCK, D), BF16),
            pltpu.VMEM((2, 1024, 512), BF16),
            pltpu.VMEM((1024, 512), BF16),
            pltpu.VMEM((4, 4, 4, 128, 256), BF16),
            pltpu.VMEM((2, 4, 4, 128, 256), BF16),
            pltpu.VMEM((2, 2, 4, 128, 256), BF16),
            pltpu.VMEM((4, 4, 128, 256), BF16),
            pltpu.VMEM((3, 4, 128, 256), BF16),
            pltpu.VMEM((4, 128, 256), F32),
            pltpu.VMEM((3, 128, 256), F32),
            pltpu.VMEM((2, 8, 128, 256), BF16),
            pltpu.VMEM((256, D), F32),
            pltpu.VMEM((ROWS, D), BF16),
            pltpu.VMEM((16, D), BF16),
            pltpu.VMEM((16, D), BF16),
            pltpu.VMEM((16, D), BF16),
            pltpu.VMEM((N_FSDP, 40, 128), F32),
            pltpu.VMEM((N_DP, 40, 128), F32),
            pltpu.VMEM((64, 128), F32),
            pltpu.VMEM((N_FSDP, 32, 128), F32),
            pltpu.VMEM((N_DP, 32, 128), F32),
            pltpu.VMEM((4, CHUNKS, 8, 128), F32),
            pltpu.VMEM((4, CHUNKS, 8, 128), F32),
            pltpu.VMEM((CHUNKS, 16, 128), F32),
            pltpu.VMEM((N_DP, 16, 128), F32),
            pltpu.VMEM((N_FSDP, 16, 128), F32),
            pltpu.VMEM((CHUNKS, 16, 128), F32),
            pltpu.SemaphoreType.DMA((SEMS.used,)),
            pltpu.SemaphoreType.DMA((SEMS.used,)),
            pltpu.SemaphoreType.DMA((3,)),
        ],
        compiler_params=pltpu.CompilerParams(
            collective_id=0, has_side_effects=True, vmem_limit_bytes=62 * 1024 * 1024
        ),
    )(
        idx,
        flags,
        bounds,
        frames.reshape(32, 16, D),
        cotangent.reshape(12, BLOCK, D),
        panel,
        kernel,
        norm_gain.reshape(CHUNKS, 128),
        norm_shift.reshape(CHUNKS, 128),
    )
    return (mapped, input_grad.reshape(SLOTS, D), *rest)


def solution(mesh):
    placed = (
        P(("dp", "fsdp"), None),
        P(None, ("dp", "fsdp")),
        P(None, "fsdp", None),
        P(),
        P(),
        P(),
        P("fsdp", None),
        P(("dp", "fsdp"), None),
    )
    return jax.shard_map(
        shards,
        mesh=mesh,
        in_specs=placed,
        out_specs=(P(("dp", "fsdp"), None), P(("dp", "fsdp"), None), P("fsdp", None), P(), P()),
        check_vma=False,
    )
```

```python
import jax
import jax.numpy as jnp
from jax import lax
from jax.experimental import pallas as pl
from jax.experimental.pallas import tpu as pltpu
from jax.sharding import PartitionSpec as P

MESH = pl.DeviceIdType.MESH
F32 = jnp.float32
BF16 = jnp.bfloat16
EPSILON = 1e-05

D = 2048
TAPS = 9
BLOCK = 32
SLOTS = 512
ROWS = 384
N_DP = 16
N_FSDP = 8
CHUNKS = D // 128
TOTAL = float(ROWS * N_DP * N_FSDP)

RANK, DEST, SEND, PICK, LIVE = 0, 16, 32, 48, 60


def peer_at(dp, slot):
    return (
        ((dp // 4 + slot // 4) % 4) * 4
        + ((dp // 2 + slot // 2) % 2) * 2
        + (dp + slot) % 2
    )


def slot_of(dp, source):
    return (
        ((dp // 4 - source // 4 + 4) % 4) * 4
        + ((dp // 2 + source // 2) % 2) * 2
        + (dp + source) % 2
    )


def routing(destinations, data_index):
    plan_table = destinations[:, 0, :]
    mine_row = lax.dynamic_index_in_dim(plan_table, data_index, 0, keepdims=False)
    labels = jnp.arange(N_DP, dtype=jnp.int32)
    peers = peer_at(data_index, labels)
    send_match = mine_row[None, :] == peers[:, None]
    send_row = jnp.sum(jnp.where(send_match, labels[None, :], 0), axis=1)
    arrives = jnp.any(plan_table == data_index, axis=1)
    earlier = (labels[None, :] < peers[:, None]) & arrives[None, :]
    rank_row = jnp.minimum(jnp.sum(earlier.astype(jnp.int32), axis=1), 11)
    source_rank = jnp.sum(((labels[None, :] < labels[:, None]) & arrives[None, :]).astype(jnp.int32), axis=1)
    wanted = jnp.arange(12, dtype=jnp.int32)
    chosen = arrives[None, :] & (source_rank[None, :] == wanted[:, None])
    source_slot = slot_of(data_index, labels)
    pick_slot = jnp.sum(jnp.where(chosen, source_slot[None, :], 0), axis=1)
    back_slot = jnp.where(mine_row >= 0, slot_of(data_index, jnp.maximum(mine_row, 0)), 0)
    blocks = jnp.sum((mine_row >= 0).astype(jnp.int32))
    tail = jnp.stack([BLOCK * blocks, 2 * blocks - 1, BLOCK * blocks - 8, blocks])
    idx = jnp.concatenate(
        [rank_row, back_slot, send_row, pick_slot, tail]
    )
    flags = jnp.concatenate([labels < blocks, labels + 1 == blocks]).astype(F32)
    count = jnp.full((8, 128), (BLOCK * blocks).astype(F32))
    return idx, jnp.concatenate([jnp.broadcast_to(flags[:, None], (32, 128)), count])


class Sems:
    def __init__(self):
        self.used = 0

    def take(self, count):
        at = self.used
        self.used += count
        return at


SEMS = Sems()
S_HALO = SEMS.take(2)
S_OWN = SEMS.take(3)
S_FWD = SEMS.take(2)
S_FAR = SEMS.take(4)
S_PAIR = SEMS.take(7)
S_COT = SEMS.take(16)
S_ST1 = SEMS.take(8)
S_ST2 = SEMS.take(16)
S_ACT = SEMS.take(16)
S_AT = SEMS.take(1)
S_CP = SEMS.take(1)
S_NG1 = SEMS.take(8)
S_NG2 = SEMS.take(16)
S_BHALO = SEMS.take(4)
S_R1 = SEMS.take(6)
S_R2 = SEMS.take(4)
S_R3 = SEMS.take(4)
S_GAT = SEMS.take(8)
S_GPAIR = SEMS.take(1)
S_K1 = SEMS.take(16)
S_K2 = SEMS.take(8)
S_K3 = SEMS.take(16)


def fused(
    idx,
    flags,
    bounds,
    frames,
    cotangent,
    panel,
    kern,
    gain,
    shift,
    mapped,
    igrad,
    pgrad,
    kgrad,
    ngrad,
    fr,
    cot,
    cs,
    cr,
    cp,
    cpp,
    ext,
    filt,
    ngx,
    msk,
    pan,
    act,
    ar,
    at,
    atp,
    gp,
    r1,
    rd,
    s1,
    r2,
    s2,
    r3,
    pgb,
    mst,
    htrail,
    hprev,
    hnext,
    st1,
    st2,
    stat,
    ng1,
    ng2,
    bsend,
    brecv,
    kg,
    kg1,
    kg2,
    kg3,
    ssem,
    rsem,
    lsem,
):
    dp = lax.axis_index("dp")
    f = lax.axis_index("fsdp")
    c = dp % 2
    zh = (dp // 2) % 2
    x = dp // 4
    y = f // 2
    zl = f % 2
    z = zh * 2 + zl
    partner = dp + 1 - 2 * c
    me = dp * N_FSDP + f
    follow = (me + 1) % (N_DP * N_FSDP)
    lead = (me + N_DP * N_FSDP - 1) % (N_DP * N_FSDP)

    def remote(src, dst, sem, to_dp, to_f):
        return pltpu.make_async_remote_copy(
            src_ref=src,
            dst_ref=dst,
            send_sem=ssem.at[sem],
            recv_sem=rsem.at[sem],
            device_id=(to_dp, to_f),
            device_id_type=MESH,
        )

    def loop(count, body, start=0):
        def step(k, carry):
            body(k)
            return carry

        lax.fori_loop(start, count, step, 0)

    def lanes(j):
        return pl.ds(pl.multiple_of(j * 128, 128), 128)

    def rows(at_row, count):
        return pl.ds(pl.multiple_of(at_row, count), count)

    load_frames = pltpu.make_async_copy(frames, fr, lsem.at[0])
    load_cot = pltpu.make_async_copy(cotangent, cot, lsem.at[1])
    load_panel = pltpu.make_async_copy(panel, pan.at[rows(f * 256, 256)], lsem.at[2])
    load_frames.start()
    load_panel.start()
    load_cot.start()

    barrier = pltpu.get_barrier_semaphore()

    def greet(to_dp, to_f):
        pl.semaphore_signal(barrier, inc=1, device_id=(to_dp, to_f), device_id_type=MESH)

    loop(N_DP, lambda k: greet((dp + k) % N_DP, f), 1)
    loop(N_FSDP, lambda k: greet(dp, (f + k) % N_FSDP), 1)
    greet(follow // N_FSDP, follow % N_FSDP)
    greet(lead // N_FSDP, lead % N_FSDP)
    greet(x * 4 + (1 - zh) * 2 + c, y * 2 + 1 - zl)

    for q in range(4):
        part = slice(128 * q, 128 * q + 128)
        before = jnp.broadcast_to(bounds[0:1, part].astype(F32), (128, 128)).T
        after = jnp.broadcast_to(bounds[1:2, part].astype(F32), (128, 128)).T
        for tap in range(TAPS):
            o = tap - 4
            keep = (before >= float(max(-o, 0))) & (after >= float(max(o, 0)))
            msk[tap, part, :] = jnp.where(keep, 1.0, 0.0)

    def unit(f_of):
        return pan.at[pl.ds(pl.multiple_of(f_of * 256 + c * 128, 128), 128)]

    def half_unit(f_of, h):
        return pan.at[pl.ds(pl.multiple_of(f_of * 256 + c * 128 + h * 64, 64), 64)]

    def shard_at(dy, dz):
        return ((y + dy) % 4) * 2 + (zl + dz) % 2

    f_z, f_up, f_down = shard_at(0, 1), shard_at(1, 0), shard_at(3, 0)
    f_upz, f_downz = shard_at(1, 1), shard_at(3, 1)
    f_far, f_farz = shard_at(2, 0), shard_at(2, 1)

    def send_unit(f_of, sem, to_f):
        return remote(unit(f_of), unit(f_of), sem, dp, to_f)

    def send_half(f_of, h, sem, to_f):
        return remote(half_unit(f_of, h), half_unit(f_of, h), sem, dp, to_f)

    def to_partner(f_of, n):
        return remote(unit(f_of), unit(f_of), S_PAIR + n, partner, f)

    own_copies = [
        send_unit(f, S_OWN, f_z),
        send_unit(f, S_OWN + 1, f_up),
        send_unit(f, S_OWN + 2, f_down),
    ]
    fwd_copies = [send_unit(f_z, S_FWD, f_up), send_unit(f_z, S_FWD + 1, f_down)]
    far_copies = [
        send_half(f_down, 0, S_FAR, f_up),
        send_half(f_up, 1, S_FAR + 1, f_down),
        send_half(f_downz, 0, S_FAR + 2, f_up),
        send_half(f_upz, 1, S_FAR + 3, f_down),
    ]
    pair_copies = [
        to_partner(g, n)
        for n, g in enumerate([f_z, f_down, f_up, f_downz, f_upz, f_far, f_farz])
    ]

    load_frames.wait()
    htrail[...] = fr[idx[LIVE + 1]]

    def widen(j):
        for q in range(4):
            part = fr[8 * q : 8 * q + 8, :, lanes(j)].reshape(128, 128)
            ext[j, 8 + 128 * q : 136 + 128 * q, :] = part.astype(F32)
        ext[j, 0:8, :] = jnp.zeros((8, 128), F32)
        ext[j, 520:528, :] = jnp.zeros((8, 128), F32)

    loop(CHUNKS, widen)

    def conv_at(j, base, count, taps):
        accum = jnp.zeros((count, 128), F32)
        for tap in range(TAPS):
            window = ext[j, pl.ds(base + 4 + tap, count), :] * taps[tap : tap + 1]
            accum = accum + msk[tap, pl.ds(base, count), :] * window
        filt[j, pl.ds(base, count), :] = accum

    def conv(j):
        taps = kern[:, lanes(j)]
        loop(8, lambda i: conv_at(j, pl.multiple_of(i * 64, 64), 64, taps))

    loop(CHUNKS, conv)

    load_cot.wait()
    load_panel.wait()
    pl.semaphore_wait(barrier, 25)

    halo_next = remote(htrail, hprev, S_HALO, follow // N_FSDP, follow % N_FSDP)
    halo_prev = remote(fr.at[0], hnext, S_HALO + 1, lead // N_FSDP, lead % N_FSDP)
    halo_next.start()
    halo_prev.start()
    for copy in own_copies:
        copy.start()

    def same_z(m):
        return (m // 2) * 4 + m % 2

    def other_z(m):
        return (m // 2) * 4 + m % 2 + 2

    def cot_copy(k):
        return remote(cs.at[k], cr.at[k], S_COT + k, peer_at(dp, k), f)

    def send_cot(k):
        cs[k] = cot[idx[RANK + k]]
        cot_copy(k).start()

    cr[0] = cot[idx[RANK]]
    loop(8, lambda m: send_cot(same_z(m)), 1)

    loop(8, lambda m: send_cot(other_z(m)))

    halo_next.wait_recv()
    halo_prev.wait_recv()

    def place(ref, j, previous, following):
        ref[j, 0:8, :] = previous
        for b in range(8, 17):
            at_row = 8 + BLOCK * b
            here = ref[j, at_row : at_row + 8, :]
            last = flags[15 + b : 16 + b, :]
            ref[j, at_row : at_row + 8, :] = here * (1.0 - last) + following * last

    def fold(value):
        return jnp.sum(value, axis=0, keepdims=True)

    def edges(j):
        place(
            ext,
            j,
            hprev[:, lanes(j)].astype(F32)[8:16],
            hnext[:, lanes(j)].astype(F32)[0:8],
        )
        taps = kern[:, lanes(j)]
        conv_at(j, 0, 8, taps)
        for b in range(8, 17):
            conv_at(j, BLOCK * b - 8, 8, taps)

        total = jnp.zeros((8, 128), F32)
        for q in range(8):
            part = filt[j, 64 * q : 64 * q + 64, :]
            total = total + jnp.sum(part.reshape(8, 8, 128), axis=0)
        total = fold(total)
        mean = total / flags[32:33, :]
        squares = jnp.zeros((8, 128), F32)
        for q in range(8):
            off = (filt[j, 64 * q : 64 * q + 64, :] - mean) * msk[4, 64 * q : 64 * q + 64, :]
            squares = squares + jnp.sum((off * off).reshape(8, 8, 128), axis=0)
        st1[0, pl.ds(j, 1), :] = total
        st1[0, pl.ds(16 + j, 1), :] = fold(squares)

    loop(CHUNKS, edges)
    st1[0, 32:40, :] = flags[32:40, :]

    def over_fsdp(buf, sem):
        def copy(k):
            return remote(buf.at[0], buf.at[k], sem + k, dp, (f + k) % N_FSDP)

        return copy

    def over_dp(buf, sem):
        def copy(k):
            return remote(buf.at[0], buf.at[k], sem + k, (dp + k) % N_DP, f)

        return copy

    def begin(copy, count):
        loop(count, lambda k: copy(k).start(), 1)

    def arrive(copy, count):
        loop(count, lambda k: copy(k).wait_recv(), 1)

    def merge(buf, count, mine):
        def slot(p):
            return (mine - p + count) % count

        def add(p, carry):
            sums, number = carry
            return sums + buf[slot(p), 0:16, :], number + buf[slot(p), 32:40, :]

        sums, number = lax.fori_loop(
            0, count, add, (jnp.zeros((16, 128), F32), jnp.zeros((8, 128), F32))
        )
        mean = sums / jnp.concatenate([number, number], axis=0)

        def spread(p, squares):
            n_p = buf[slot(p), 32:40, :]
            n_p = jnp.concatenate([n_p, n_p], axis=0)
            off = buf[slot(p), 0:16, :] / n_p - mean
            return squares + (buf[slot(p), 16:32, :] + n_p * off * off)

        squares = lax.fori_loop(0, count, spread, jnp.zeros((16, 128), F32))
        return sums, squares, number

    def ordered(buf, count, mine, shape):
        def add(p, total):
            return total + buf[(mine - p + count) % count]

        return lax.fori_loop(0, count, add, jnp.zeros(shape, F32))

    copy_st1 = over_fsdp(st1, S_ST1)
    copy_st2 = over_dp(st2, S_ST2)
    begin(copy_st1, N_FSDP)

    own_copies[0].wait_recv()
    fwd_copies[0].start()
    fwd_copies[1].start()
    pair_copies[0].start()
    own_copies[1].wait_recv()
    far_copies[0].start()
    pair_copies[1].start()
    own_copies[2].wait_recv()
    far_copies[1].start()
    pair_copies[2].start()

    arrive(copy_st1, N_FSDP)
    sums, squares, number = merge(st1, N_FSDP, f)
    st2[0, 0:16, :] = sums
    st2[0, 16:32, :] = squares
    st2[0, 32:40, :] = number
    begin(copy_st2, N_DP)

    arrive(copy_st2, N_DP)
    sums, squares, number = merge(st2, N_DP, dp)
    stat[0:16, :] = sums / TOTAL
    stat[16:32, :] = lax.rsqrt(squares / TOTAL + EPSILON)

    def activate(j):
        average = stat[pl.ds(j, 1), :]
        inverse = stat[pl.ds(16 + j, 1), :]
        g = gain[pl.ds(j, 1), :]
        b = shift[pl.ds(j, 1), :]
        for q in range(4):
            base = 128 * q
            keep = msk[4, base : base + 128, :]
            whitened = (filt[j, base : base + 128, :] - average) * inverse
            normed = whitened * g + b
            logistic = 1.0 / (1.0 + jnp.exp(-normed))
            value = normed * logistic * keep
            filt[j, base : base + 128, :] = whitened
            act[4 * q : 4 * q + 4, :, lanes(j)] = value.astype(BF16).reshape(4, BLOCK, 128)
            at[j % 2, rows((j // 2) * 128, 128), base : base + 128] = value.T.astype(BF16)

    loop(CHUNKS, activate)
    copy_at = remote(at.at[1 - c], atp, S_AT, partner, f)
    copy_at.start()

    fwd_copies[0].wait_recv()
    far_copies[2].start()
    pair_copies[3].start()
    fwd_copies[1].wait_recv()
    far_copies[3].start()
    pair_copies[4].start()

    loop(N_DP, lambda k: cot_copy(k).wait_recv(), 1)

    def back_block(b):
        block = cr[idx[DEST + b]]
        kept = jnp.broadcast_to(flags[pl.ds(b, 1), 0:1].astype(BF16), (BLOCK, D))
        cp[rows(b * BLOCK, BLOCK), :] = block * kept

    loop(16, back_block)
    copy_cp = remote(cp, cpp, S_CP, partner, f)
    copy_cp.start()

    ar[0] = act[idx[SEND]]

    def act_copy(k):
        return remote(cs.at[k], ar.at[k], S_ACT + k, peer_at(dp, k), f)

    def send_act(k):
        cot_copy(k).wait_send()
        cs[k] = act[idx[SEND + k]]
        act_copy(k).start()

    loop(N_DP, send_act, 1)

    far_copies[0].wait_recv()
    far_copies[1].wait_recv()
    pair_copies[5].start()

    up, down, across = (y + 1) % 4, (y + 3) % 4, (y + 2) % 4
    f_above, f_below = up * 2 + zl, down * 2 + zl

    def half(ref, h):
        return ref.at[pl.ds(2 * h, 2)]

    across_up = remote(half(gp.at[across], 0), rd.at[0], S_R1, dp, f_above)
    across_down = remote(half(gp.at[across], 1), rd.at[1], S_R1 + 1, dp, f_below)
    plain_up = remote(half(gp.at[up], 1), half(r1.at[0], 1), S_R1 + 2, dp, f_above)
    plain_down = remote(half(gp.at[down], 0), half(r1.at[1], 0), S_R1 + 3, dp, f_below)
    added_up = remote(half(gp.at[up], 0), half(r1.at[0], 0), S_R1 + 4, dp, f_above)
    added_down = remote(half(gp.at[down], 1), half(r1.at[1], 1), S_R1 + 5, dp, f_below)

    def copy_r2(k):
        b = (x + k) % 4
        return remote(s1.at[b], r2.at[k - 1], S_R2 + k, b * 4 + zh * 2 + c, f)

    def copy_r3(k):
        to_z = (z + k) % 4
        return remote(
            s2.at[to_z], r3.at[k - 1], S_R3 + k, x * 4 + (to_z // 2) * 2 + c, y * 2 + to_z % 2
        )

    def products(a):
        def product(b):
            d_rows = rows(a * 256, 256)
            columns = pl.ds(pl.multiple_of(b * 512, 512), 512)
            value = jnp.dot(at[c, d_rows, :], cp[:, columns], preferred_element_type=F32)
            value = value + jnp.dot(
                atp[d_rows, :], cpp[:, columns], preferred_element_type=F32
            )
            for h in range(2):
                for low in range(2):
                    piece = value[low * 128 : low * 128 + 128, h * 256 : h * 256 + 256]
                    gp[a, b, h * 2 + low] = piece.astype(BF16)

        loop(4, product)

    copy_at.wait_recv()
    copy_cp.wait_recv()
    products(across)
    across_up.start()
    across_down.start()
    far_copies[2].wait_recv()
    far_copies[3].wait_recv()
    pair_copies[6].start()
    products(up)
    plain_up.start()
    products(down)
    plain_down.start()
    for copy in pair_copies:
        copy.wait_recv()

    def act_grad(f_of):
        value = lax.dot_general(
            cp[...],
            pan[rows(f_of * 256, 256), :],
            (((1,), (1,)), ((), ())),
            preferred_element_type=F32,
        )
        value = value.astype(BF16).astype(F32)
        ngx[f_of * 2, 8:520, :] = value[:, 0:128]
        ngx[f_of * 2 + 1, 8:520, :] = value[:, 128:256]

    loop(N_FSDP, act_grad)

    def slopes(j):
        g = gain[pl.ds(j, 1), :]
        b = shift[pl.ds(j, 1), :]
        sum_w = jnp.zeros((8, 128), F32)
        sum_1 = jnp.zeros((8, 128), F32)
        for q in range(4):
            base = 128 * q
            whitened = filt[j, base : base + 128, :]
            normed = whitened * g + b
            logistic = 1.0 / (1.0 + jnp.exp(-normed))
            slope = logistic + normed * logistic * (1.0 - logistic)
            grad = ngx[j, 8 + base : 136 + base, :] * slope
            ngx[j, 8 + base : 136 + base, :] = grad
            sum_w = sum_w + jnp.sum((grad * whitened).reshape(16, 8, 128), axis=0)
            sum_1 = sum_1 + jnp.sum(grad.reshape(16, 8, 128), axis=0)
        ng1[0, pl.ds(j, 1), :] = fold(sum_w)
        ng1[0, pl.ds(16 + j, 1), :] = fold(sum_1)
        bsend[0, j] = ngx[j, 8:16, :]
        bsend[1, j] = filt[j, 0:8, :]
        bsend[2, j] = ngx[j, pl.ds(idx[LIVE], 8), :]
        bsend[3, j] = filt[j, pl.ds(idx[LIVE + 2], 8), :]

    loop(CHUNKS, slopes)

    copy_ng1 = over_fsdp(ng1, S_NG1)
    copy_ng2 = over_dp(ng2, S_NG2)
    begin(copy_ng1, N_FSDP)
    halo_copies = [
        remote(bsend.at[0], brecv.at[0], S_BHALO, lead // N_FSDP, lead % N_FSDP),
        remote(bsend.at[1], brecv.at[1], S_BHALO + 1, lead // N_FSDP, lead % N_FSDP),
        remote(bsend.at[2], brecv.at[2], S_BHALO + 2, follow // N_FSDP, follow % N_FSDP),
        remote(bsend.at[3], brecv.at[3], S_BHALO + 3, follow // N_FSDP, follow % N_FSDP),
    ]
    for copy in halo_copies:
        copy.start()

    def pass_on(a, h, n):
        def add(i):
            b, m = i // 4, i % 4
            value = gp[a, 2 * h + b, m].astype(F32) + rd[n, b, m].astype(F32)
            gp[a, 2 * h + b, m] = value.astype(BF16)

        loop(8, add)

    across_up.wait_recv()
    pass_on(up, 0, 0)
    added_up.start()
    across_down.wait_recv()
    pass_on(down, 1, 1)
    added_down.start()

    arrive(copy_ng1, N_FSDP)
    ng2[0] = ordered(ng1, N_FSDP, f, (32, 128))
    begin(copy_ng2, N_DP)
    products(y)

    arrive(copy_ng2, N_DP)
    ng_total = ordered(ng2, N_DP, dp, (32, 128))
    stat[32:64, :] = ng_total
    for j in range(CHUNKS):
        ngrad[0:1, 128 * j : 128 * j + 128] = ng_total[j : j + 1]
        ngrad[1:2, 128 * j : 128 * j + 128] = ng_total[16 + j : 17 + j]
    for copy in halo_copies:
        copy.wait_recv()

    def back(j):
        taps = kern[:, lanes(j)]
        scale = gain[pl.ds(j, 1), :] * stat[pl.ds(16 + j, 1), :]
        mean_w = stat[pl.ds(32 + j, 1), :] / TOTAL
        mean_1 = stat[pl.ds(48 + j, 1), :] / TOTAL

        def center(grad, whitened):
            return scale * (grad - mean_1 - whitened * mean_w)

        for q in range(4):
            base = 128 * q
            ngx[j, 8 + base : 136 + base, :] = center(
                ngx[j, 8 + base : 136 + base, :], filt[j, base : base + 128, :]
            )
        ngx[j, 520:528, :] = jnp.zeros((8, 128), F32)
        place(
            ngx, j, center(brecv[2, j], brecv[3, j]), center(brecv[0, j], brecv[1, j])
        )

        def part(i, sums):
            base = i * 32
            accum = jnp.zeros((32, 128), F32)
            here = ext[j, pl.ds(pl.multiple_of(base + 8, 8), 32), :]
            new = []
            for tap in range(TAPS):
                window = ngx[j, pl.ds(base + 12 - tap, 32), :]
                window = window * msk[8 - tap, rows(base, 32), :]
                accum = accum + window * taps[tap : tap + 1]
                new.append(sums[tap] + jnp.sum((window * here).reshape(4, 8, 128), axis=0))
            fr[pl.ds(i * 2, 2), :, lanes(j)] = accum.astype(BF16).reshape(2, 16, 128)
            return tuple(new)

        sums = lax.fori_loop(
            0, 16, part, tuple(jnp.zeros((8, 128), F32) for _ in range(TAPS))
        )
        kg[j, 8:16, :] = jnp.zeros((8, 128), F32)
        for tap in range(TAPS):
            kg[j, tap : tap + 1, :] = fold(sums[tap])

    halo_prev.wait_send()
    loop(8, back)

    for copy in (plain_up, plain_down, added_up, added_down):
        copy.wait_recv()

    def add_first(b):
        for n in range(4):
            value = gp[y, b, n].astype(F32)
            for k in range(2):
                value = value + r1[k, b, n].astype(F32)
            s1[b, n] = value.astype(BF16)

    loop(4, add_first)
    for k in (1, 2, 3):
        copy_r2(k).start()

    loop(CHUNKS, back, 8)
    store_igrad = pltpu.make_async_copy(fr, igrad, lsem.at[0])
    store_igrad.start()

    def copy_k1(k):
        peer = (dp + k) % N_DP
        return remote(kg.at[peer], kg1.at[k], S_K1 + k, peer, f)

    begin(copy_k1, N_DP)
    kg1[0] = kg[dp]

    arrive(copy_k1, N_DP)
    kg2[0] = ordered(kg1, N_DP, dp, (16, 128))
    copy_k2 = over_fsdp(kg2, S_K2)
    begin(copy_k2, N_FSDP)

    loop(N_DP, lambda k: act_copy(k).wait_recv(), 1)

    def pick(r):
        cot[r] = ar[idx[PICK + r]]

    loop(12, pick)

    def project(n):
        columns = pl.ds(pl.multiple_of(n * 256, 256), 256)
        value = jnp.dot(cot[...].reshape(ROWS, D), pan[:, columns], preferred_element_type=F32)
        mst[:, columns] = value.astype(BF16)

    loop(4, project)

    for k in (1, 2, 3):
        copy_r2(k).wait_recv()

    def add_second(n):
        value = s1[x, n].astype(F32)
        for k in range(3):
            value = value + r2[k, n].astype(F32)
        s2[n] = value

    loop(4, add_second)
    for k in (1, 2, 3):
        copy_r3(k).start()

    arrive(copy_k2, N_FSDP)
    kg3[dp] = ordered(kg2, N_FSDP, f, (16, 128))

    def copy_k3(k):
        return remote(kg3.at[dp], kg3.at[dp], S_K3 + k, (dp + k) % N_DP, f)

    begin(copy_k3, N_DP)

    loop(8, project, 4)
    store_mapped = pltpu.make_async_copy(mst, mapped, lsem.at[1])
    store_mapped.start()

    for k in (1, 2, 3):
        copy_r3(k).wait_recv()
    value = s2[z]
    for k in range(3):
        value = value + r3[k]
    place_of = x * 2 + zh
    pgb[c, place_of] = value.astype(BF16)

    def copy_gather(k):
        to = (place_of + k) % 8
        mine = pgb.at[c, place_of]
        return remote(mine, mine, S_GAT + k, to * 2 + c, f)

    begin(copy_gather, 8)
    arrive(copy_gather, 8)
    copy_gpair = remote(pgb.at[c], pgb.at[c], S_GPAIR, partner, f)
    copy_gpair.start()

    arrive(copy_k3, N_DP)
    for j in range(CHUNKS):
        kgrad[:, 128 * j : 128 * j + 128] = kg3[j, 0:TAPS, :]

    copy_gpair.wait_recv()
    store_pgrad = pltpu.make_async_copy(pgb, pgrad, lsem.at[2])
    store_pgrad.start()

    halo_next.wait_send()
    for copy in own_copies + fwd_copies + far_copies + pair_copies + halo_copies:
        copy.wait_send()
    copy_cp.wait_send()
    copy_at.wait_send()
    for copy in (across_up, across_down, plain_up, plain_down, added_up, added_down):
        copy.wait_send()
    copy_gpair.wait_send()
    for k in (1, 2, 3):
        copy_r2(k).wait_send()
        copy_r3(k).wait_send()
    for copy in (copy_st2, act_copy, copy_ng2, copy_k1, copy_k3):
        loop(N_DP, lambda k, copy=copy: copy(k).wait_send(), 1)
    for copy in (copy_st1, copy_ng1, copy_k2, copy_gather):
        loop(N_FSDP, lambda k, copy=copy: copy(k).wait_send(), 1)
    store_igrad.wait()
    store_mapped.wait()
    store_pgrad.wait()


def finish(mapped, igrad, pieces, kgrad, ngrad, o_mapped, o_igrad, o_pgrad, o_kgrad, o_ngrad, sems):
    copies = [
        pltpu.make_async_copy(source, target, sems.at[n])
        for n, (source, target) in enumerate(
            [(igrad, o_igrad), (mapped, o_mapped), (kgrad, o_kgrad), (ngrad, o_ngrad)]
        )
    ]
    for copy in copies:
        copy.start()
    for half in range(2):
        for u in range(8):
            o_pgrad[128 * half : 128 * half + 128, 256 * u : 256 * u + 256] = pieces[
                half, u
            ].astype(F32)
    for copy in copies:
        copy.wait()


def shards(frames, bounds, destinations, kernel, norm_gain, norm_shift, panel, cotangent):
    idx, flags = routing(destinations, lax.axis_index("dp"))
    hbm = pl.BlockSpec(memory_space=pl.ANY)
    vmem = pl.BlockSpec(memory_space=pltpu.VMEM)
    shape = jax.ShapeDtypeStruct
    mapped, input_grad, *rest = pl.pallas_call(
        fused,
        out_shape=(
            shape((ROWS, D), BF16),
            shape((32, 16, D), BF16),
            shape((2, 8, 128, 256), BF16),
            shape((TAPS, D), F32),
            shape((2, D), F32),
        ),
        in_specs=[pl.BlockSpec(memory_space=pltpu.SMEM), vmem, vmem, hbm, hbm, hbm, vmem, vmem, vmem],
        out_specs=(hbm, hbm, hbm, vmem, vmem),
        scratch_shapes=[
            pltpu.VMEM((32, 16, D), BF16),
            pltpu.VMEM((12, BLOCK, D), BF16),
            pltpu.VMEM((16, BLOCK, D), BF16),
            pltpu.VMEM((16, BLOCK, D), BF16),
            pltpu.VMEM((SLOTS, D), BF16),
            pltpu.VMEM((SLOTS, D), BF16),
            pltpu.VMEM((CHUNKS, 528, 128), F32),
            pltpu.VMEM((CHUNKS, 512, 128), F32),
            pltpu.VMEM((CHUNKS, 528, 128), F32),
            pltpu.VMEM((TAPS, 512, 128), F32),
            pltpu.VMEM((D, D), BF16),
            pltpu.VMEM((16, BLOCK, D), BF16),
            pltpu.VMEM((16, BLOCK, D), BF16),
            pltpu.VMEM((2, 1024, 512), BF16),
            pltpu.VMEM((1024, 512), BF16),
            pltpu.VMEM((4, 4, 4, 128, 256), BF16),
            pltpu.VMEM((2, 4, 4, 128, 256), BF16),
            pltpu.VMEM((2, 2, 4, 128, 256), BF16),
            pltpu.VMEM((4, 4, 128, 256), BF16),
            pltpu.VMEM((3, 4, 128, 256), BF16),
            pltpu.VMEM((4, 128, 256), F32),
            pltpu.VMEM((3, 128, 256), F32),
            pltpu.VMEM((2, 8, 128, 256), BF16),
            pltpu.VMEM((ROWS, D), BF16),
            pltpu.VMEM((16, D), BF16),
            pltpu.VMEM((16, D), BF16),
            pltpu.VMEM((16, D), BF16),
            pltpu.VMEM((N_FSDP, 40, 128), F32),
            pltpu.VMEM((N_DP, 40, 128), F32),
            pltpu.VMEM((64, 128), F32),
            pltpu.VMEM((N_FSDP, 32, 128), F32),
            pltpu.VMEM((N_DP, 32, 128), F32),
            pltpu.VMEM((4, CHUNKS, 8, 128), F32),
            pltpu.VMEM((4, CHUNKS, 8, 128), F32),
            pltpu.VMEM((CHUNKS, 16, 128), F32),
            pltpu.VMEM((N_DP, 16, 128), F32),
            pltpu.VMEM((N_FSDP, 16, 128), F32),
            pltpu.VMEM((CHUNKS, 16, 128), F32),
            pltpu.SemaphoreType.DMA((SEMS.used,)),
            pltpu.SemaphoreType.DMA((SEMS.used,)),
            pltpu.SemaphoreType.DMA((3,)),
        ],
        compiler_params=pltpu.CompilerParams(
            collective_id=0, has_side_effects=True, vmem_limit_bytes=62 * 1024 * 1024
        ),
    )(
        idx,
        flags,
        bounds,
        frames.reshape(32, 16, D),
        cotangent.reshape(12, BLOCK, D),
        panel,
        kernel,
        norm_gain.reshape(CHUNKS, 128),
        norm_shift.reshape(CHUNKS, 128),
    )
    results = (mapped, input_grad, *rest)
    mapped, input_grad, *rest = pl.pallas_call(
        finish,
        out_shape=(
            shape((ROWS, D), BF16),
            shape((32, 16, D), BF16),
            shape((256, D), F32),
            shape((TAPS, D), F32),
            shape((2, D), F32),
        ),
        in_specs=[hbm, hbm, vmem, hbm, hbm],
        out_specs=(hbm, hbm, vmem, hbm, hbm),
        scratch_shapes=[pltpu.SemaphoreType.DMA((4,))],
        compiler_params=pltpu.CompilerParams(vmem_limit_bytes=60 * 1024 * 1024),
    )(*results)
    return (mapped, input_grad.reshape(SLOTS, D), *rest)


def solution(mesh):
    placed = (
        P(("dp", "fsdp"), None),
        P(None, ("dp", "fsdp")),
        P(None, "fsdp", None),
        P(),
        P(),
        P(),
        P("fsdp", None),
        P(("dp", "fsdp"), None),
    )
    return jax.shard_map(
        shards,
        mesh=mesh,
        in_specs=placed,
        out_specs=(P(("dp", "fsdp"), None), P(("dp", "fsdp"), None), P("fsdp", None), P(), P()),
        check_vma=False,
    )
```

```python
import jax
import jax.numpy as jnp
from jax import lax
from jax.experimental import pallas as pl
from jax.experimental.pallas import tpu as pltpu
from jax.sharding import PartitionSpec as P

MESH = pl.DeviceIdType.MESH
F32 = jnp.float32
BF16 = jnp.bfloat16
EPSILON = 1e-05

D = 2048
TAPS = 9
BLOCK = 32
SLOTS = 512
ROWS = 384
N_DP = 16
N_FSDP = 8
CHUNKS = D // 128
TOTAL = float(ROWS * N_DP * N_FSDP)

RANK, DEST, SEND, PICK, LIVE = 0, 16, 32, 48, 60


def peer_at(dp, slot):
    return (
        ((dp // 4 + slot // 4) % 4) * 4
        + ((dp // 2 + slot // 2) % 2) * 2
        + (dp + slot) % 2
    )


def slot_of(dp, source):
    return (
        ((dp // 4 - source // 4 + 4) % 4) * 4
        + ((dp // 2 + source // 2) % 2) * 2
        + (dp + source) % 2
    )


def routing(dest, idx, flags):
    dp = lax.axis_index("dp")
    mine = [dest[dp, 0, b] for b in range(16)]
    blocks = jnp.int32(0)
    for b in range(16):
        live = (mine[b] >= 0).astype(jnp.int32)
        blocks = blocks + live
        idx[DEST + b] = live * slot_of(dp, jnp.maximum(mine[b], 0))
        flags[b : b + 1, :] = jnp.full((1, 128), live.astype(F32), F32)

    def sends(k, carry):
        peer = peer_at(dp, k)
        block = jnp.int32(0)
        for b in range(16):
            block = jnp.where(mine[b] == peer, b, block)
        idx[SEND + k] = block
        return carry

    lax.fori_loop(0, N_DP, sends, 0)

    def ranks(source, count):
        arrives = jnp.int32(0)
        for b in range(16):
            arrives = jnp.where(dest[source, 0, b] == dp, 1, arrives)
        idx[64 + source] = jnp.minimum(count, 11)
        idx[80 + source] = jnp.where(arrives == 1, count, -1)
        return count + arrives

    lax.fori_loop(0, N_DP, ranks, jnp.int32(0))

    def by_slot(k, carry):
        idx[RANK + k] = idx[64 + peer_at(dp, k)]
        return carry

    lax.fori_loop(0, N_DP, by_slot, 0)

    def picks(wanted, carry):
        slot = jnp.int32(0)
        for source in range(N_DP):
            slot = jnp.where(idx[80 + source] == wanted, slot_of(dp, source), slot)
        idx[PICK + wanted] = slot
        return carry

    lax.fori_loop(0, 12, picks, 0)
    for b in range(16):
        last = (blocks == b + 1).astype(F32)
        flags[16 + b : 17 + b, :] = jnp.full((1, 128), last, F32)
    flags[32:40, :] = jnp.full((8, 128), (blocks * BLOCK).astype(F32), F32)
    idx[LIVE] = BLOCK * blocks
    idx[LIVE + 1] = 2 * blocks - 1
    idx[LIVE + 2] = BLOCK * blocks - 8


class Sems:
    def __init__(self):
        self.used = 0

    def take(self, count):
        at = self.used
        self.used += count
        return at


SEMS = Sems()
S_HALO = SEMS.take(2)
S_OWN = SEMS.take(3)
S_FWD = SEMS.take(2)
S_FAR = SEMS.take(4)
S_PAIR = SEMS.take(7)
S_COT = SEMS.take(16)
S_ST1 = SEMS.take(8)
S_ST2 = SEMS.take(16)
S_ACT = SEMS.take(16)
S_AT = SEMS.take(1)
S_CP = SEMS.take(1)
S_NG1 = SEMS.take(8)
S_NG2 = SEMS.take(16)
S_BHALO = SEMS.take(4)
S_R1 = SEMS.take(6)
S_R2 = SEMS.take(4)
S_R3 = SEMS.take(4)
S_GAT = SEMS.take(8)
S_GPAIR = SEMS.take(1)
S_K1 = SEMS.take(16)
S_K2 = SEMS.take(8)
S_K3 = SEMS.take(16)


def fused(
    idx,
    flags,
    bounds,
    frames,
    cotangent,
    panel,
    kern,
    gain,
    shift,
    mapped,
    igrad,
    pgrad,
    kgrad,
    ngrad,
    fr,
    cot,
    cs,
    cr,
    cp,
    cpp,
    ext,
    filt,
    ngx,
    msk,
    pan,
    act,
    ar,
    at,
    atp,
    gp,
    r1,
    rd,
    s1,
    r2,
    s2,
    r3,
    pgb,
    mst,
    htrail,
    hprev,
    hnext,
    st1,
    st2,
    stat,
    ng1,
    ng2,
    bsend,
    brecv,
    kg,
    kg1,
    kg2,
    kg3,
    ssem,
    rsem,
    lsem,
):
    dp = lax.axis_index("dp")
    f = lax.axis_index("fsdp")
    c = dp % 2
    zh = (dp // 2) % 2
    x = dp // 4
    y = f // 2
    zl = f % 2
    z = zh * 2 + zl
    partner = dp + 1 - 2 * c
    me = dp * N_FSDP + f
    follow = (me + 1) % (N_DP * N_FSDP)
    lead = (me + N_DP * N_FSDP - 1) % (N_DP * N_FSDP)

    def remote(src, dst, sem, to_dp, to_f):
        return pltpu.make_async_remote_copy(
            src_ref=src,
            dst_ref=dst,
            send_sem=ssem.at[sem],
            recv_sem=rsem.at[sem],
            device_id=(to_dp, to_f),
            device_id_type=MESH,
        )

    def loop(count, body, start=0):
        def step(k, carry):
            body(k)
            return carry

        lax.fori_loop(start, count, step, 0)

    def lanes(j):
        return pl.ds(pl.multiple_of(j * 128, 128), 128)

    def rows(at_row, count):
        return pl.ds(pl.multiple_of(at_row, count), count)

    load_frames = pltpu.make_async_copy(frames, fr, lsem.at[0])
    load_cot = pltpu.make_async_copy(cotangent, cot, lsem.at[1])
    load_panel = pltpu.make_async_copy(panel, pan.at[rows(f * 256, 256)], lsem.at[2])
    load_frames.start()
    load_panel.start()
    load_cot.start()

    barrier = pltpu.get_barrier_semaphore()

    def greet(to_dp, to_f):
        pl.semaphore_signal(barrier, inc=1, device_id=(to_dp, to_f), device_id_type=MESH)

    loop(N_DP, lambda k: greet((dp + k) % N_DP, f), 1)
    loop(N_FSDP, lambda k: greet(dp, (f + k) % N_FSDP), 1)
    greet(follow // N_FSDP, follow % N_FSDP)
    greet(lead // N_FSDP, lead % N_FSDP)
    greet(x * 4 + (1 - zh) * 2 + c, y * 2 + 1 - zl)

    for q in range(4):
        part = slice(128 * q, 128 * q + 128)
        before = jnp.broadcast_to(bounds[0:1, part].astype(F32), (128, 128)).T
        after = jnp.broadcast_to(bounds[1:2, part].astype(F32), (128, 128)).T
        for tap in range(TAPS):
            o = tap - 4
            keep = (before >= float(max(-o, 0))) & (after >= float(max(o, 0)))
            msk[tap, part, :] = jnp.where(keep, 1.0, 0.0)

    def unit(f_of):
        return pan.at[pl.ds(pl.multiple_of(f_of * 256 + c * 128, 128), 128)]

    def half_unit(f_of, h):
        return pan.at[pl.ds(pl.multiple_of(f_of * 256 + c * 128 + h * 64, 64), 64)]

    def shard_at(dy, dz):
        return ((y + dy) % 4) * 2 + (zl + dz) % 2

    f_z, f_up, f_down = shard_at(0, 1), shard_at(1, 0), shard_at(3, 0)
    f_upz, f_downz = shard_at(1, 1), shard_at(3, 1)
    f_far, f_farz = shard_at(2, 0), shard_at(2, 1)

    def send_unit(f_of, sem, to_f):
        return remote(unit(f_of), unit(f_of), sem, dp, to_f)

    def send_half(f_of, h, sem, to_f):
        return remote(half_unit(f_of, h), half_unit(f_of, h), sem, dp, to_f)

    def to_partner(f_of, n):
        return remote(unit(f_of), unit(f_of), S_PAIR + n, partner, f)

    own_copies = [
        send_unit(f, S_OWN, f_z),
        send_unit(f, S_OWN + 1, f_up),
        send_unit(f, S_OWN + 2, f_down),
    ]
    fwd_copies = [send_unit(f_z, S_FWD, f_up), send_unit(f_z, S_FWD + 1, f_down)]
    far_copies = [
        send_half(f_down, 0, S_FAR, f_up),
        send_half(f_up, 1, S_FAR + 1, f_down),
        send_half(f_downz, 0, S_FAR + 2, f_up),
        send_half(f_upz, 1, S_FAR + 3, f_down),
    ]
    pair_copies = [
        to_partner(g, n)
        for n, g in enumerate([f_z, f_down, f_up, f_downz, f_upz, f_far, f_farz])
    ]

    load_frames.wait()
    htrail[...] = fr[idx[LIVE + 1]]

    def widen(j):
        for q in range(4):
            part = fr[8 * q : 8 * q + 8, :, lanes(j)].reshape(128, 128)
            ext[j, 8 + 128 * q : 136 + 128 * q, :] = part.astype(F32)
        ext[j, 0:8, :] = jnp.zeros((8, 128), F32)
        ext[j, 520:528, :] = jnp.zeros((8, 128), F32)

    loop(CHUNKS, widen)

    def conv_at(j, base, count, taps):
        accum = jnp.zeros((count, 128), F32)
        for tap in range(TAPS):
            window = ext[j, pl.ds(base + 4 + tap, count), :] * taps[tap : tap + 1]
            accum = accum + msk[tap, pl.ds(base, count), :] * window
        filt[j, pl.ds(base, count), :] = accum

    def conv(j):
        taps = kern[:, lanes(j)]
        loop(8, lambda i: conv_at(j, pl.multiple_of(i * 64, 64), 64, taps))

    loop(CHUNKS, conv)

    load_cot.wait()
    load_panel.wait()
    pl.semaphore_wait(barrier, 25)

    halo_next = remote(htrail, hprev, S_HALO, follow // N_FSDP, follow % N_FSDP)
    halo_prev = remote(fr.at[0], hnext, S_HALO + 1, lead // N_FSDP, lead % N_FSDP)
    halo_next.start()
    halo_prev.start()
    for copy in own_copies:
        copy.start()

    def same_z(m):
        return (m // 2) * 4 + m % 2

    def other_z(m):
        return (m // 2) * 4 + m % 2 + 2

    def cot_copy(k):
        return remote(cs.at[k], cr.at[k], S_COT + k, peer_at(dp, k), f)

    def send_cot(k):
        cs[k] = cot[idx[RANK + k]]
        cot_copy(k).start()

    cr[0] = cot[idx[RANK]]
    loop(8, lambda m: send_cot(same_z(m)), 1)

    loop(8, lambda m: send_cot(other_z(m)))

    halo_next.wait_recv()
    halo_prev.wait_recv()

    def place(ref, j, previous, following):
        ref[j, 0:8, :] = previous
        for b in range(8, 17):
            at_row = 8 + BLOCK * b
            here = ref[j, at_row : at_row + 8, :]
            last = flags[15 + b : 16 + b, :]
            ref[j, at_row : at_row + 8, :] = here * (1.0 - last) + following * last

    def fold(value):
        return jnp.sum(value, axis=0, keepdims=True)

    def edges(j):
        place(
            ext,
            j,
            hprev[:, lanes(j)].astype(F32)[8:16],
            hnext[:, lanes(j)].astype(F32)[0:8],
        )
        taps = kern[:, lanes(j)]
        conv_at(j, 0, 8, taps)
        for b in range(8, 17):
            conv_at(j, BLOCK * b - 8, 8, taps)

        total = jnp.zeros((8, 128), F32)
        for q in range(8):
            part = filt[j, 64 * q : 64 * q + 64, :]
            total = total + jnp.sum(part.reshape(8, 8, 128), axis=0)
        total = fold(total)
        mean = total / flags[32:33, :]
        squares = jnp.zeros((8, 128), F32)
        for q in range(8):
            off = (filt[j, 64 * q : 64 * q + 64, :] - mean) * msk[4, 64 * q : 64 * q + 64, :]
            squares = squares + jnp.sum((off * off).reshape(8, 8, 128), axis=0)
        st1[0, pl.ds(j, 1), :] = total
        st1[0, pl.ds(16 + j, 1), :] = fold(squares)

    loop(CHUNKS, edges)
    st1[0, 32:40, :] = flags[32:40, :]

    def over_fsdp(buf, sem):
        def copy(k):
            return remote(buf.at[0], buf.at[k], sem + k, dp, (f + k) % N_FSDP)

        return copy

    def over_dp(buf, sem):
        def copy(k):
            return remote(buf.at[0], buf.at[k], sem + k, (dp + k) % N_DP, f)

        return copy

    def begin(copy, count):
        loop(count, lambda k: copy(k).start(), 1)

    def arrive(copy, count):
        loop(count, lambda k: copy(k).wait_recv(), 1)

    def merge(buf, count, mine):
        def slot(p):
            return (mine - p + count) % count

        def add(p, carry):
            sums, number = carry
            return sums + buf[slot(p), 0:16, :], number + buf[slot(p), 32:40, :]

        sums, number = lax.fori_loop(
            0, count, add, (jnp.zeros((16, 128), F32), jnp.zeros((8, 128), F32))
        )
        mean = sums / jnp.concatenate([number, number], axis=0)

        def spread(p, squares):
            n_p = buf[slot(p), 32:40, :]
            n_p = jnp.concatenate([n_p, n_p], axis=0)
            off = buf[slot(p), 0:16, :] / n_p - mean
            return squares + (buf[slot(p), 16:32, :] + n_p * off * off)

        squares = lax.fori_loop(0, count, spread, jnp.zeros((16, 128), F32))
        return sums, squares, number

    def ordered(buf, count, mine, shape):
        def add(p, total):
            return total + buf[(mine - p + count) % count]

        return lax.fori_loop(0, count, add, jnp.zeros(shape, F32))

    copy_st1 = over_fsdp(st1, S_ST1)
    copy_st2 = over_dp(st2, S_ST2)
    begin(copy_st1, N_FSDP)

    own_copies[0].wait_recv()
    fwd_copies[0].start()
    fwd_copies[1].start()
    pair_copies[0].start()
    own_copies[1].wait_recv()
    far_copies[0].start()
    pair_copies[1].start()
    own_copies[2].wait_recv()
    far_copies[1].start()
    pair_copies[2].start()

    arrive(copy_st1, N_FSDP)
    sums, squares, number = merge(st1, N_FSDP, f)
    st2[0, 0:16, :] = sums
    st2[0, 16:32, :] = squares
    st2[0, 32:40, :] = number
    begin(copy_st2, N_DP)

    arrive(copy_st2, N_DP)
    sums, squares, number = merge(st2, N_DP, dp)
    stat[0:16, :] = sums / TOTAL
    stat[16:32, :] = lax.rsqrt(squares / TOTAL + EPSILON)

    def activate(j):
        average = stat[pl.ds(j, 1), :]
        inverse = stat[pl.ds(16 + j, 1), :]
        g = gain[pl.ds(j, 1), :]
        b = shift[pl.ds(j, 1), :]
        for q in range(4):
            base = 128 * q
            keep = msk[4, base : base + 128, :]
            whitened = (filt[j, base : base + 128, :] - average) * inverse
            normed = whitened * g + b
            logistic = 1.0 / (1.0 + jnp.exp(-normed))
            value = normed * logistic * keep
            filt[j, base : base + 128, :] = whitened
            act[4 * q : 4 * q + 4, :, lanes(j)] = value.astype(BF16).reshape(4, BLOCK, 128)
            at[j % 2, rows((j // 2) * 128, 128), base : base + 128] = value.T.astype(BF16)

    loop(CHUNKS, activate)
    copy_at = remote(at.at[1 - c], atp, S_AT, partner, f)
    copy_at.start()

    fwd_copies[0].wait_recv()
    far_copies[2].start()
    pair_copies[3].start()
    fwd_copies[1].wait_recv()
    far_copies[3].start()
    pair_copies[4].start()

    loop(N_DP, lambda k: cot_copy(k).wait_recv(), 1)

    def back_block(b):
        block = cr[idx[DEST + b]]
        kept = jnp.broadcast_to(flags[pl.ds(b, 1), 0:1].astype(BF16), (BLOCK, D))
        cp[rows(b * BLOCK, BLOCK), :] = block * kept

    loop(16, back_block)
    copy_cp = remote(cp, cpp, S_CP, partner, f)
    copy_cp.start()

    ar[0] = act[idx[SEND]]

    def act_copy(k):
        return remote(cs.at[k], ar.at[k], S_ACT + k, peer_at(dp, k), f)

    def send_act(k):
        cot_copy(k).wait_send()
        cs[k] = act[idx[SEND + k]]
        act_copy(k).start()

    loop(N_DP, send_act, 1)

    far_copies[0].wait_recv()
    far_copies[1].wait_recv()
    pair_copies[5].start()

    up, down, across = (y + 1) % 4, (y + 3) % 4, (y + 2) % 4
    f_above, f_below = up * 2 + zl, down * 2 + zl

    def half(ref, h):
        return ref.at[pl.ds(2 * h, 2)]

    across_up = remote(half(gp.at[across], 0), rd.at[0], S_R1, dp, f_above)
    across_down = remote(half(gp.at[across], 1), rd.at[1], S_R1 + 1, dp, f_below)
    plain_up = remote(half(gp.at[up], 1), half(r1.at[0], 1), S_R1 + 2, dp, f_above)
    plain_down = remote(half(gp.at[down], 0), half(r1.at[1], 0), S_R1 + 3, dp, f_below)
    added_up = remote(half(gp.at[up], 0), half(r1.at[0], 0), S_R1 + 4, dp, f_above)
    added_down = remote(half(gp.at[down], 1), half(r1.at[1], 1), S_R1 + 5, dp, f_below)

    def copy_r2(k):
        b = (x + k) % 4
        return remote(s1.at[b], r2.at[k - 1], S_R2 + k, b * 4 + zh * 2 + c, f)

    def copy_r3(k):
        to_z = (z + k) % 4
        return remote(
            s2.at[to_z], r3.at[k - 1], S_R3 + k, x * 4 + (to_z // 2) * 2 + c, y * 2 + to_z % 2
        )

    def products(a):
        def product(b):
            d_rows = rows(a * 256, 256)
            columns = pl.ds(pl.multiple_of(b * 512, 512), 512)
            value = jnp.dot(at[c, d_rows, :], cp[:, columns], preferred_element_type=F32)
            value = value + jnp.dot(
                atp[d_rows, :], cpp[:, columns], preferred_element_type=F32
            )
            for h in range(2):
                for low in range(2):
                    piece = value[low * 128 : low * 128 + 128, h * 256 : h * 256 + 256]
                    gp[a, b, h * 2 + low] = piece.astype(BF16)

        loop(4, product)

    copy_at.wait_recv()
    copy_cp.wait_recv()
    products(across)
    across_up.start()
    across_down.start()
    far_copies[2].wait_recv()
    far_copies[3].wait_recv()
    pair_copies[6].start()
    products(up)
    plain_up.start()
    products(down)
    plain_down.start()
    for copy in pair_copies:
        copy.wait_recv()

    def act_grad(f_of):
        value = lax.dot_general(
            cp[...],
            pan[rows(f_of * 256, 256), :],
            (((1,), (1,)), ((), ())),
            preferred_element_type=F32,
        )
        value = value.astype(BF16).astype(F32)
        ngx[f_of * 2, 8:520, :] = value[:, 0:128]
        ngx[f_of * 2 + 1, 8:520, :] = value[:, 128:256]

    loop(N_FSDP, act_grad)

    def slopes(j):
        g = gain[pl.ds(j, 1), :]
        b = shift[pl.ds(j, 1), :]
        sum_w = jnp.zeros((8, 128), F32)
        sum_1 = jnp.zeros((8, 128), F32)
        for q in range(4):
            base = 128 * q
            whitened = filt[j, base : base + 128, :]
            normed = whitened * g + b
            logistic = 1.0 / (1.0 + jnp.exp(-normed))
            slope = logistic + normed * logistic * (1.0 - logistic)
            grad = ngx[j, 8 + base : 136 + base, :] * slope
            ngx[j, 8 + base : 136 + base, :] = grad
            sum_w = sum_w + jnp.sum((grad * whitened).reshape(16, 8, 128), axis=0)
            sum_1 = sum_1 + jnp.sum(grad.reshape(16, 8, 128), axis=0)
        ng1[0, pl.ds(j, 1), :] = fold(sum_w)
        ng1[0, pl.ds(16 + j, 1), :] = fold(sum_1)
        bsend[0, j] = ngx[j, 8:16, :]
        bsend[1, j] = filt[j, 0:8, :]
        bsend[2, j] = ngx[j, pl.ds(idx[LIVE], 8), :]
        bsend[3, j] = filt[j, pl.ds(idx[LIVE + 2], 8), :]

    loop(CHUNKS, slopes)

    copy_ng1 = over_fsdp(ng1, S_NG1)
    copy_ng2 = over_dp(ng2, S_NG2)
    begin(copy_ng1, N_FSDP)
    halo_copies = [
        remote(bsend.at[0], brecv.at[0], S_BHALO, lead // N_FSDP, lead % N_FSDP),
        remote(bsend.at[1], brecv.at[1], S_BHALO + 1, lead // N_FSDP, lead % N_FSDP),
        remote(bsend.at[2], brecv.at[2], S_BHALO + 2, follow // N_FSDP, follow % N_FSDP),
        remote(bsend.at[3], brecv.at[3], S_BHALO + 3, follow // N_FSDP, follow % N_FSDP),
    ]
    for copy in halo_copies:
        copy.start()

    def pass_on(a, h, n):
        def add(i):
            b, m = i // 4, i % 4
            value = gp[a, 2 * h + b, m].astype(F32) + rd[n, b, m].astype(F32)
            gp[a, 2 * h + b, m] = value.astype(BF16)

        loop(8, add)

    across_up.wait_recv()
    pass_on(up, 0, 0)
    added_up.start()
    across_down.wait_recv()
    pass_on(down, 1, 1)
    added_down.start()

    arrive(copy_ng1, N_FSDP)
    ng2[0] = ordered(ng1, N_FSDP, f, (32, 128))
    begin(copy_ng2, N_DP)
    products(y)

    arrive(copy_ng2, N_DP)
    ng_total = ordered(ng2, N_DP, dp, (32, 128))
    stat[32:64, :] = ng_total
    for j in range(CHUNKS):
        ngrad[0:1, 128 * j : 128 * j + 128] = ng_total[j : j + 1]
        ngrad[1:2, 128 * j : 128 * j + 128] = ng_total[16 + j : 17 + j]
    for copy in halo_copies:
        copy.wait_recv()

    def back(j):
        taps = kern[:, lanes(j)]
        scale = gain[pl.ds(j, 1), :] * stat[pl.ds(16 + j, 1), :]
        mean_w = stat[pl.ds(32 + j, 1), :] / TOTAL
        mean_1 = stat[pl.ds(48 + j, 1), :] / TOTAL

        def center(grad, whitened):
            return scale * (grad - mean_1 - whitened * mean_w)

        for q in range(4):
            base = 128 * q
            ngx[j, 8 + base : 136 + base, :] = center(
                ngx[j, 8 + base : 136 + base, :], filt[j, base : base + 128, :]
            )
        ngx[j, 520:528, :] = jnp.zeros((8, 128), F32)
        place(
            ngx, j, center(brecv[2, j], brecv[3, j]), center(brecv[0, j], brecv[1, j])
        )

        def part(i, sums):
            base = i * 32
            accum = jnp.zeros((32, 128), F32)
            here = ext[j, pl.ds(pl.multiple_of(base + 8, 8), 32), :]
            new = []
            for tap in range(TAPS):
                window = ngx[j, pl.ds(base + 12 - tap, 32), :]
                window = window * msk[8 - tap, rows(base, 32), :]
                accum = accum + window * taps[tap : tap + 1]
                new.append(sums[tap] + jnp.sum((window * here).reshape(4, 8, 128), axis=0))
            fr[pl.ds(i * 2, 2), :, lanes(j)] = accum.astype(BF16).reshape(2, 16, 128)
            return tuple(new)

        sums = lax.fori_loop(
            0, 16, part, tuple(jnp.zeros((8, 128), F32) for _ in range(TAPS))
        )
        kg[j, 8:16, :] = jnp.zeros((8, 128), F32)
        for tap in range(TAPS):
            kg[j, tap : tap + 1, :] = fold(sums[tap])

    halo_prev.wait_send()
    loop(8, back)

    for copy in (plain_up, plain_down, added_up, added_down):
        copy.wait_recv()

    def add_first(b):
        for n in range(4):
            value = gp[y, b, n].astype(F32)
            for k in range(2):
                value = value + r1[k, b, n].astype(F32)
            s1[b, n] = value.astype(BF16)

    loop(4, add_first)
    for k in (1, 2, 3):
        copy_r2(k).start()

    loop(CHUNKS, back, 8)
    store_igrad = pltpu.make_async_copy(fr, igrad, lsem.at[0])
    store_igrad.start()

    def copy_k1(k):
        peer = (dp + k) % N_DP
        return remote(kg.at[peer], kg1.at[k], S_K1 + k, peer, f)

    begin(copy_k1, N_DP)
    kg1[0] = kg[dp]

    arrive(copy_k1, N_DP)
    kg2[0] = ordered(kg1, N_DP, dp, (16, 128))
    copy_k2 = over_fsdp(kg2, S_K2)
    begin(copy_k2, N_FSDP)

    loop(N_DP, lambda k: act_copy(k).wait_recv(), 1)

    def pick(r):
        cot[r] = ar[idx[PICK + r]]

    loop(12, pick)

    def project(n):
        columns = pl.ds(pl.multiple_of(n * 256, 256), 256)
        value = jnp.dot(cot[...].reshape(ROWS, D), pan[:, columns], preferred_element_type=F32)
        mst[:, columns] = value.astype(BF16)

    loop(4, project)

    for k in (1, 2, 3):
        copy_r2(k).wait_recv()

    def add_second(n):
        value = s1[x, n].astype(F32)
        for k in range(3):
            value = value + r2[k, n].astype(F32)
        s2[n] = value

    loop(4, add_second)
    for k in (1, 2, 3):
        copy_r3(k).start()

    arrive(copy_k2, N_FSDP)
    kg3[dp] = ordered(kg2, N_FSDP, f, (16, 128))

    def copy_k3(k):
        return remote(kg3.at[dp], kg3.at[dp], S_K3 + k, (dp + k) % N_DP, f)

    begin(copy_k3, N_DP)

    loop(8, project, 4)
    store_mapped = pltpu.make_async_copy(mst, mapped, lsem.at[1])
    store_mapped.start()

    for k in (1, 2, 3):
        copy_r3(k).wait_recv()
    value = s2[z]
    for k in range(3):
        value = value + r3[k]
    place_of = x * 2 + zh
    pgb[c, place_of] = value.astype(BF16)

    def copy_gather(k):
        to = (place_of + k) % 8
        mine = pgb.at[c, place_of]
        return remote(mine, mine, S_GAT + k, to * 2 + c, f)

    begin(copy_gather, 8)
    arrive(copy_gather, 8)
    copy_gpair = remote(pgb.at[c], pgb.at[c], S_GPAIR, partner, f)
    copy_gpair.start()

    arrive(copy_k3, N_DP)
    for j in range(CHUNKS):
        kgrad[:, 128 * j : 128 * j + 128] = kg3[j, 0:TAPS, :]

    copy_gpair.wait_recv()
    store_pgrad = pltpu.make_async_copy(pgb, pgrad, lsem.at[2])
    store_pgrad.start()

    halo_next.wait_send()
    for copy in own_copies + fwd_copies + far_copies + pair_copies + halo_copies:
        copy.wait_send()
    copy_cp.wait_send()
    copy_at.wait_send()
    for copy in (across_up, across_down, plain_up, plain_down, added_up, added_down):
        copy.wait_send()
    copy_gpair.wait_send()
    for k in (1, 2, 3):
        copy_r2(k).wait_send()
        copy_r3(k).wait_send()
    for copy in (copy_st2, act_copy, copy_ng2, copy_k1, copy_k3):
        loop(N_DP, lambda k, copy=copy: copy(k).wait_send(), 1)
    for copy in (copy_st1, copy_ng1, copy_k2, copy_gather):
        loop(N_FSDP, lambda k, copy=copy: copy(k).wait_send(), 1)
    store_igrad.wait()
    store_mapped.wait()
    store_pgrad.wait()


def finish(
    mapped, igrad, pieces, kgrad, ngrad, o_mapped, o_igrad, o_pgrad, o_kgrad, o_ngrad,
    v_mapped, v_igrad, v_pieces, v_pgrad, sems,
):
    loads = [
        pltpu.make_async_copy(source, target, sems.at[n])
        for n, (source, target) in enumerate(
            [(pieces, v_pieces), (igrad, v_igrad), (mapped, v_mapped)]
        )
    ]
    for copy in loads:
        copy.start()
    o_kgrad[...] = kgrad[...]
    o_ngrad[...] = ngrad[...]
    loads[0].wait()
    stores = []
    for part in range(2):
        for u in range(8):
            v_pgrad[128 * part : 128 * part + 128, 256 * u : 256 * u + 256] = v_pieces[
                part, u
            ].astype(F32)
        half = pl.ds(128 * part, 128)
        stores.append(
            pltpu.make_async_copy(v_pgrad.at[half], o_pgrad.at[half], sems.at[3 + part])
        )
        stores[-1].start()
    loads[1].wait()
    stores.append(pltpu.make_async_copy(v_igrad, o_igrad, sems.at[5]))
    stores[-1].start()
    loads[2].wait()
    stores.append(pltpu.make_async_copy(v_mapped, o_mapped, sems.at[6]))
    stores[-1].start()
    for copy in stores:
        copy.wait()


def shards(frames, bounds, destinations, kernel, norm_gain, norm_shift, panel, cotangent):
    hbm = pl.BlockSpec(memory_space=pl.ANY)
    vmem = pl.BlockSpec(memory_space=pltpu.VMEM)
    smem = pl.BlockSpec(memory_space=pltpu.SMEM)
    shape = jax.ShapeDtypeStruct
    idx, flags = pl.pallas_call(
        routing,
        out_shape=(shape((96,), jnp.int32), shape((40, 128), F32)),
        in_specs=[smem],
        out_specs=(smem, vmem),
    )(destinations)
    mapped, input_grad, *rest = pl.pallas_call(
        fused,
        out_shape=(
            shape((ROWS, D), BF16),
            shape((32, 16, D), BF16),
            shape((2, 8, 128, 256), BF16),
            shape((TAPS, D), F32),
            shape((2, D), F32),
        ),
        in_specs=[pl.BlockSpec(memory_space=pltpu.SMEM), vmem, vmem, hbm, hbm, hbm, vmem, vmem, vmem],
        out_specs=(hbm, hbm, hbm, vmem, vmem),
        scratch_shapes=[
            pltpu.VMEM((32, 16, D), BF16),
            pltpu.VMEM((12, BLOCK, D), BF16),
            pltpu.VMEM((16, BLOCK, D), BF16),
            pltpu.VMEM((16, BLOCK, D), BF16),
            pltpu.VMEM((SLOTS, D), BF16),
            pltpu.VMEM((SLOTS, D), BF16),
            pltpu.VMEM((CHUNKS, 528, 128), F32),
            pltpu.VMEM((CHUNKS, 512, 128), F32),
            pltpu.VMEM((CHUNKS, 528, 128), F32),
            pltpu.VMEM((TAPS, 512, 128), F32),
            pltpu.VMEM((D, D), BF16),
            pltpu.VMEM((16, BLOCK, D), BF16),
            pltpu.VMEM((16, BLOCK, D), BF16),
            pltpu.VMEM((2, 1024, 512), BF16),
            pltpu.VMEM((1024, 512), BF16),
            pltpu.VMEM((4, 4, 4, 128, 256), BF16),
            pltpu.VMEM((2, 4, 4, 128, 256), BF16),
            pltpu.VMEM((2, 2, 4, 128, 256), BF16),
            pltpu.VMEM((4, 4, 128, 256), BF16),
            pltpu.VMEM((3, 4, 128, 256), BF16),
            pltpu.VMEM((4, 128, 256), F32),
            pltpu.VMEM((3, 128, 256), F32),
            pltpu.VMEM((2, 8, 128, 256), BF16),
            pltpu.VMEM((ROWS, D), BF16),
            pltpu.VMEM((16, D), BF16),
            pltpu.VMEM((16, D), BF16),
            pltpu.VMEM((16, D), BF16),
            pltpu.VMEM((N_FSDP, 40, 128), F32),
            pltpu.VMEM((N_DP, 40, 128), F32),
            pltpu.VMEM((64, 128), F32),
            pltpu.VMEM((N_FSDP, 32, 128), F32),
            pltpu.VMEM((N_DP, 32, 128), F32),
            pltpu.VMEM((4, CHUNKS, 8, 128), F32),
            pltpu.VMEM((4, CHUNKS, 8, 128), F32),
            pltpu.VMEM((CHUNKS, 16, 128), F32),
            pltpu.VMEM((N_DP, 16, 128), F32),
            pltpu.VMEM((N_FSDP, 16, 128), F32),
            pltpu.VMEM((CHUNKS, 16, 128), F32),
            pltpu.SemaphoreType.DMA((SEMS.used,)),
            pltpu.SemaphoreType.DMA((SEMS.used,)),
            pltpu.SemaphoreType.DMA((3,)),
        ],
        compiler_params=pltpu.CompilerParams(
            collective_id=0, has_side_effects=True, vmem_limit_bytes=62 * 1024 * 1024
        ),
    )(
        idx,
        flags,
        bounds,
        frames.reshape(32, 16, D),
        cotangent.reshape(12, BLOCK, D),
        panel,
        kernel,
        norm_gain.reshape(CHUNKS, 128),
        norm_shift.reshape(CHUNKS, 128),
    )
    results = (mapped, input_grad, *rest)
    mapped, input_grad, *rest = pl.pallas_call(
        finish,
        out_shape=(
            shape((ROWS, D), BF16),
            shape((32, 16, D), BF16),
            shape((256, D), F32),
            shape((TAPS, D), F32),
            shape((2, D), F32),
        ),
        in_specs=[hbm, hbm, hbm, vmem, vmem],
        out_specs=(hbm, hbm, hbm, vmem, vmem),
        scratch_shapes=[
            pltpu.VMEM((ROWS, D), BF16),
            pltpu.VMEM((32, 16, D), BF16),
            pltpu.VMEM((2, 8, 128, 256), BF16),
            pltpu.VMEM((256, D), F32),
            pltpu.SemaphoreType.DMA((7,)),
        ],
        compiler_params=pltpu.CompilerParams(vmem_limit_bytes=60 * 1024 * 1024),
    )(*results)
    return (mapped, input_grad.reshape(SLOTS, D), *rest)


def solution(mesh):
    placed = (
        P(("dp", "fsdp"), None),
        P(None, ("dp", "fsdp")),
        P(None, "fsdp", None),
        P(),
        P(),
        P(),
        P("fsdp", None),
        P(("dp", "fsdp"), None),
    )
    return jax.shard_map(
        shards,
        mesh=mesh,
        in_specs=placed,
        out_specs=(P(("dp", "fsdp"), None), P(("dp", "fsdp"), None), P("fsdp", None), P(), P()),
        check_vma=False,
    )
```

```python
import jax
import jax.numpy as jnp
from jax import lax
from jax.experimental import pallas as pl
from jax.experimental.pallas import tpu as pltpu
from jax.sharding import PartitionSpec as P

MESH = pl.DeviceIdType.MESH
F32 = jnp.float32
BF16 = jnp.bfloat16
EPSILON = 1e-05

D = 2048
TAPS = 9
BLOCK = 32
SLOTS = 512
ROWS = 384
N_DP = 16
N_FSDP = 8
CHUNKS = D // 128
TOTAL = float(ROWS * N_DP * N_FSDP)

RANK, DEST, SEND, PICK, LIVE = 0, 16, 32, 48, 60


def peer_at(dp, slot):
    return (
        ((dp // 4 + slot // 4) % 4) * 4
        + ((dp // 2 + slot // 2) % 2) * 2
        + (dp + slot) % 2
    )


def slot_of(dp, source):
    return (
        ((dp // 4 - source // 4 + 4) % 4) * 4
        + ((dp // 2 + source // 2) % 2) * 2
        + (dp + source) % 2
    )


def routing(dest, idx, flags):
    dp = lax.axis_index("dp")
    mine = [dest[dp, 0, b] for b in range(16)]
    blocks = jnp.int32(0)
    for b in range(16):
        live = (mine[b] >= 0).astype(jnp.int32)
        blocks = blocks + live
        idx[DEST + b] = live * slot_of(dp, jnp.maximum(mine[b], 0))
        flags[b : b + 1, :] = jnp.full((1, 128), live.astype(F32), F32)

    def sends(k, carry):
        peer = peer_at(dp, k)
        block = jnp.int32(0)
        for b in range(16):
            block = jnp.where(mine[b] == peer, b, block)
        idx[SEND + k] = block
        return carry

    lax.fori_loop(0, N_DP, sends, 0)

    def ranks(source, count):
        arrives = jnp.int32(0)
        for b in range(16):
            arrives = jnp.where(dest[source, 0, b] == dp, 1, arrives)
        idx[64 + source] = jnp.minimum(count, 11)
        idx[80 + source] = jnp.where(arrives == 1, count, -1)
        return count + arrives

    lax.fori_loop(0, N_DP, ranks, jnp.int32(0))

    def by_slot(k, carry):
        idx[RANK + k] = idx[64 + peer_at(dp, k)]
        return carry

    lax.fori_loop(0, N_DP, by_slot, 0)

    def picks(wanted, carry):
        slot = jnp.int32(0)
        for source in range(N_DP):
            slot = jnp.where(idx[80 + source] == wanted, slot_of(dp, source), slot)
        idx[PICK + wanted] = slot
        return carry

    lax.fori_loop(0, 12, picks, 0)
    for b in range(16):
        last = (blocks == b + 1).astype(F32)
        flags[16 + b : 17 + b, :] = jnp.full((1, 128), last, F32)
    flags[32:40, :] = jnp.full((8, 128), (blocks * BLOCK).astype(F32), F32)
    idx[LIVE] = BLOCK * blocks
    idx[LIVE + 1] = 2 * blocks - 1
    idx[LIVE + 2] = BLOCK * blocks - 8


class Sems:
    def __init__(self):
        self.used = 0

    def take(self, count):
        at = self.used
        self.used += count
        return at


SEMS = Sems()
S_HALO = SEMS.take(2)
S_OWN = SEMS.take(3)
S_FWD = SEMS.take(2)
S_FAR = SEMS.take(4)
S_PAIR = SEMS.take(7)
S_COT = SEMS.take(16)
S_ST1 = SEMS.take(8)
S_ST2 = SEMS.take(16)
S_ACT = SEMS.take(16)
S_AT = SEMS.take(1)
S_CP = SEMS.take(1)
S_NG1 = SEMS.take(8)
S_NG2 = SEMS.take(16)
S_BHALO = SEMS.take(4)
S_R1 = SEMS.take(6)
S_R2 = SEMS.take(4)
S_R3 = SEMS.take(4)
S_GAT = SEMS.take(8)
S_GPAIR = SEMS.take(1)
S_K1 = SEMS.take(16)
S_K2 = SEMS.take(8)
S_K3 = SEMS.take(16)


def fused(
    idx,
    flags,
    bounds,
    frames,
    cotangent,
    panel,
    kern,
    gain,
    shift,
    mapped,
    igrad,
    pgrad,
    kgrad,
    ngrad,
    fr,
    cot,
    cs,
    cr,
    cp,
    cpp,
    ext,
    filt,
    ngx,
    msk,
    pan,
    act,
    ar,
    at,
    atp,
    gp,
    r1,
    rd,
    s1,
    r2,
    s2,
    r3,
    pgb,
    mst,
    htrail,
    hprev,
    hnext,
    st1,
    st2,
    stat,
    ng1,
    ng2,
    bsend,
    brecv,
    kg,
    kg1,
    kg2,
    kg3,
    ssem,
    rsem,
    lsem,
):
    dp = lax.axis_index("dp")
    f = lax.axis_index("fsdp")
    c = dp % 2
    zh = (dp // 2) % 2
    x = dp // 4
    y = f // 2
    zl = f % 2
    z = zh * 2 + zl
    partner = dp + 1 - 2 * c
    me = dp * N_FSDP + f
    follow = (me + 1) % (N_DP * N_FSDP)
    lead = (me + N_DP * N_FSDP - 1) % (N_DP * N_FSDP)

    def remote(src, dst, sem, to_dp, to_f):
        return pltpu.make_async_remote_copy(
            src_ref=src,
            dst_ref=dst,
            send_sem=ssem.at[sem],
            recv_sem=rsem.at[sem],
            device_id=(to_dp, to_f),
            device_id_type=MESH,
        )

    def loop(count, body, start=0):
        def step(k, carry):
            body(k)
            return carry

        lax.fori_loop(start, count, step, 0)

    def lanes(j):
        return pl.ds(pl.multiple_of(j * 128, 128), 128)

    def rows(at_row, count):
        return pl.ds(pl.multiple_of(at_row, count), count)

    load_frames = pltpu.make_async_copy(frames, fr, lsem.at[0])
    load_cot = pltpu.make_async_copy(cotangent, cot, lsem.at[1])
    load_panel = pltpu.make_async_copy(panel, pan.at[rows(f * 256, 256)], lsem.at[2])
    load_frames.start()
    load_panel.start()
    load_cot.start()

    barrier = pltpu.get_barrier_semaphore()

    def greet(to_dp, to_f):
        pl.semaphore_signal(barrier, inc=1, device_id=(to_dp, to_f), device_id_type=MESH)

    loop(N_DP, lambda k: greet((dp + k) % N_DP, f), 1)
    loop(N_FSDP, lambda k: greet(dp, (f + k) % N_FSDP), 1)
    greet(follow // N_FSDP, follow % N_FSDP)
    greet(lead // N_FSDP, lead % N_FSDP)
    greet(x * 4 + (1 - zh) * 2 + c, y * 2 + 1 - zl)

    for q in range(4):
        part = slice(128 * q, 128 * q + 128)
        before = jnp.broadcast_to(bounds[0:1, part].astype(F32), (128, 128)).T
        after = jnp.broadcast_to(bounds[1:2, part].astype(F32), (128, 128)).T
        for tap in range(TAPS):
            o = tap - 4
            keep = (before >= float(max(-o, 0))) & (after >= float(max(o, 0)))
            msk[tap, part, :] = jnp.where(keep, 1.0, 0.0)

    def unit(f_of):
        return pan.at[pl.ds(pl.multiple_of(f_of * 256 + c * 128, 128), 128)]

    def half_unit(f_of, h):
        return pan.at[pl.ds(pl.multiple_of(f_of * 256 + c * 128 + h * 64, 64), 64)]

    def shard_at(dy, dz):
        return ((y + dy) % 4) * 2 + (zl + dz) % 2

    f_z, f_up, f_down = shard_at(0, 1), shard_at(1, 0), shard_at(3, 0)
    f_upz, f_downz = shard_at(1, 1), shard_at(3, 1)
    f_far, f_farz = shard_at(2, 0), shard_at(2, 1)

    def send_unit(f_of, sem, to_f):
        return remote(unit(f_of), unit(f_of), sem, dp, to_f)

    def send_half(f_of, h, sem, to_f):
        return remote(half_unit(f_of, h), half_unit(f_of, h), sem, dp, to_f)

    def to_partner(f_of, n):
        return remote(unit(f_of), unit(f_of), S_PAIR + n, partner, f)

    own_copies = [
        send_unit(f, S_OWN, f_z),
        send_unit(f, S_OWN + 1, f_up),
        send_unit(f, S_OWN + 2, f_down),
    ]
    fwd_copies = [send_unit(f_z, S_FWD, f_up), send_unit(f_z, S_FWD + 1, f_down)]
    far_copies = [
        send_half(f_down, 0, S_FAR, f_up),
        send_half(f_up, 1, S_FAR + 1, f_down),
        send_half(f_downz, 0, S_FAR + 2, f_up),
        send_half(f_upz, 1, S_FAR + 3, f_down),
    ]
    pair_copies = [
        to_partner(g, n)
        for n, g in enumerate([f_z, f_down, f_up, f_downz, f_upz, f_far, f_farz])
    ]

    load_frames.wait()
    htrail[...] = fr[idx[LIVE + 1]]

    def widen(j):
        for q in range(4):
            part = fr[8 * q : 8 * q + 8, :, lanes(j)].reshape(128, 128)
            ext[j, 8 + 128 * q : 136 + 128 * q, :] = part.astype(F32)
        ext[j, 0:8, :] = jnp.zeros((8, 128), F32)
        ext[j, 520:528, :] = jnp.zeros((8, 128), F32)

    loop(CHUNKS, widen)

    def conv_at(j, base, count, taps):
        accum = jnp.zeros((count, 128), F32)
        for tap in range(TAPS):
            window = ext[j, pl.ds(base + 4 + tap, count), :] * taps[tap : tap + 1]
            accum = accum + msk[tap, pl.ds(base, count), :] * window
        filt[j, pl.ds(base, count), :] = accum

    def conv(j):
        taps = kern[:, lanes(j)]
        loop(8, lambda i: conv_at(j, pl.multiple_of(i * 64, 64), 64, taps))


    load_cot.wait()
    load_panel.wait()
    pl.semaphore_wait(barrier, 25)

    halo_next = remote(htrail, hprev, S_HALO, follow // N_FSDP, follow % N_FSDP)
    halo_prev = remote(fr.at[0], hnext, S_HALO + 1, lead // N_FSDP, lead % N_FSDP)
    halo_next.start()
    halo_prev.start()
    for copy in own_copies:
        copy.start()

    def same_z(m):
        return (m // 2) * 4 + m % 2

    def other_z(m):
        return (m // 2) * 4 + m % 2 + 2

    def cot_copy(k):
        return remote(cs.at[k], cr.at[k], S_COT + k, peer_at(dp, k), f)

    def send_cot(k):
        cs[k] = cot[idx[RANK + k]]
        cot_copy(k).start()

    cr[0] = cot[idx[RANK]]
    loop(8, lambda m: send_cot(same_z(m)), 1)

    loop(8, lambda m: send_cot(other_z(m)))

    loop(CHUNKS, conv)

    halo_next.wait_recv()
    halo_prev.wait_recv()

    def place(ref, j, previous, following):
        ref[j, 0:8, :] = previous
        for b in range(8, 17):
            at_row = 8 + BLOCK * b
            here = ref[j, at_row : at_row + 8, :]
            last = flags[15 + b : 16 + b, :]
            ref[j, at_row : at_row + 8, :] = here * (1.0 - last) + following * last

    def fold(value):
        return jnp.sum(value, axis=0, keepdims=True)

    def edges(j):
        place(
            ext,
            j,
            hprev[:, lanes(j)].astype(F32)[8:16],
            hnext[:, lanes(j)].astype(F32)[0:8],
        )
        taps = kern[:, lanes(j)]
        conv_at(j, 0, 8, taps)
        for b in range(8, 17):
            conv_at(j, BLOCK * b - 8, 8, taps)

        total = jnp.zeros((8, 128), F32)
        for q in range(8):
            part = filt[j, 64 * q : 64 * q + 64, :]
            total = total + jnp.sum(part.reshape(8, 8, 128), axis=0)
        total = fold(total)
        mean = total / flags[32:33, :]
        squares = jnp.zeros((8, 128), F32)
        for q in range(8):
            off = (filt[j, 64 * q : 64 * q + 64, :] - mean) * msk[4, 64 * q : 64 * q + 64, :]
            squares = squares + jnp.sum((off * off).reshape(8, 8, 128), axis=0)
        st1[0, pl.ds(j, 1), :] = total
        st1[0, pl.ds(16 + j, 1), :] = fold(squares)

    loop(CHUNKS, edges)
    st1[0, 32:40, :] = flags[32:40, :]

    def over_fsdp(buf, sem):
        def copy(k):
            return remote(buf.at[0], buf.at[k], sem + k, dp, (f + k) % N_FSDP)

        return copy

    def over_dp(buf, sem):
        def copy(k):
            return remote(buf.at[0], buf.at[k], sem + k, (dp + k) % N_DP, f)

        return copy

    def begin(copy, count):
        loop(count, lambda k: copy(k).start(), 1)

    def arrive(copy, count):
        loop(count, lambda k: copy(k).wait_recv(), 1)

    def merge(buf, count, mine):
        def slot(p):
            return (mine - p + count) % count

        def add(p, carry):
            sums, number = carry
            return sums + buf[slot(p), 0:16, :], number + buf[slot(p), 32:40, :]

        sums, number = lax.fori_loop(
            0, count, add, (jnp.zeros((16, 128), F32), jnp.zeros((8, 128), F32))
        )
        mean = sums / jnp.concatenate([number, number], axis=0)

        def spread(p, squares):
            n_p = buf[slot(p), 32:40, :]
            n_p = jnp.concatenate([n_p, n_p], axis=0)
            off = buf[slot(p), 0:16, :] / n_p - mean
            return squares + (buf[slot(p), 16:32, :] + n_p * off * off)

        squares = lax.fori_loop(0, count, spread, jnp.zeros((16, 128), F32))
        return sums, squares, number

    def ordered(buf, count, mine, shape):
        def add(p, total):
            return total + buf[(mine - p + count) % count]

        return lax.fori_loop(0, count, add, jnp.zeros(shape, F32))

    copy_st1 = over_fsdp(st1, S_ST1)
    copy_st2 = over_dp(st2, S_ST2)
    begin(copy_st1, N_FSDP)

    own_copies[0].wait_recv()
    fwd_copies[0].start()
    fwd_copies[1].start()
    pair_copies[0].start()
    own_copies[1].wait_recv()
    far_copies[0].start()
    pair_copies[1].start()
    own_copies[2].wait_recv()
    far_copies[1].start()
    pair_copies[2].start()

    arrive(copy_st1, N_FSDP)
    sums, squares, number = merge(st1, N_FSDP, f)
    st2[0, 0:16, :] = sums
    st2[0, 16:32, :] = squares
    st2[0, 32:40, :] = number
    begin(copy_st2, N_DP)

    arrive(copy_st2, N_DP)
    sums, squares, number = merge(st2, N_DP, dp)
    stat[0:16, :] = sums / TOTAL
    stat[16:32, :] = lax.rsqrt(squares / TOTAL + EPSILON)

    def activate(j):
        average = stat[pl.ds(j, 1), :]
        inverse = stat[pl.ds(16 + j, 1), :]
        g = gain[pl.ds(j, 1), :]
        b = shift[pl.ds(j, 1), :]
        for q in range(4):
            base = 128 * q
            keep = msk[4, base : base + 128, :]
            whitened = (filt[j, base : base + 128, :] - average) * inverse
            normed = whitened * g + b
            logistic = 1.0 / (1.0 + jnp.exp(-normed))
            value = normed * logistic * keep
            filt[j, base : base + 128, :] = whitened
            act[4 * q : 4 * q + 4, :, lanes(j)] = value.astype(BF16).reshape(4, BLOCK, 128)
            at[j % 2, rows((j // 2) * 128, 128), base : base + 128] = value.T.astype(BF16)

    loop(CHUNKS, activate)
    copy_at = remote(at.at[1 - c], atp, S_AT, partner, f)
    copy_at.start()

    fwd_copies[0].wait_recv()
    far_copies[2].start()
    pair_copies[3].start()
    fwd_copies[1].wait_recv()
    far_copies[3].start()
    pair_copies[4].start()

    loop(N_DP, lambda k: cot_copy(k).wait_recv(), 1)

    def back_block(b):
        block = cr[idx[DEST + b]]
        kept = jnp.broadcast_to(flags[pl.ds(b, 1), 0:1].astype(BF16), (BLOCK, D))
        cp[rows(b * BLOCK, BLOCK), :] = block * kept

    loop(16, back_block)
    copy_cp = remote(cp, cpp, S_CP, partner, f)
    copy_cp.start()

    ar[0] = act[idx[SEND]]

    def act_copy(k):
        return remote(cs.at[k], ar.at[k], S_ACT + k, peer_at(dp, k), f)

    def send_act(k):
        cot_copy(k).wait_send()
        cs[k] = act[idx[SEND + k]]
        act_copy(k).start()

    loop(N_DP, send_act, 1)

    far_copies[0].wait_recv()
    far_copies[1].wait_recv()
    pair_copies[5].start()

    up, down, across = (y + 1) % 4, (y + 3) % 4, (y + 2) % 4
    f_above, f_below = up * 2 + zl, down * 2 + zl

    def half(ref, h):
        return ref.at[pl.ds(2 * h, 2)]

    across_up = remote(half(gp.at[across], 0), rd.at[0], S_R1, dp, f_above)
    across_down = remote(half(gp.at[across], 1), rd.at[1], S_R1 + 1, dp, f_below)
    plain_up = remote(half(gp.at[up], 1), half(r1.at[0], 1), S_R1 + 2, dp, f_above)
    plain_down = remote(half(gp.at[down], 0), half(r1.at[1], 0), S_R1 + 3, dp, f_below)
    added_up = remote(half(gp.at[up], 0), half(r1.at[0], 0), S_R1 + 4, dp, f_above)
    added_down = remote(half(gp.at[down], 1), half(r1.at[1], 1), S_R1 + 5, dp, f_below)

    def copy_r2(k):
        b = (x + k) % 4
        return remote(s1.at[b], r2.at[k - 1], S_R2 + k, b * 4 + zh * 2 + c, f)

    def copy_r3(k):
        to_z = (z + k) % 4
        return remote(
            s2.at[to_z], r3.at[k - 1], S_R3 + k, x * 4 + (to_z // 2) * 2 + c, y * 2 + to_z % 2
        )

    def products(a):
        def product(b):
            d_rows = rows(a * 256, 256)
            columns = pl.ds(pl.multiple_of(b * 512, 512), 512)
            value = jnp.dot(at[c, d_rows, :], cp[:, columns], preferred_element_type=F32)
            value = value + jnp.dot(
                atp[d_rows, :], cpp[:, columns], preferred_element_type=F32
            )
            for h in range(2):
                for low in range(2):
                    piece = value[low * 128 : low * 128 + 128, h * 256 : h * 256 + 256]
                    gp[a, b, h * 2 + low] = piece.astype(BF16)

        loop(4, product)

    copy_at.wait_recv()
    copy_cp.wait_recv()
    products(across)
    across_up.start()
    across_down.start()
    far_copies[2].wait_recv()
    far_copies[3].wait_recv()
    pair_copies[6].start()
    products(up)
    plain_up.start()
    products(down)
    plain_down.start()
    for copy in pair_copies:
        copy.wait_recv()

    def act_grad(f_of):
        value = lax.dot_general(
            cp[...],
            pan[rows(f_of * 256, 256), :],
            (((1,), (1,)), ((), ())),
            preferred_element_type=F32,
        )
        value = value.astype(BF16).astype(F32)
        ngx[f_of * 2, 8:520, :] = value[:, 0:128]
        ngx[f_of * 2 + 1, 8:520, :] = value[:, 128:256]

    loop(N_FSDP, act_grad)

    def slopes(j):
        g = gain[pl.ds(j, 1), :]
        b = shift[pl.ds(j, 1), :]
        sum_w = jnp.zeros((8, 128), F32)
        sum_1 = jnp.zeros((8, 128), F32)
        for q in range(4):
            base = 128 * q
            whitened = filt[j, base : base + 128, :]
            normed = whitened * g + b
            logistic = 1.0 / (1.0 + jnp.exp(-normed))
            slope = logistic + normed * logistic * (1.0 - logistic)
            grad = ngx[j, 8 + base : 136 + base, :] * slope
            ngx[j, 8 + base : 136 + base, :] = grad
            sum_w = sum_w + jnp.sum((grad * whitened).reshape(16, 8, 128), axis=0)
            sum_1 = sum_1 + jnp.sum(grad.reshape(16, 8, 128), axis=0)
        ng1[0, pl.ds(j, 1), :] = fold(sum_w)
        ng1[0, pl.ds(16 + j, 1), :] = fold(sum_1)
        bsend[0, j] = ngx[j, 8:16, :]
        bsend[1, j] = filt[j, 0:8, :]
        bsend[2, j] = ngx[j, pl.ds(idx[LIVE], 8), :]
        bsend[3, j] = filt[j, pl.ds(idx[LIVE + 2], 8), :]

    loop(CHUNKS, slopes)

    copy_ng1 = over_fsdp(ng1, S_NG1)
    copy_ng2 = over_dp(ng2, S_NG2)
    begin(copy_ng1, N_FSDP)
    halo_copies = [
        remote(bsend.at[0], brecv.at[0], S_BHALO, lead // N_FSDP, lead % N_FSDP),
        remote(bsend.at[1], brecv.at[1], S_BHALO + 1, lead // N_FSDP, lead % N_FSDP),
        remote(bsend.at[2], brecv.at[2], S_BHALO + 2, follow // N_FSDP, follow % N_FSDP),
        remote(bsend.at[3], brecv.at[3], S_BHALO + 3, follow // N_FSDP, follow % N_FSDP),
    ]
    for copy in halo_copies:
        copy.start()

    def pass_on(a, h, n):
        def add(i):
            b, m = i // 4, i % 4
            value = gp[a, 2 * h + b, m].astype(F32) + rd[n, b, m].astype(F32)
            gp[a, 2 * h + b, m] = value.astype(BF16)

        loop(8, add)

    across_up.wait_recv()
    pass_on(up, 0, 0)
    added_up.start()
    across_down.wait_recv()
    pass_on(down, 1, 1)
    added_down.start()

    arrive(copy_ng1, N_FSDP)
    ng2[0] = ordered(ng1, N_FSDP, f, (32, 128))
    begin(copy_ng2, N_DP)
    products(y)

    arrive(copy_ng2, N_DP)
    ng_total = ordered(ng2, N_DP, dp, (32, 128))
    stat[32:64, :] = ng_total
    for j in range(CHUNKS):
        ngrad[0:1, 128 * j : 128 * j + 128] = ng_total[j : j + 1]
        ngrad[1:2, 128 * j : 128 * j + 128] = ng_total[16 + j : 17 + j]
    for copy in halo_copies:
        copy.wait_recv()

    def back(j):
        taps = kern[:, lanes(j)]
        scale = gain[pl.ds(j, 1), :] * stat[pl.ds(16 + j, 1), :]
        mean_w = stat[pl.ds(32 + j, 1), :] / TOTAL
        mean_1 = stat[pl.ds(48 + j, 1), :] / TOTAL

        def center(grad, whitened):
            return scale * (grad - mean_1 - whitened * mean_w)

        for q in range(4):
            base = 128 * q
            ngx[j, 8 + base : 136 + base, :] = center(
                ngx[j, 8 + base : 136 + base, :], filt[j, base : base + 128, :]
            )
        ngx[j, 520:528, :] = jnp.zeros((8, 128), F32)
        place(
            ngx, j, center(brecv[2, j], brecv[3, j]), center(brecv[0, j], brecv[1, j])
        )

        def part(i, sums):
            base = i * 32
            accum = jnp.zeros((32, 128), F32)
            here = ext[j, pl.ds(pl.multiple_of(base + 8, 8), 32), :]
            new = []
            for tap in range(TAPS):
                window = ngx[j, pl.ds(base + 12 - tap, 32), :]
                window = window * msk[8 - tap, rows(base, 32), :]
                accum = accum + window * taps[tap : tap + 1]
                new.append(sums[tap] + jnp.sum((window * here).reshape(4, 8, 128), axis=0))
            fr[pl.ds(i * 2, 2), :, lanes(j)] = accum.astype(BF16).reshape(2, 16, 128)
            return tuple(new)

        sums = lax.fori_loop(
            0, 16, part, tuple(jnp.zeros((8, 128), F32) for _ in range(TAPS))
        )
        kg[j, 8:16, :] = jnp.zeros((8, 128), F32)
        for tap in range(TAPS):
            kg[j, tap : tap + 1, :] = fold(sums[tap])

    halo_prev.wait_send()
    loop(8, back)

    for copy in (plain_up, plain_down, added_up, added_down):
        copy.wait_recv()

    def add_first(b):
        for n in range(4):
            value = gp[y, b, n].astype(F32)
            for k in range(2):
                value = value + r1[k, b, n].astype(F32)
            s1[b, n] = value.astype(BF16)

    loop(4, add_first)
    for k in (1, 2, 3):
        copy_r2(k).start()

    loop(CHUNKS, back, 8)
    store_igrad = pltpu.make_async_copy(fr, igrad, lsem.at[0])
    store_igrad.start()

    def copy_k1(k):
        peer = (dp + k) % N_DP
        return remote(kg.at[peer], kg1.at[k], S_K1 + k, peer, f)

    begin(copy_k1, N_DP)
    kg1[0] = kg[dp]

    arrive(copy_k1, N_DP)
    kg2[0] = ordered(kg1, N_DP, dp, (16, 128))
    copy_k2 = over_fsdp(kg2, S_K2)
    begin(copy_k2, N_FSDP)

    loop(N_DP, lambda k: act_copy(k).wait_recv(), 1)

    def pick(r):
        cot[r] = ar[idx[PICK + r]]

    loop(12, pick)

    def project(n):
        columns = pl.ds(pl.multiple_of(n * 256, 256), 256)
        value = jnp.dot(cot[...].reshape(ROWS, D), pan[:, columns], preferred_element_type=F32)
        mst[:, columns] = value.astype(BF16)

    loop(4, project)

    for k in (1, 2, 3):
        copy_r2(k).wait_recv()

    def add_second(n):
        value = s1[x, n].astype(F32)
        for k in range(3):
            value = value + r2[k, n].astype(F32)
        s2[n] = value

    loop(4, add_second)
    for k in (1, 2, 3):
        copy_r3(k).start()

    arrive(copy_k2, N_FSDP)
    kg3[dp] = ordered(kg2, N_FSDP, f, (16, 128))

    def copy_k3(k):
        return remote(kg3.at[dp], kg3.at[dp], S_K3 + k, (dp + k) % N_DP, f)

    begin(copy_k3, N_DP)

    loop(8, project, 4)
    store_mapped = pltpu.make_async_copy(mst, mapped, lsem.at[1])
    store_mapped.start()

    for k in (1, 2, 3):
        copy_r3(k).wait_recv()
    value = s2[z]
    for k in range(3):
        value = value + r3[k]
    place_of = x * 2 + zh
    pgb[c, place_of] = value.astype(BF16)

    def copy_gather(k):
        to = (place_of + k) % 8
        mine = pgb.at[c, place_of]
        return remote(mine, mine, S_GAT + k, to * 2 + c, f)

    begin(copy_gather, 8)
    arrive(copy_gather, 8)
    copy_gpair = remote(pgb.at[c], pgb.at[c], S_GPAIR, partner, f)
    copy_gpair.start()

    arrive(copy_k3, N_DP)
    for j in range(CHUNKS):
        kgrad[:, 128 * j : 128 * j + 128] = kg3[j, 0:TAPS, :]

    copy_gpair.wait_recv()
    store_pgrad = pltpu.make_async_copy(pgb, pgrad, lsem.at[2])
    store_pgrad.start()

    halo_next.wait_send()
    for copy in own_copies + fwd_copies + far_copies + pair_copies + halo_copies:
        copy.wait_send()
    copy_cp.wait_send()
    copy_at.wait_send()
    for copy in (across_up, across_down, plain_up, plain_down, added_up, added_down):
        copy.wait_send()
    copy_gpair.wait_send()
    for k in (1, 2, 3):
        copy_r2(k).wait_send()
        copy_r3(k).wait_send()
    for copy in (copy_st2, act_copy, copy_ng2, copy_k1, copy_k3):
        loop(N_DP, lambda k, copy=copy: copy(k).wait_send(), 1)
    for copy in (copy_st1, copy_ng1, copy_k2, copy_gather):
        loop(N_FSDP, lambda k, copy=copy: copy(k).wait_send(), 1)
    store_igrad.wait()
    store_mapped.wait()
    store_pgrad.wait()


def finish(
    mapped, igrad, pieces, kgrad, ngrad, o_mapped, o_igrad, o_pgrad, o_kgrad, o_ngrad,
    v_mapped, v_igrad, v_pieces, v_pgrad, sems,
):
    loads = [
        pltpu.make_async_copy(source, target, sems.at[n])
        for n, (source, target) in enumerate(
            [(pieces, v_pieces), (igrad, v_igrad), (mapped, v_mapped)]
        )
    ]
    for copy in loads:
        copy.start()
    o_kgrad[...] = kgrad[...]
    o_ngrad[...] = ngrad[...]
    loads[0].wait()
    stores = []
    for part in range(2):
        for u in range(8):
            v_pgrad[128 * part : 128 * part + 128, 256 * u : 256 * u + 256] = v_pieces[
                part, u
            ].astype(F32)
        half = pl.ds(128 * part, 128)
        stores.append(
            pltpu.make_async_copy(v_pgrad.at[half], o_pgrad.at[half], sems.at[3 + part])
        )
        stores[-1].start()
    loads[1].wait()
    stores.append(pltpu.make_async_copy(v_igrad, o_igrad, sems.at[5]))
    stores[-1].start()
    loads[2].wait()
    stores.append(pltpu.make_async_copy(v_mapped, o_mapped, sems.at[6]))
    stores[-1].start()
    for copy in stores:
        copy.wait()


def shards(frames, bounds, destinations, kernel, norm_gain, norm_shift, panel, cotangent):
    hbm = pl.BlockSpec(memory_space=pl.ANY)
    vmem = pl.BlockSpec(memory_space=pltpu.VMEM)
    smem = pl.BlockSpec(memory_space=pltpu.SMEM)
    shape = jax.ShapeDtypeStruct
    idx, flags = pl.pallas_call(
        routing,
        out_shape=(shape((96,), jnp.int32), shape((40, 128), F32)),
        in_specs=[smem],
        out_specs=(smem, vmem),
    )(destinations)
    mapped, input_grad, *rest = pl.pallas_call(
        fused,
        out_shape=(
            shape((ROWS, D), BF16),
            shape((32, 16, D), BF16),
            shape((2, 8, 128, 256), BF16),
            shape((TAPS, D), F32),
            shape((2, D), F32),
        ),
        in_specs=[pl.BlockSpec(memory_space=pltpu.SMEM), vmem, vmem, hbm, hbm, hbm, vmem, vmem, vmem],
        out_specs=(hbm, hbm, hbm, vmem, vmem),
        scratch_shapes=[
            pltpu.VMEM((32, 16, D), BF16),
            pltpu.VMEM((12, BLOCK, D), BF16),
            pltpu.VMEM((16, BLOCK, D), BF16),
            pltpu.VMEM((16, BLOCK, D), BF16),
            pltpu.VMEM((SLOTS, D), BF16),
            pltpu.VMEM((SLOTS, D), BF16),
            pltpu.VMEM((CHUNKS, 528, 128), F32),
            pltpu.VMEM((CHUNKS, 512, 128), F32),
            pltpu.VMEM((CHUNKS, 528, 128), F32),
            pltpu.VMEM((TAPS, 512, 128), F32),
            pltpu.VMEM((D, D), BF16),
            pltpu.VMEM((16, BLOCK, D), BF16),
            pltpu.VMEM((16, BLOCK, D), BF16),
            pltpu.VMEM((2, 1024, 512), BF16),
            pltpu.VMEM((1024, 512), BF16),
            pltpu.VMEM((4, 4, 4, 128, 256), BF16),
            pltpu.VMEM((2, 4, 4, 128, 256), BF16),
            pltpu.VMEM((2, 2, 4, 128, 256), BF16),
            pltpu.VMEM((4, 4, 128, 256), BF16),
            pltpu.VMEM((3, 4, 128, 256), BF16),
            pltpu.VMEM((4, 128, 256), F32),
            pltpu.VMEM((3, 128, 256), F32),
            pltpu.VMEM((2, 8, 128, 256), BF16),
            pltpu.VMEM((ROWS, D), BF16),
            pltpu.VMEM((16, D), BF16),
            pltpu.VMEM((16, D), BF16),
            pltpu.VMEM((16, D), BF16),
            pltpu.VMEM((N_FSDP, 40, 128), F32),
            pltpu.VMEM((N_DP, 40, 128), F32),
            pltpu.VMEM((64, 128), F32),
            pltpu.VMEM((N_FSDP, 32, 128), F32),
            pltpu.VMEM((N_DP, 32, 128), F32),
            pltpu.VMEM((4, CHUNKS, 8, 128), F32),
            pltpu.VMEM((4, CHUNKS, 8, 128), F32),
            pltpu.VMEM((CHUNKS, 16, 128), F32),
            pltpu.VMEM((N_DP, 16, 128), F32),
            pltpu.VMEM((N_FSDP, 16, 128), F32),
            pltpu.VMEM((CHUNKS, 16, 128), F32),
            pltpu.SemaphoreType.DMA((SEMS.used,)),
            pltpu.SemaphoreType.DMA((SEMS.used,)),
            pltpu.SemaphoreType.DMA((3,)),
        ],
        compiler_params=pltpu.CompilerParams(
            collective_id=0, has_side_effects=True, vmem_limit_bytes=62 * 1024 * 1024
        ),
    )(
        idx,
        flags,
        bounds,
        frames.reshape(32, 16, D),
        cotangent.reshape(12, BLOCK, D),
        panel,
        kernel,
        norm_gain.reshape(CHUNKS, 128),
        norm_shift.reshape(CHUNKS, 128),
    )
    results = (mapped, input_grad, *rest)
    mapped, input_grad, *rest = pl.pallas_call(
        finish,
        out_shape=(
            shape((ROWS, D), BF16),
            shape((32, 16, D), BF16),
            shape((256, D), F32),
            shape((TAPS, D), F32),
            shape((2, D), F32),
        ),
        in_specs=[hbm, hbm, hbm, vmem, vmem],
        out_specs=(hbm, hbm, hbm, vmem, vmem),
        scratch_shapes=[
            pltpu.VMEM((ROWS, D), BF16),
            pltpu.VMEM((32, 16, D), BF16),
            pltpu.VMEM((2, 8, 128, 256), BF16),
            pltpu.VMEM((256, D), F32),
            pltpu.SemaphoreType.DMA((7,)),
        ],
        compiler_params=pltpu.CompilerParams(vmem_limit_bytes=60 * 1024 * 1024),
    )(*results)
    return (mapped, input_grad.reshape(SLOTS, D), *rest)


def solution(mesh):
    placed = (
        P(("dp", "fsdp"), None),
        P(None, ("dp", "fsdp")),
        P(None, "fsdp", None),
        P(),
        P(),
        P(),
        P("fsdp", None),
        P(("dp", "fsdp"), None),
    )
    return jax.shard_map(
        shards,
        mesh=mesh,
        in_specs=placed,
        out_specs=(P(("dp", "fsdp"), None), P(("dp", "fsdp"), None), P("fsdp", None), P(), P()),
        check_vma=False,
    )
```

```python
import jax
import jax.numpy as jnp
from jax import lax
from jax.experimental import pallas as pl
from jax.experimental.pallas import tpu as pltpu
from jax.sharding import PartitionSpec as P

MESH = pl.DeviceIdType.MESH
F32 = jnp.float32
BF16 = jnp.bfloat16
EPSILON = 1e-05

D = 2048
TAPS = 9
BLOCK = 32
SLOTS = 512
ROWS = 384
N_DP = 16
N_FSDP = 8
CHUNKS = D // 128
TOTAL = float(ROWS * N_DP * N_FSDP)

RANK, DEST, SEND, PICK, LIVE = 0, 16, 32, 48, 60


def peer_at(dp, slot):
    return (
        ((dp // 4 + slot // 4) % 4) * 4
        + ((dp // 2 + slot // 2) % 2) * 2
        + (dp + slot) % 2
    )


def slot_of(dp, source):
    return (
        ((dp // 4 - source // 4 + 4) % 4) * 4
        + ((dp // 2 + source // 2) % 2) * 2
        + (dp + source) % 2
    )


def routing(dest, idx, flags):
    dp = lax.axis_index("dp")
    mine = [dest[dp, 0, b] for b in range(16)]
    blocks = jnp.int32(0)
    for b in range(16):
        live = (mine[b] >= 0).astype(jnp.int32)
        blocks = blocks + live
        idx[DEST + b] = live * slot_of(dp, jnp.maximum(mine[b], 0))
        flags[b : b + 1, :] = jnp.full((1, 128), live.astype(F32), F32)

    def sends(k, carry):
        peer = peer_at(dp, k)
        block = jnp.int32(0)
        for b in range(16):
            block = jnp.where(mine[b] == peer, b, block)
        idx[SEND + k] = block
        return carry

    lax.fori_loop(0, N_DP, sends, 0)

    def ranks(source, count):
        arrives = jnp.int32(0)
        for b in range(16):
            arrives = jnp.where(dest[source, 0, b] == dp, 1, arrives)
        idx[64 + source] = jnp.minimum(count, 11)
        idx[80 + source] = jnp.where(arrives == 1, count, -1)
        return count + arrives

    lax.fori_loop(0, N_DP, ranks, jnp.int32(0))

    def by_slot(k, carry):
        idx[RANK + k] = idx[64 + peer_at(dp, k)]
        return carry

    lax.fori_loop(0, N_DP, by_slot, 0)

    def picks(wanted, carry):
        slot = jnp.int32(0)
        for source in range(N_DP):
            slot = jnp.where(idx[80 + source] == wanted, slot_of(dp, source), slot)
        idx[PICK + wanted] = slot
        return carry

    lax.fori_loop(0, 12, picks, 0)
    for b in range(16):
        last = (blocks == b + 1).astype(F32)
        flags[16 + b : 17 + b, :] = jnp.full((1, 128), last, F32)
    flags[32:40, :] = jnp.full((8, 128), (blocks * BLOCK).astype(F32), F32)
    idx[LIVE] = BLOCK * blocks
    idx[LIVE + 1] = 2 * blocks - 1
    idx[LIVE + 2] = BLOCK * blocks - 8


class Sems:
    def __init__(self):
        self.used = 0

    def take(self, count):
        at = self.used
        self.used += count
        return at


SEMS = Sems()
S_HALO = SEMS.take(2)
S_OWN = SEMS.take(3)
S_FWD = SEMS.take(2)
S_FAR = SEMS.take(4)
S_PAIR = SEMS.take(7)
S_COT = SEMS.take(16)
S_ST1 = SEMS.take(8)
S_ST2 = SEMS.take(16)
S_ACT = SEMS.take(16)
S_AT = SEMS.take(1)
S_CP = SEMS.take(1)
S_NG1 = SEMS.take(8)
S_NG2 = SEMS.take(16)
S_BHALO = SEMS.take(4)
S_R1 = SEMS.take(6)
S_R2 = SEMS.take(4)
S_R3 = SEMS.take(4)
S_GAT = SEMS.take(8)
S_GPAIR = SEMS.take(1)
S_K1 = SEMS.take(16)
S_K2 = SEMS.take(8)
S_K3 = SEMS.take(16)


def fused(
    idx,
    flags,
    bounds,
    frames,
    cotangent,
    panel,
    kern,
    gain,
    shift,
    mapped,
    igrad,
    pgrad,
    kgrad,
    ngrad,
    fr,
    cot,
    cs,
    cr,
    cp,
    cpp,
    ext,
    filt,
    ngx,
    msk,
    pan,
    act,
    ar,
    at,
    atp,
    gp,
    r1,
    rd,
    s1,
    r2,
    s2,
    r3,
    pgb,
    mst,
    htrail,
    hprev,
    hnext,
    st1,
    st2,
    stat,
    ng1,
    ng2,
    bsend,
    brecv,
    kg,
    kg1,
    kg2,
    kg3,
    ssem,
    rsem,
    lsem,
):
    dp = lax.axis_index("dp")
    f = lax.axis_index("fsdp")
    c = dp % 2
    zh = (dp // 2) % 2
    x = dp // 4
    y = f // 2
    zl = f % 2
    z = zh * 2 + zl
    partner = dp + 1 - 2 * c
    me = dp * N_FSDP + f
    follow = (me + 1) % (N_DP * N_FSDP)
    lead = (me + N_DP * N_FSDP - 1) % (N_DP * N_FSDP)

    def remote(src, dst, sem, to_dp, to_f):
        return pltpu.make_async_remote_copy(
            src_ref=src,
            dst_ref=dst,
            send_sem=ssem.at[sem],
            recv_sem=rsem.at[sem],
            device_id=(to_dp, to_f),
            device_id_type=MESH,
        )

    def loop(count, body, start=0):
        def step(k, carry):
            body(k)
            return carry

        lax.fori_loop(start, count, step, 0)

    def lanes(j):
        return pl.ds(pl.multiple_of(j * 128, 128), 128)

    def rows(at_row, count):
        return pl.ds(pl.multiple_of(at_row, count), count)

    load_frames = pltpu.make_async_copy(frames, fr, lsem.at[0])
    load_cot = pltpu.make_async_copy(cotangent, cot, lsem.at[1])
    load_panel = pltpu.make_async_copy(panel, pan.at[rows(f * 256, 256)], lsem.at[2])
    load_frames.start()
    load_panel.start()
    load_cot.start()

    barrier = pltpu.get_barrier_semaphore()

    def greet(to_dp, to_f):
        pl.semaphore_signal(barrier, inc=1, device_id=(to_dp, to_f), device_id_type=MESH)

    loop(N_DP, lambda k: greet((dp + k) % N_DP, f), 1)
    loop(N_FSDP, lambda k: greet(dp, (f + k) % N_FSDP), 1)
    greet(follow // N_FSDP, follow % N_FSDP)
    greet(lead // N_FSDP, lead % N_FSDP)
    greet(x * 4 + (1 - zh) * 2 + c, y * 2 + 1 - zl)

    for q in range(4):
        part = slice(128 * q, 128 * q + 128)
        before = jnp.broadcast_to(bounds[0:1, part].astype(F32), (128, 128)).T
        after = jnp.broadcast_to(bounds[1:2, part].astype(F32), (128, 128)).T
        for tap in range(TAPS):
            o = tap - 4
            keep = (before >= float(max(-o, 0))) & (after >= float(max(o, 0)))
            msk[tap, part, :] = jnp.where(keep, 1.0, 0.0)

    def unit(f_of):
        return pan.at[pl.ds(pl.multiple_of(f_of * 256 + c * 128, 128), 128)]

    def half_unit(f_of, h):
        return pan.at[pl.ds(pl.multiple_of(f_of * 256 + c * 128 + h * 64, 64), 64)]

    def shard_at(dy, dz):
        return ((y + dy) % 4) * 2 + (zl + dz) % 2

    f_z, f_up, f_down = shard_at(0, 1), shard_at(1, 0), shard_at(3, 0)
    f_upz, f_downz = shard_at(1, 1), shard_at(3, 1)
    f_far, f_farz = shard_at(2, 0), shard_at(2, 1)

    def send_unit(f_of, sem, to_f):
        return remote(unit(f_of), unit(f_of), sem, dp, to_f)

    def send_half(f_of, h, sem, to_f):
        return remote(half_unit(f_of, h), half_unit(f_of, h), sem, dp, to_f)

    def to_partner(f_of, n):
        return remote(unit(f_of), unit(f_of), S_PAIR + n, partner, f)

    own_copies = [
        send_unit(f, S_OWN, f_z),
        send_unit(f, S_OWN + 1, f_up),
        send_unit(f, S_OWN + 2, f_down),
    ]
    fwd_copies = [send_unit(f_z, S_FWD, f_up), send_unit(f_z, S_FWD + 1, f_down)]
    far_copies = [
        send_half(f_down, 0, S_FAR, f_up),
        send_half(f_up, 1, S_FAR + 1, f_down),
        send_half(f_downz, 0, S_FAR + 2, f_up),
        send_half(f_upz, 1, S_FAR + 3, f_down),
    ]
    pair_copies = [
        to_partner(g, n)
        for n, g in enumerate([f_z, f_down, f_up, f_downz, f_upz, f_far, f_farz])
    ]

    load_frames.wait()
    htrail[...] = fr[idx[LIVE + 1]]

    def widen(j):
        for q in range(4):
            part = fr[8 * q : 8 * q + 8, :, lanes(j)].reshape(128, 128)
            ext[j, 8 + 128 * q : 136 + 128 * q, :] = part.astype(F32)
        ext[j, 0:8, :] = jnp.zeros((8, 128), F32)
        ext[j, 520:528, :] = jnp.zeros((8, 128), F32)

    loop(CHUNKS, widen)

    def conv_at(j, base, count, taps):
        accum = jnp.zeros((count, 128), F32)
        for tap in range(TAPS):
            window = ext[j, pl.ds(base + 4 + tap, count), :] * taps[tap : tap + 1]
            accum = accum + msk[tap, pl.ds(base, count), :] * window
        filt[j, pl.ds(base, count), :] = accum

    def conv(j):
        taps = kern[:, lanes(j)]
        loop(8, lambda i: conv_at(j, pl.multiple_of(i * 64, 64), 64, taps))


    load_cot.wait()
    load_panel.wait()
    pl.semaphore_wait(barrier, 25)

    halo_next = remote(htrail, hprev, S_HALO, follow // N_FSDP, follow % N_FSDP)
    halo_prev = remote(fr.at[0], hnext, S_HALO + 1, lead // N_FSDP, lead % N_FSDP)
    halo_next.start()
    halo_prev.start()
    for copy in own_copies:
        copy.start()

    def same_z(m):
        return (m // 2) * 4 + m % 2

    def other_z(m):
        return (m // 2) * 4 + m % 2 + 2

    def cot_copy(k):
        return remote(cs.at[k], cr.at[k], S_COT + k, peer_at(dp, k), f)

    def send_cot(k):
        cs[k] = cot[idx[RANK + k]]
        cot_copy(k).start()

    cr[0] = cot[idx[RANK]]
    loop(8, lambda m: send_cot(same_z(m)), 1)


    loop(CHUNKS, conv)

    own_copies[0].wait_recv()
    fwd_copies[0].start()
    fwd_copies[1].start()
    pair_copies[0].start()
    loop(8, lambda m: send_cot(other_z(m)))

    halo_next.wait_recv()
    halo_prev.wait_recv()

    def place(ref, j, previous, following):
        ref[j, 0:8, :] = previous
        for b in range(8, 17):
            at_row = 8 + BLOCK * b
            here = ref[j, at_row : at_row + 8, :]
            last = flags[15 + b : 16 + b, :]
            ref[j, at_row : at_row + 8, :] = here * (1.0 - last) + following * last

    def fold(value):
        return jnp.sum(value, axis=0, keepdims=True)

    def edges(j):
        place(
            ext,
            j,
            hprev[:, lanes(j)].astype(F32)[8:16],
            hnext[:, lanes(j)].astype(F32)[0:8],
        )
        taps = kern[:, lanes(j)]
        conv_at(j, 0, 8, taps)
        for b in range(8, 17):
            conv_at(j, BLOCK * b - 8, 8, taps)

        total = jnp.zeros((8, 128), F32)
        for q in range(8):
            part = filt[j, 64 * q : 64 * q + 64, :]
            total = total + jnp.sum(part.reshape(8, 8, 128), axis=0)
        total = fold(total)
        mean = total / flags[32:33, :]
        squares = jnp.zeros((8, 128), F32)
        for q in range(8):
            off = (filt[j, 64 * q : 64 * q + 64, :] - mean) * msk[4, 64 * q : 64 * q + 64, :]
            squares = squares + jnp.sum((off * off).reshape(8, 8, 128), axis=0)
        st1[0, pl.ds(j, 1), :] = total
        st1[0, pl.ds(16 + j, 1), :] = fold(squares)

    loop(CHUNKS, edges)
    st1[0, 32:40, :] = flags[32:40, :]

    def over_fsdp(buf, sem):
        def copy(k):
            return remote(buf.at[0], buf.at[k], sem + k, dp, (f + k) % N_FSDP)

        return copy

    def over_dp(buf, sem):
        def copy(k):
            return remote(buf.at[0], buf.at[k], sem + k, (dp + k) % N_DP, f)

        return copy

    def begin(copy, count):
        loop(count, lambda k: copy(k).start(), 1)

    def arrive(copy, count):
        loop(count, lambda k: copy(k).wait_recv(), 1)

    def merge(buf, count, mine):
        def slot(p):
            return (mine - p + count) % count

        def add(p, carry):
            sums, number = carry
            return sums + buf[slot(p), 0:16, :], number + buf[slot(p), 32:40, :]

        sums, number = lax.fori_loop(
            0, count, add, (jnp.zeros((16, 128), F32), jnp.zeros((8, 128), F32))
        )
        mean = sums / jnp.concatenate([number, number], axis=0)

        def spread(p, squares):
            n_p = buf[slot(p), 32:40, :]
            n_p = jnp.concatenate([n_p, n_p], axis=0)
            off = buf[slot(p), 0:16, :] / n_p - mean
            return squares + (buf[slot(p), 16:32, :] + n_p * off * off)

        squares = lax.fori_loop(0, count, spread, jnp.zeros((16, 128), F32))
        return sums, squares, number

    def ordered(buf, count, mine, shape):
        def add(p, total):
            return total + buf[(mine - p + count) % count]

        return lax.fori_loop(0, count, add, jnp.zeros(shape, F32))

    copy_st1 = over_fsdp(st1, S_ST1)
    copy_st2 = over_dp(st2, S_ST2)
    begin(copy_st1, N_FSDP)

    own_copies[1].wait_recv()
    far_copies[0].start()
    pair_copies[1].start()
    own_copies[2].wait_recv()
    far_copies[1].start()
    pair_copies[2].start()

    arrive(copy_st1, N_FSDP)
    sums, squares, number = merge(st1, N_FSDP, f)
    st2[0, 0:16, :] = sums
    st2[0, 16:32, :] = squares
    st2[0, 32:40, :] = number
    begin(copy_st2, N_DP)

    arrive(copy_st2, N_DP)
    sums, squares, number = merge(st2, N_DP, dp)
    stat[0:16, :] = sums / TOTAL
    stat[16:32, :] = lax.rsqrt(squares / TOTAL + EPSILON)

    def activate(j):
        average = stat[pl.ds(j, 1), :]
        inverse = stat[pl.ds(16 + j, 1), :]
        g = gain[pl.ds(j, 1), :]
        b = shift[pl.ds(j, 1), :]
        for q in range(4):
            base = 128 * q
            keep = msk[4, base : base + 128, :]
            whitened = (filt[j, base : base + 128, :] - average) * inverse
            normed = whitened * g + b
            logistic = 1.0 / (1.0 + jnp.exp(-normed))
            value = normed * logistic * keep
            filt[j, base : base + 128, :] = whitened
            act[4 * q : 4 * q + 4, :, lanes(j)] = value.astype(BF16).reshape(4, BLOCK, 128)
            at[j % 2, rows((j // 2) * 128, 128), base : base + 128] = value.T.astype(BF16)

    loop(CHUNKS, activate)
    copy_at = remote(at.at[1 - c], atp, S_AT, partner, f)
    copy_at.start()

    fwd_copies[0].wait_recv()
    far_copies[2].start()
    pair_copies[3].start()
    fwd_copies[1].wait_recv()
    far_copies[3].start()
    pair_copies[4].start()

    loop(N_DP, lambda k: cot_copy(k).wait_recv(), 1)

    def back_block(b):
        block = cr[idx[DEST + b]]
        kept = jnp.broadcast_to(flags[pl.ds(b, 1), 0:1].astype(BF16), (BLOCK, D))
        cp[rows(b * BLOCK, BLOCK), :] = block * kept

    loop(16, back_block)
    copy_cp = remote(cp, cpp, S_CP, partner, f)
    copy_cp.start()

    ar[0] = act[idx[SEND]]

    def act_copy(k):
        return remote(cs.at[k], ar.at[k], S_ACT + k, peer_at(dp, k), f)

    def send_act(k):
        cot_copy(k).wait_send()
        cs[k] = act[idx[SEND + k]]
        act_copy(k).start()

    loop(N_DP, send_act, 1)

    far_copies[0].wait_recv()
    far_copies[1].wait_recv()
    pair_copies[5].start()

    up, down, across = (y + 1) % 4, (y + 3) % 4, (y + 2) % 4
    f_above, f_below = up * 2 + zl, down * 2 + zl

    def half(ref, h):
        return ref.at[pl.ds(2 * h, 2)]

    across_up = remote(half(gp.at[across], 0), rd.at[0], S_R1, dp, f_above)
    across_down = remote(half(gp.at[across], 1), rd.at[1], S_R1 + 1, dp, f_below)
    plain_up = remote(half(gp.at[up], 1), half(r1.at[0], 1), S_R1 + 2, dp, f_above)
    plain_down = remote(half(gp.at[down], 0), half(r1.at[1], 0), S_R1 + 3, dp, f_below)
    added_up = remote(half(gp.at[up], 0), half(r1.at[0], 0), S_R1 + 4, dp, f_above)
    added_down = remote(half(gp.at[down], 1), half(r1.at[1], 1), S_R1 + 5, dp, f_below)

    def copy_r2(k):
        b = (x + k) % 4
        return remote(s1.at[b], r2.at[k - 1], S_R2 + k, b * 4 + zh * 2 + c, f)

    def copy_r3(k):
        to_z = (z + k) % 4
        return remote(
            s2.at[to_z], r3.at[k - 1], S_R3 + k, x * 4 + (to_z // 2) * 2 + c, y * 2 + to_z % 2
        )

    def products(a):
        def product(b):
            d_rows = rows(a * 256, 256)
            columns = pl.ds(pl.multiple_of(b * 512, 512), 512)
            value = jnp.dot(at[c, d_rows, :], cp[:, columns], preferred_element_type=F32)
            value = value + jnp.dot(
                atp[d_rows, :], cpp[:, columns], preferred_element_type=F32
            )
            for h in range(2):
                for low in range(2):
                    piece = value[low * 128 : low * 128 + 128, h * 256 : h * 256 + 256]
                    gp[a, b, h * 2 + low] = piece.astype(BF16)

        loop(4, product)

    copy_at.wait_recv()
    copy_cp.wait_recv()
    products(across)
    across_up.start()
    across_down.start()
    far_copies[2].wait_recv()
    far_copies[3].wait_recv()
    pair_copies[6].start()
    products(up)
    plain_up.start()
    products(down)
    plain_down.start()
    for copy in pair_copies:
        copy.wait_recv()

    def act_grad(f_of):
        value = lax.dot_general(
            cp[...],
            pan[rows(f_of * 256, 256), :],
            (((1,), (1,)), ((), ())),
            preferred_element_type=F32,
        )
        value = value.astype(BF16).astype(F32)
        ngx[f_of * 2, 8:520, :] = value[:, 0:128]
        ngx[f_of * 2 + 1, 8:520, :] = value[:, 128:256]

    loop(N_FSDP, act_grad)

    def slopes(j):
        g = gain[pl.ds(j, 1), :]
        b = shift[pl.ds(j, 1), :]
        sum_w = jnp.zeros((8, 128), F32)
        sum_1 = jnp.zeros((8, 128), F32)
        for q in range(4):
            base = 128 * q
            whitened = filt[j, base : base + 128, :]
            normed = whitened * g + b
            logistic = 1.0 / (1.0 + jnp.exp(-normed))
            slope = logistic + normed * logistic * (1.0 - logistic)
            grad = ngx[j, 8 + base : 136 + base, :] * slope
            ngx[j, 8 + base : 136 + base, :] = grad
            sum_w = sum_w + jnp.sum((grad * whitened).reshape(16, 8, 128), axis=0)
            sum_1 = sum_1 + jnp.sum(grad.reshape(16, 8, 128), axis=0)
        ng1[0, pl.ds(j, 1), :] = fold(sum_w)
        ng1[0, pl.ds(16 + j, 1), :] = fold(sum_1)
        bsend[0, j] = ngx[j, 8:16, :]
        bsend[1, j] = filt[j, 0:8, :]
        bsend[2, j] = ngx[j, pl.ds(idx[LIVE], 8), :]
        bsend[3, j] = filt[j, pl.ds(idx[LIVE + 2], 8), :]

    loop(CHUNKS, slopes)

    copy_ng1 = over_fsdp(ng1, S_NG1)
    copy_ng2 = over_dp(ng2, S_NG2)
    begin(copy_ng1, N_FSDP)
    halo_copies = [
        remote(bsend.at[0], brecv.at[0], S_BHALO, lead // N_FSDP, lead % N_FSDP),
        remote(bsend.at[1], brecv.at[1], S_BHALO + 1, lead // N_FSDP, lead % N_FSDP),
        remote(bsend.at[2], brecv.at[2], S_BHALO + 2, follow // N_FSDP, follow % N_FSDP),
        remote(bsend.at[3], brecv.at[3], S_BHALO + 3, follow // N_FSDP, follow % N_FSDP),
    ]
    for copy in halo_copies:
        copy.start()

    def pass_on(a, h, n):
        def add(i):
            b, m = i // 4, i % 4
            value = gp[a, 2 * h + b, m].astype(F32) + rd[n, b, m].astype(F32)
            gp[a, 2 * h + b, m] = value.astype(BF16)

        loop(8, add)

    across_up.wait_recv()
    pass_on(up, 0, 0)
    added_up.start()
    across_down.wait_recv()
    pass_on(down, 1, 1)
    added_down.start()

    arrive(copy_ng1, N_FSDP)
    ng2[0] = ordered(ng1, N_FSDP, f, (32, 128))
    begin(copy_ng2, N_DP)
    products(y)

    arrive(copy_ng2, N_DP)
    ng_total = ordered(ng2, N_DP, dp, (32, 128))
    stat[32:64, :] = ng_total
    for j in range(CHUNKS):
        ngrad[0:1, 128 * j : 128 * j + 128] = ng_total[j : j + 1]
        ngrad[1:2, 128 * j : 128 * j + 128] = ng_total[16 + j : 17 + j]
    for copy in halo_copies:
        copy.wait_recv()

    def back(j):
        taps = kern[:, lanes(j)]
        scale = gain[pl.ds(j, 1), :] * stat[pl.ds(16 + j, 1), :]
        mean_w = stat[pl.ds(32 + j, 1), :] / TOTAL
        mean_1 = stat[pl.ds(48 + j, 1), :] / TOTAL

        def center(grad, whitened):
            return scale * (grad - mean_1 - whitened * mean_w)

        for q in range(4):
            base = 128 * q
            ngx[j, 8 + base : 136 + base, :] = center(
                ngx[j, 8 + base : 136 + base, :], filt[j, base : base + 128, :]
            )
        ngx[j, 520:528, :] = jnp.zeros((8, 128), F32)
        place(
            ngx, j, center(brecv[2, j], brecv[3, j]), center(brecv[0, j], brecv[1, j])
        )

        def part(i, sums):
            base = i * 32
            accum = jnp.zeros((32, 128), F32)
            here = ext[j, pl.ds(pl.multiple_of(base + 8, 8), 32), :]
            new = []
            for tap in range(TAPS):
                window = ngx[j, pl.ds(base + 12 - tap, 32), :]
                window = window * msk[8 - tap, rows(base, 32), :]
                accum = accum + window * taps[tap : tap + 1]
                new.append(sums[tap] + jnp.sum((window * here).reshape(4, 8, 128), axis=0))
            fr[pl.ds(i * 2, 2), :, lanes(j)] = accum.astype(BF16).reshape(2, 16, 128)
            return tuple(new)

        sums = lax.fori_loop(
            0, 16, part, tuple(jnp.zeros((8, 128), F32) for _ in range(TAPS))
        )
        kg[j, 8:16, :] = jnp.zeros((8, 128), F32)
        for tap in range(TAPS):
            kg[j, tap : tap + 1, :] = fold(sums[tap])

    halo_prev.wait_send()
    loop(8, back)

    for copy in (plain_up, plain_down, added_up, added_down):
        copy.wait_recv()

    def add_first(b):
        for n in range(4):
            value = gp[y, b, n].astype(F32)
            for k in range(2):
                value = value + r1[k, b, n].astype(F32)
            s1[b, n] = value.astype(BF16)

    loop(4, add_first)
    for k in (1, 2, 3):
        copy_r2(k).start()

    loop(CHUNKS, back, 8)
    store_igrad = pltpu.make_async_copy(fr, igrad, lsem.at[0])
    store_igrad.start()

    def copy_k1(k):
        peer = (dp + k) % N_DP
        return remote(kg.at[peer], kg1.at[k], S_K1 + k, peer, f)

    begin(copy_k1, N_DP)
    kg1[0] = kg[dp]

    arrive(copy_k1, N_DP)
    kg2[0] = ordered(kg1, N_DP, dp, (16, 128))
    copy_k2 = over_fsdp(kg2, S_K2)
    begin(copy_k2, N_FSDP)

    loop(N_DP, lambda k: act_copy(k).wait_recv(), 1)

    def pick(r):
        cot[r] = ar[idx[PICK + r]]

    loop(12, pick)

    def project(n):
        columns = pl.ds(pl.multiple_of(n * 256, 256), 256)
        value = jnp.dot(cot[...].reshape(ROWS, D), pan[:, columns], preferred_element_type=F32)
        mst[:, columns] = value.astype(BF16)

    loop(4, project)

    for k in (1, 2, 3):
        copy_r2(k).wait_recv()

    def add_second(n):
        value = s1[x, n].astype(F32)
        for k in range(3):
            value = value + r2[k, n].astype(F32)
        s2[n] = value

    loop(4, add_second)
    for k in (1, 2, 3):
        copy_r3(k).start()

    arrive(copy_k2, N_FSDP)
    kg3[dp] = ordered(kg2, N_FSDP, f, (16, 128))

    def copy_k3(k):
        return remote(kg3.at[dp], kg3.at[dp], S_K3 + k, (dp + k) % N_DP, f)

    begin(copy_k3, N_DP)

    loop(8, project, 4)
    store_mapped = pltpu.make_async_copy(mst, mapped, lsem.at[1])
    store_mapped.start()

    for k in (1, 2, 3):
        copy_r3(k).wait_recv()
    value = s2[z]
    for k in range(3):
        value = value + r3[k]
    place_of = x * 2 + zh
    pgb[c, place_of] = value.astype(BF16)

    def copy_gather(k):
        to = (place_of + k) % 8
        mine = pgb.at[c, place_of]
        return remote(mine, mine, S_GAT + k, to * 2 + c, f)

    begin(copy_gather, 8)
    arrive(copy_gather, 8)
    copy_gpair = remote(pgb.at[c], pgb.at[c], S_GPAIR, partner, f)
    copy_gpair.start()

    arrive(copy_k3, N_DP)
    for j in range(CHUNKS):
        kgrad[:, 128 * j : 128 * j + 128] = kg3[j, 0:TAPS, :]

    copy_gpair.wait_recv()
    store_pgrad = pltpu.make_async_copy(pgb, pgrad, lsem.at[2])
    store_pgrad.start()

    halo_next.wait_send()
    for copy in own_copies + fwd_copies + far_copies + pair_copies + halo_copies:
        copy.wait_send()
    copy_cp.wait_send()
    copy_at.wait_send()
    for copy in (across_up, across_down, plain_up, plain_down, added_up, added_down):
        copy.wait_send()
    copy_gpair.wait_send()
    for k in (1, 2, 3):
        copy_r2(k).wait_send()
        copy_r3(k).wait_send()
    for copy in (copy_st2, act_copy, copy_ng2, copy_k1, copy_k3):
        loop(N_DP, lambda k, copy=copy: copy(k).wait_send(), 1)
    for copy in (copy_st1, copy_ng1, copy_k2, copy_gather):
        loop(N_FSDP, lambda k, copy=copy: copy(k).wait_send(), 1)
    store_igrad.wait()
    store_mapped.wait()
    store_pgrad.wait()


def finish(
    mapped, igrad, pieces, kgrad, ngrad, o_mapped, o_igrad, o_pgrad, o_kgrad, o_ngrad,
    v_mapped, v_igrad, v_pieces, v_pgrad, sems,
):
    loads = [
        pltpu.make_async_copy(source, target, sems.at[n])
        for n, (source, target) in enumerate(
            [(pieces, v_pieces), (igrad, v_igrad), (mapped, v_mapped)]
        )
    ]
    for copy in loads:
        copy.start()
    o_kgrad[...] = kgrad[...]
    o_ngrad[...] = ngrad[...]
    loads[0].wait()
    stores = []
    for part in range(2):
        for u in range(8):
            v_pgrad[128 * part : 128 * part + 128, 256 * u : 256 * u + 256] = v_pieces[
                part, u
            ].astype(F32)
        half = pl.ds(128 * part, 128)
        stores.append(
            pltpu.make_async_copy(v_pgrad.at[half], o_pgrad.at[half], sems.at[3 + part])
        )
        stores[-1].start()
    loads[1].wait()
    stores.append(pltpu.make_async_copy(v_igrad, o_igrad, sems.at[5]))
    stores[-1].start()
    loads[2].wait()
    stores.append(pltpu.make_async_copy(v_mapped, o_mapped, sems.at[6]))
    stores[-1].start()
    for copy in stores:
        copy.wait()


def shards(frames, bounds, destinations, kernel, norm_gain, norm_shift, panel, cotangent):
    hbm = pl.BlockSpec(memory_space=pl.ANY)
    vmem = pl.BlockSpec(memory_space=pltpu.VMEM)
    smem = pl.BlockSpec(memory_space=pltpu.SMEM)
    shape = jax.ShapeDtypeStruct
    idx, flags = pl.pallas_call(
        routing,
        out_shape=(shape((96,), jnp.int32), shape((40, 128), F32)),
        in_specs=[smem],
        out_specs=(smem, vmem),
    )(destinations)
    mapped, input_grad, *rest = pl.pallas_call(
        fused,
        out_shape=(
            shape((ROWS, D), BF16),
            shape((32, 16, D), BF16),
            shape((2, 8, 128, 256), BF16),
            shape((TAPS, D), F32),
            shape((2, D), F32),
        ),
        in_specs=[pl.BlockSpec(memory_space=pltpu.SMEM), vmem, vmem, hbm, hbm, hbm, vmem, vmem, vmem],
        out_specs=(hbm, hbm, hbm, vmem, vmem),
        scratch_shapes=[
            pltpu.VMEM((32, 16, D), BF16),
            pltpu.VMEM((12, BLOCK, D), BF16),
            pltpu.VMEM((16, BLOCK, D), BF16),
            pltpu.VMEM((16, BLOCK, D), BF16),
            pltpu.VMEM((SLOTS, D), BF16),
            pltpu.VMEM((SLOTS, D), BF16),
            pltpu.VMEM((CHUNKS, 528, 128), F32),
            pltpu.VMEM((CHUNKS, 512, 128), F32),
            pltpu.VMEM((CHUNKS, 528, 128), F32),
            pltpu.VMEM((TAPS, 512, 128), F32),
            pltpu.VMEM((D, D), BF16),
            pltpu.VMEM((16, BLOCK, D), BF16),
            pltpu.VMEM((16, BLOCK, D), BF16),
            pltpu.VMEM((2, 1024, 512), BF16),
            pltpu.VMEM((1024, 512), BF16),
            pltpu.VMEM((4, 4, 4, 128, 256), BF16),
            pltpu.VMEM((2, 4, 4, 128, 256), BF16),
            pltpu.VMEM((2, 2, 4, 128, 256), BF16),
            pltpu.VMEM((4, 4, 128, 256), BF16),
            pltpu.VMEM((3, 4, 128, 256), BF16),
            pltpu.VMEM((4, 128, 256), F32),
            pltpu.VMEM((3, 128, 256), F32),
            pltpu.VMEM((2, 8, 128, 256), BF16),
            pltpu.VMEM((ROWS, D), BF16),
            pltpu.VMEM((16, D), BF16),
            pltpu.VMEM((16, D), BF16),
            pltpu.VMEM((16, D), BF16),
            pltpu.VMEM((N_FSDP, 40, 128), F32),
            pltpu.VMEM((N_DP, 40, 128), F32),
            pltpu.VMEM((64, 128), F32),
            pltpu.VMEM((N_FSDP, 32, 128), F32),
            pltpu.VMEM((N_DP, 32, 128), F32),
            pltpu.VMEM((4, CHUNKS, 8, 128), F32),
            pltpu.VMEM((4, CHUNKS, 8, 128), F32),
            pltpu.VMEM((CHUNKS, 16, 128), F32),
            pltpu.VMEM((N_DP, 16, 128), F32),
            pltpu.VMEM((N_FSDP, 16, 128), F32),
            pltpu.VMEM((CHUNKS, 16, 128), F32),
            pltpu.SemaphoreType.DMA((SEMS.used,)),
            pltpu.SemaphoreType.DMA((SEMS.used,)),
            pltpu.SemaphoreType.DMA((3,)),
        ],
        compiler_params=pltpu.CompilerParams(
            collective_id=0, has_side_effects=True, vmem_limit_bytes=62 * 1024 * 1024
        ),
    )(
        idx,
        flags,
        bounds,
        frames.reshape(32, 16, D),
        cotangent.reshape(12, BLOCK, D),
        panel,
        kernel,
        norm_gain.reshape(CHUNKS, 128),
        norm_shift.reshape(CHUNKS, 128),
    )
    results = (mapped, input_grad, *rest)
    mapped, input_grad, *rest = pl.pallas_call(
        finish,
        out_shape=(
            shape((ROWS, D), BF16),
            shape((32, 16, D), BF16),
            shape((256, D), F32),
            shape((TAPS, D), F32),
            shape((2, D), F32),
        ),
        in_specs=[hbm, hbm, hbm, vmem, vmem],
        out_specs=(hbm, hbm, hbm, vmem, vmem),
        scratch_shapes=[
            pltpu.VMEM((ROWS, D), BF16),
            pltpu.VMEM((32, 16, D), BF16),
            pltpu.VMEM((2, 8, 128, 256), BF16),
            pltpu.VMEM((256, D), F32),
            pltpu.SemaphoreType.DMA((7,)),
        ],
        compiler_params=pltpu.CompilerParams(vmem_limit_bytes=60 * 1024 * 1024),
    )(*results)
    return (mapped, input_grad.reshape(SLOTS, D), *rest)


def solution(mesh):
    placed = (
        P(("dp", "fsdp"), None),
        P(None, ("dp", "fsdp")),
        P(None, "fsdp", None),
        P(),
        P(),
        P(),
        P("fsdp", None),
        P(("dp", "fsdp"), None),
    )
    return jax.shard_map(
        shards,
        mesh=mesh,
        in_specs=placed,
        out_specs=(P(("dp", "fsdp"), None), P(("dp", "fsdp"), None), P("fsdp", None), P(), P()),
        check_vma=False,
    )
```
